32 devices in a mesh: wide: 16 (over z, y, x), narrow: 2 (over core).
Axes of the slice: x: 2, y: 2, z: 4, core: 2. Of those that a mesh axis runs over, the one named last changes fastest.
Arguments:
- tokens: bfloat16 [212992, 192], P(('wide', 'narrow')), may hold values from -6 to 6
- cotangent: bfloat16 [212992, 192], P(('wide', 'narrow')), may hold values from -6 to 6
- group: int32 [2048], P(('wide', 'narrow')), may hold values from 0 to 2, as said below
- counts: int32 [2048], P(('wide', 'narrow')), may hold values from 1 to 100, as said below
- attn_w: float32 [768, 192], P('wide')
- ffn_in: float32 [512, 192], P('wide'), may hold values from -0.4375 to 0.4375
- ffn_out: float32 [256, 192], P('wide'), may hold values from -0.375 to 0.375
- vectors: float32 [2048], P('wide')
- attn_m: float32 [768, 192], P('wide')
- attn_v: float32 [768, 192], P('wide'), as said below
- in_m: float32 [512, 192], P('wide')
- in_v: float32 [512, 192], P('wide'), as said below
- out_m: float32 [256, 192], P('wide')
- out_v: float32 [256, 192], P('wide'), as said below
- vec_m: float32 [2048], P('wide')
- vec_v: float32 [2048], P('wide'), as said below
Outputs:
- out_tokens: bfloat16 [212992, 192], P(('wide', 'narrow'))
- input_grad: float32 [212992, 192], P(('wide', 'narrow'))
- attn_new: float32 [768, 192], P('wide')
- attn_first: float32 [768, 192], P('wide')
- attn_second: float32 [768, 192], P('wide')
- in_new: float32 [512, 192], P('wide')
- in_first: float32 [512, 192], P('wide')
- in_second: float32 [512, 192], P('wide')
- out_new: float32 [256, 192], P('wide')
- out_first: float32 [256, 192], P('wide')
- out_second: float32 [256, 192], P('wide')
- vec_new: float32 [2048], P('wide')
- vec_first: float32 [2048], P('wide')
- vec_second: float32 [2048], P('wide')
The draws below stay inside these ranges and needn't reach their ends.
Inputs may be any that keep to these rules, and one draw needn't show every extreme that they name: `group`: dataset of each sample: 0, 1 or 2 for padded lengths 40, 68, 100. `counts`: at most the padded length of the sample's dataset. `attn_v`: positive. `in_v`: positive. `out_v`: positive. `vec_v`: positive.
All inputs are finite; a program needn't handle non-finite values.
Results may differ from the reference program's by a relative error of at most 0.012.
The reference program's roundings to bfloat16 on the way count: a program that leaves them out, or rounds other values in their place, can miss the bound.
Values may be sent and summed in bfloat16 or wider, within the bound.
A program may use at most 192 MiB of HBM per device.

```python
import math
import jax
import jax.numpy as jnp
from jax import lax

D = 192
HEADS = 8
FF = 256
SLOT = 104
L1 = 40
L2 = 68
L3 = 100
STEP = 10
SAMPLES = 2048
ROWS = 212992
NVEC = 2048


OUT_BOOST = 3.0


def sample_table(key):
    kind_key, count_key = jax.random.split(key)
    kinds = jax.random.randint(kind_key, (SAMPLES,), 0, 3).astype(jnp.int32)
    kinds = kinds.at[0].set(2)
    limits = jnp.where(kinds == 0, L1, jnp.where(kinds == 1, L2, L3)).astype(jnp.int32)
    drawn = jax.random.randint(count_key, (SAMPLES,), 0, 1 << 20).astype(jnp.int32)
    live = (1 + drawn % limits).astype(jnp.int32)
    live = live.at[0].set(L3)
    return (kinds, live)


def draw_group(key, part):
    return sample_table(key)[0]


def draw_counts(key, part):
    return sample_table(key)[1]


def draw_attn_w(key, part):
    key = jax.random.fold_in(key, 3)
    noise = jax.random.normal(key, (4 * D, D))
    rows = jnp.arange(4 * D)[:, None]
    factor = jnp.where(rows < 3 * D, 1.0, OUT_BOOST) / math.sqrt(D)
    return (noise * factor).astype(jnp.float32)


def draw_vectors(key, part):
    key = jax.random.fold_in(key, 5)
    place = jnp.arange(NVEC)
    gainlike = (place < D) | (place >= 2 * D) & (place < 3 * D)
    spread = jax.random.uniform(key, (NVEC,), minval=-1.0, maxval=1.0)
    shifts = jax.random.normal(jax.random.fold_in(key, 1), (NVEC,))
    return jnp.where(gainlike, 1.0 + 0.15 * spread, 0.3 * shifts).astype(jnp.float32)


def attn_size():
    rows = jnp.arange(4 * D)[:, None]
    return jnp.where(rows < 3 * D, 0.3, 0.1) * math.sqrt(SAMPLES * SLOT)


def first_moment(key, shape, size):
    return (jax.random.normal(key, shape) * size / 9.0).astype(jnp.float32)


def second_moment(key, shape, size):
    factor = jnp.exp(jax.random.uniform(key, shape, minval=0.0, maxval=math.log(4.0)))
    return (factor * 0.001 * size * size).astype(jnp.float32)


def draw_attn_m(key, part):
    key = jax.random.fold_in(key, 7)
    return first_moment(key, (4 * D, D), attn_size())


def draw_attn_v(key, part):
    key = jax.random.fold_in(key, 8)
    return second_moment(key, (4 * D, D), attn_size())


def draw_in_m(key, part):
    key = jax.random.fold_in(key, 9)
    return first_moment(key, (2 * FF, D), 0.6 * math.sqrt(SAMPLES * SLOT))


def draw_in_v(key, part):
    key = jax.random.fold_in(key, 10)
    return second_moment(key, (2 * FF, D), 0.6 * math.sqrt(SAMPLES * SLOT))


def draw_out_m(key, part):
    key = jax.random.fold_in(key, 12)
    return first_moment(key, (FF, D), 0.5 * math.sqrt(SAMPLES * SLOT))


def draw_out_v(key, part):
    key = jax.random.fold_in(key, 13)
    return second_moment(key, (FF, D), 0.5 * math.sqrt(SAMPLES * SLOT))


def draw_vec_m(key, part):
    key = jax.random.fold_in(key, 14)
    return first_moment(key, (NVEC,), 0.8 * math.sqrt(SAMPLES * SLOT))


def draw_vec_v(key, part):
    key = jax.random.fold_in(key, 15)
    return second_moment(key, (NVEC,), 0.8 * math.sqrt(SAMPLES * SLOT))


def level_of(stream_key, dims, cuts, smallest, largest):
    loudness, own = 1.0, jax.random.fold_in(stream_key, 6)
    for dim, shards_of in cuts:
        draws = jnp.exp(jax.random.uniform(jax.random.fold_in(own, dim), (shards_of,), jnp.float32, smallest / len(cuts), largest / len(cuts)))
        loudness = loudness * jnp.repeat(draws, dims[dim] // shards_of).reshape([-1 if axis == dim else 1 for axis in range(len(dims))])
    return loudness


def gaussian(rng, extent, width, bound, cuts=(), kind=jnp.bfloat16):
    loudness = level_of(rng, extent, cuts, -0.22, 0.18) if cuts else 1.0
    array = jax.random.normal(rng, extent, jnp.float32) * width * loudness
    return jnp.minimum(jnp.maximum(array, -bound), bound).astype(kind)


def setup_inputs(seed: int = 0) -> dict:
    arg_keys = jax.random.split(jax.random.key(seed), 17)
    return {
        "tokens": gaussian(arg_keys[0], (ROWS, D), 1.0, 6.0, ((0, 32),)),
        "cotangent": gaussian(arg_keys[1], (ROWS, D), 1.0, 6.0, ((0, 32),)),
        "group": draw_group(jax.random.fold_in(arg_keys[16], 71), 0),
        "counts": draw_counts(jax.random.fold_in(arg_keys[16], 71), 0),
        "attn_w": draw_attn_w(jax.random.fold_in(arg_keys[16], 71), 0),
        "ffn_in": gaussian(arg_keys[5], (2 * FF, D), D ** -0.5, 0.4375, ((0, 16),), jnp.float32),
        "ffn_out": gaussian(arg_keys[6], (FF, D), FF ** -0.5, 0.375, ((0, 16),), jnp.float32),
        "vectors": draw_vectors(jax.random.fold_in(arg_keys[16], 71), 0),
        "attn_m": draw_attn_m(jax.random.fold_in(arg_keys[16], 71), 0),
        "attn_v": draw_attn_v(jax.random.fold_in(arg_keys[16], 71), 0),
        "in_m": draw_in_m(jax.random.fold_in(arg_keys[16], 71), 0),
        "in_v": draw_in_v(jax.random.fold_in(arg_keys[16], 71), 0),
        "out_m": draw_out_m(jax.random.fold_in(arg_keys[16], 71), 0),
        "out_v": draw_out_v(jax.random.fold_in(arg_keys[16], 71), 0),
        "vec_m": draw_vec_m(jax.random.fold_in(arg_keys[16], 71), 0),
        "vec_v": draw_vec_v(jax.random.fold_in(arg_keys[16], 71), 0),
    }


@jax.custom_vjp
def low(v):
    return lax.optimization_barrier(v.astype(jnp.bfloat16)).astype(jnp.float32)

@jax.custom_vjp
def low_back(v):
    return v

def low_keep(v):
    return (low(v), None)

def low_pass(kept, grad):
    return (grad,)

def back_keep(v):
    return (v, None)

def back_low(kept, grad):
    return (low(grad),)
low.defvjp(low_keep, low_pass)
low_back.defvjp(back_keep, back_low)
NORM_EPS = 1e-05
BETA_ONE = 0.9
BETA_TWO = 0.999
ADAM_EPS = 1e-08
LEARN_RATE = 0.1
WEIGHT_DECAY = 0.01
MASK_VALUE = -1e+30

def normed(values, scales, offset):
    centre = values - lax.optimization_barrier(jnp.mean(values, -1, keepdims=True))
    spread = lax.optimization_barrier(jnp.mean(centre * centre, -1, keepdims=True))
    return centre * lax.rsqrt(spread + NORM_EPS) * scales + offset

def gated(gate_part, up_part):
    return jax.nn.gelu(gate_part, approximate=True) * up_part

def adamw_update(master, gradient, moment, square):
    moment_new = BETA_ONE * moment + (1.0 - BETA_ONE) * gradient
    square_new = BETA_TWO * square + (1.0 - BETA_TWO) * gradient * gradient
    moment_hat = moment_new / (1.0 - BETA_ONE ** STEP)
    square_hat = square_new / (1.0 - BETA_TWO ** STEP)
    master_new = master - LEARN_RATE * (moment_hat / (jnp.sqrt(square_hat) + ADAM_EPS) + WEIGHT_DECAY * master)
    return (master_new, moment_new, square_new)

def attend(query, keys, values, live_counts):
    batch = query.shape[0]
    head_size = D // HEADS
    score_scale = 1.0 / math.sqrt(head_size)
    shape_four = (batch, SLOT, HEADS, head_size)
    scores = jnp.einsum('sqhd,skhd->shqk', query.reshape(shape_four), keys.reshape(shape_four), precision=lax.Precision.HIGHEST) * score_scale
    scores = low_back(scores)
    live = jnp.arange(SLOT)[None, :] < live_counts[:, None]
    scores = jnp.where(live[:, None, None, :], scores, MASK_VALUE)
    row_top = lax.optimization_barrier(jnp.max(scores, -1, keepdims=True))
    exponent = jnp.exp(scores - row_top)
    probs = low(exponent / lax.optimization_barrier(jnp.sum(exponent, -1, keepdims=True)))
    mixed = jnp.einsum('shqk,skhd->sqhd', probs, values.reshape(shape_four), precision=lax.Precision.HIGHEST)
    return mixed.reshape(batch, SLOT, D)

def reference(tokens, cotangent, group, counts, attn_w, ffn_in, ffn_out, vectors, attn_m, attn_v, in_m, in_v, out_m, out_v, vec_m, vec_v):
    highest = lax.Precision.HIGHEST
    position = jnp.arange(SLOT)
    limit = jnp.where(group == 0, L1, jnp.where(group == 1, L2, L3))
    row_keep = (position[None, :] < limit[:, None]).astype(jnp.float32).reshape(SAMPLES * SLOT, 1)
    blocks = SAMPLES // 32
    block_counts = counts.reshape(blocks, 32)
    checked = jax.checkpoint(lambda packed: attend(packed[0], packed[1], packed[2], packed[3]))

    def forward(inputs, attn_master, in_master, out_master, vec_master):
        attn_low = low(attn_master)
        in_low = low(in_master)
        out_low = low(out_master)
        vec_low = low(vec_master)
        pieces = [vec_low[member * D:(member + 1) * D] for member in range(8)]
        in_bias = vec_low[8 * D:]
        normed_one = low(normed(inputs, pieces[0], pieces[1]))
        qkv = jnp.einsum('rd,kde->kre', normed_one, attn_low[:3 * D].reshape(3, D, D), precision=highest)
        query = low_back(low(qkv[0] + pieces[4]))
        keys = low_back(low(qkv[1]))
        values = low_back(low(qkv[2] + pieces[5]))
        mixed = lax.map(checked, (query.reshape(blocks, 32, SLOT, D), keys.reshape(blocks, 32, SLOT, D), values.reshape(blocks, 32, SLOT, D), block_counts))
        mixed = low_back(low(mixed.reshape(SAMPLES * SLOT, D)))
        attn_out = low_back(jnp.dot(mixed, attn_low[3 * D:], precision=highest) + pieces[6])
        after_attn = inputs + row_keep * attn_out
        normed_two = low(normed(after_attn, pieces[2], pieces[3]))
        projected = low_back(jnp.dot(normed_two, in_low.T, precision=highest) + in_bias)
        hidden_act = low(gated(projected[:, :FF], projected[:, FF:]))
        ffn_result = low_back(jnp.dot(hidden_act, out_low, precision=highest) + pieces[7])
        return after_attn + row_keep * ffn_result
    result, pullback = jax.vjp(forward, tokens.astype(jnp.float32), attn_w, ffn_in, ffn_out, vectors)
    input_grad, attn_grad, in_grad, out_grad, vec_grad = pullback(cotangent.astype(jnp.float32))
    attn_update = adamw_update(attn_w, attn_grad, attn_m, attn_v)
    in_update = adamw_update(ffn_in, in_grad, in_m, in_v)
    out_update = adamw_update(ffn_out, out_grad, out_m, out_v)
    vec_update = adamw_update(vectors, vec_grad, vec_m, vec_v)
    return (result.astype(jnp.bfloat16), input_grad, attn_update[0], attn_update[1], attn_update[2], in_update[0], in_update[1], in_update[2], out_update[0], out_update[1], out_update[2], vec_update[0], vec_update[1], vec_update[2])
```

```python
import functools
import math

import jax
import jax.numpy as jnp
from jax import lax
from jax.experimental import pallas as pl
from jax.experimental.pallas import tpu as pltpu
from jax.sharding import PartitionSpec as P

HEADS = 8
SLOT = 104
L1 = 40
L2 = 68
L3 = 100
STEP = 10

NORM_EPS = 1e-05
BETA_ONE = 0.9
BETA_TWO = 0.999
ADAM_EPS = 1e-08
LEARN_RATE = 0.1
WEIGHT_DECAY = 0.01
MASK_VALUE = -1e30

F32 = jnp.float32
BF16 = jnp.bfloat16
LANE = 128
STRIDE = 32
NN = (((1,), (0,)), ((), ()))
NT = (((1,), (1,)), ((), ()))
TN = (((0,), (0,)), ((), ()))
BATCH = 4
SPARE = 24


def adamw_update(master, gradient, moment, square):
    moment_new = BETA_ONE * moment + (1.0 - BETA_ONE) * gradient
    square_new = BETA_TWO * square + (1.0 - BETA_TWO) * gradient * gradient
    moment_hat = moment_new / (1.0 - BETA_ONE**STEP)
    square_hat = square_new / (1.0 - BETA_TWO**STEP)
    master_new = master - LEARN_RATE * (
        moment_hat / (jnp.sqrt(square_hat) + ADAM_EPS) + WEIGHT_DECAY * master
    )
    return (master_new, moment_new, square_new)


def dot(a, b, dims=NN):
    return lax.dot_general(a, b, dims, preferred_element_type=F32)


def iota(shape, dim):
    return lax.broadcasted_iota(jnp.int32, shape, dim)


def partial_sums(value):
    rows, cols = value.shape
    return jnp.sum(value.reshape(rows // 8, 8, cols), axis=0)


def piece(vec, member, width):
    start = member * width
    parts, at = [], start
    while at < start + width:
        row, lane = divmod(at, LANE)
        take = min(LANE - lane, start + width - at)
        parts.append(vec[row : row + 1, lane : lane + take])
        at += take
    return jnp.concatenate(parts, axis=1)


def layer_kernel(
    group_ref,
    counts_ref,
    tok_ref,
    cot_ref,
    attn_ref,
    in_ref,
    out_ref,
    vec_ref,
    y_ref,
    dx_ref,
    g_attn_ref,
    g_in_ref,
    g_out_ref,
    g_vec_ref,
    order,
    slots,
    xrow,
    crow,
    w_qkv,
    w_qkv_t,
    w_o,
    w_o_t,
    w_in,
    w_out_t,
    probs,
    acc_qkv,
    acc_o,
    acc_in,
    acc_out,
    acc_small,
):
    width = attn_ref.shape[1]
    hidden = out_ref.shape[0]
    samples = group_ref.shape[0]
    rows_all = tok_ref.shape[1]
    head = width // HEADS
    pad = HEADS * STRIDE
    scale = 1.0 / math.sqrt(head)
    log2e = math.log2(math.e)
    q_scale = scale * log2e

    slots[0] = 0
    slots[1] = 0
    slots[2] = 0

    def count(s, carry):
        g = group_ref[s]
        slots[g] = slots[g] + 1
        return carry

    lax.fori_loop(0, samples, count, 0)
    first = slots[0]
    second = slots[1]
    slots[0] = 0
    slots[1] = first
    slots[2] = first + second

    def place(s, carry):
        g = group_ref[s]
        at = slots[g]
        order[at] = s
        slots[g] = at + 1
        return carry

    lax.fori_loop(0, samples, place, 0)

    spread_row = iota((width, pad), 0)
    spread_col = iota((width, pad), 1)
    within = spread_col & (STRIDE - 1)
    spread = jnp.where(
        (within < head) & (spread_row == (spread_col >> 5) * head + within), 1.0, 0.0
    ).astype(BF16)
    vec = vec_ref[...].astype(F32)
    pieces = [piece(vec, member, width) for member in range(8)]
    g1, b1, g2, b2, bq, bv, bo, bf = pieces
    bi = jnp.concatenate([vec[row : row + 1] for row in range(12, 16)], axis=1)
    zero_rows = jnp.zeros((pad - width - 8, pad), F32)

    def first_row(row):
        return jnp.concatenate([row, jnp.zeros((7, row.shape[1]), F32)], axis=0)

    spare_lane = (iota((1, pad), 1) & (STRIDE - 1)) == SPARE
    for member in range(3):
        spread_w = dot(attn_ref[member * width : (member + 1) * width, :], spread)
        if member == 0:
            bias = dot(bq.astype(BF16), spread) + jnp.where(spare_lane, 1.0, 0.0)
        elif member == 1:
            bias = jnp.zeros((1, pad), F32)
        else:
            bias = dot(bv.astype(BF16), spread)
        w_qkv[:, member * pad : (member + 1) * pad] = jnp.concatenate(
            [spread_w, first_row(bias), zero_rows], axis=0
        ).astype(BF16)
        w_qkv_t[member * pad : (member + 1) * pad, :] = spread_w.T.astype(BF16)
    spread_o = dot(spread, attn_ref[3 * width :, :], TN)
    w_o_t[...] = spread_o.T.astype(BF16)
    w_o[...] = jnp.where(iota((pad, width), 0) == SPARE, bo, spread_o).astype(BF16)
    w_in[...] = jnp.concatenate(
        [
            in_ref[...].astype(F32).T,
            first_row(bi),
            jnp.zeros((pad - width - 8, 2 * hidden), F32),
        ],
        axis=0,
    ).astype(BF16)
    w_out_t[...] = out_ref[...].astype(F32).T.astype(BF16)

    acc_qkv[...] = jnp.zeros_like(acc_qkv)
    acc_o[...] = jnp.zeros_like(acc_o)
    acc_in[...] = jnp.zeros_like(acc_in)
    acc_out[...] = jnp.zeros_like(acc_out)
    acc_small[...] = jnp.zeros_like(acc_small)

    def unfold(tile, carry):
        at = pl.multiple_of(tile * LANE, LANE)
        xrow[pl.ds(at, LANE), :] = tok_ref[:, pl.ds(at, LANE)].T.astype(F32)
        crow[pl.ds(at, LANE), :] = cot_ref[:, pl.ds(at, LANE)].T.astype(F32)
        return carry

    lax.fori_loop(0, rows_all // LANE, unfold, 0, unroll=4)

    def norm_stats(x):
        centre = x - jnp.sum(x, -1, keepdims=True) * (1.0 / width)
        spread_sq = jnp.sum(centre * centre, -1, keepdims=True) * (1.0 / width)
        inv = lax.rsqrt(spread_sq + NORM_EPS)
        return centre * inv, inv

    def norm_back(grad, gain, hat, inv):
        scaled = grad * gain
        mean_one = jnp.sum(scaled, -1, keepdims=True) * (1.0 / width)
        mean_two = jnp.sum(scaled * hat, -1, keepdims=True) * (1.0 / width)
        return inv * (scaled - mean_one - hat * mean_two)

    def with_one(value):
        rows = value.shape[0]
        tail = jnp.where(iota((rows, pad - width), 1) == 0, 1.0, 0.0)
        return jnp.concatenate([value, tail], axis=1).astype(BF16)

    half = [
        (iota((1, LANE), 1) >> 5) == member for member in range(LANE // STRIDE)
    ]

    def pair_rows(block, pair):
        tile = block[:, (pair // 2) * LANE : (pair // 2 + 1) * LANE]
        at = 2 * (pair % 2)
        zero = jnp.zeros_like(tile)
        return jnp.concatenate(
            [jnp.where(half[at], tile, zero), jnp.where(half[at + 1], tile, zero)], axis=0
        )

    def pad_rows(value):
        rows = value.shape[0]
        return jnp.concatenate([value, jnp.zeros((LANE - rows, value.shape[1]), F32)], axis=0)

    def batch(step, n):
        at, kept, live = [], [], []
        for j in range(BATCH):
            s = order[step * BATCH + j]
            g = group_ref[s]
            limit = jnp.where(g == 0, L1, jnp.where(g == 1, L2, L3))
            at.append(pl.multiple_of(s * SLOT, 8))
            kept.append(jnp.where(iota((n, 1), 0) < limit, 1.0, 0.0))
            live.append(counts_ref[s])
        keep = jnp.concatenate(kept, axis=0)
        x = jnp.concatenate([xrow[pl.ds(a, n), :] for a in at], axis=0)
        c = jnp.concatenate([crow[pl.ds(a, n), :] for a in at], axis=0)

        hat1, inv1 = norm_stats(x)
        h1 = with_one(hat1 * g1 + b1)
        qkv = dot(h1, w_qkv[...])
        q_pad, k_low, v_low, mixed = [], [], [], []
        for j in range(BATCH):
            rows = slice(j * n, (j + 1) * n)
            q = pad_rows(qkv[rows, :pad] * q_scale).astype(BF16)
            dead = iota((n, 1), 0) >= live[j]
            k = jnp.where(
                dead & spare_lane, MASK_VALUE, qkv[rows, pad : 2 * pad]
            ).astype(BF16)
            v32 = qkv[rows, 2 * pad :]
            v = v32.astype(BF16)
            v_t = pad_rows(v32).astype(BF16).T
            q_pad.append(q)
            k_low.append(k)
            v_low.append(v)
            blocks = []
            for pair in range(HEADS // 2):
                tile = slice((pair // 2) * LANE, (pair // 2 + 1) * LANE)
                scores = dot(k[:, tile], pair_rows(q, pair), NT)
                top = jnp.max(scores, axis=0, keepdims=True)
                e = jnp.exp2(scores - top)
                p = e * (1.0 / jnp.sum(e, axis=0, keepdims=True))
                probs[j, pair, :n, :] = p
                o_t = dot(v_t[64 * pair : 64 * pair + 64, :n], p.astype(BF16))
                blocks += [o_t[:STRIDE, :LANE], o_t[STRIDE:, LANE:]]
            mixed.append(jnp.concatenate(blocks, axis=0).T[:n])
        mixed = jnp.concatenate(mixed, axis=0)
        o = jnp.where(iota((1, pad), 1) == SPARE, 1.0, mixed).astype(BF16)
        y1 = x + keep * dot(o, w_o[...])
        hat2, inv2 = norm_stats(y1)
        h2 = with_one(hat2 * g2 + b2)
        u = dot(h2, w_in[...])
        z, up = u[:, :hidden], u[:, hidden:]
        alpha, beta = 0.7978845608028654, 0.044715
        zz = z * z
        t = jnp.tanh(z * (alpha + (alpha * beta) * zz))
        half_t = 0.5 + 0.5 * t
        act = z * half_t
        slope = half_t + (z * (0.5 - 0.5 * t * t)) * (alpha + (3.0 * alpha * beta) * zz)
        hid = (act * up).astype(BF16)
        f = dot(hid, out_ref[...]) + bf
        out = y1 + keep * f
        df = keep * c
        df_low = df.astype(BF16)
        acc_small[0:8, :] += partial_sums(df)
        acc_out[...] += dot(hid, df_low, TN)
        dhid = dot(df_low, w_out_t[...])
        du = jnp.concatenate([dhid * up * slope, dhid * act], axis=1).astype(BF16)
        acc_in[...] += dot(h2, du, TN)
        dh2 = dot(du, in_ref[...])
        acc_small[8:16, :] += partial_sums(dh2 * hat2)
        acc_small[16:24, :] += partial_sums(dh2)
        dy1 = c + norm_back(dh2, g2, hat2, inv2)
        da = (keep * dy1).astype(BF16)
        acc_o[...] += dot(o, da, TN)
        do = dot(da, w_o_t[...])
        dqkv = []
        for j in range(BATCH):
            d_low = pad_rows(do[j * n : (j + 1) * n]).astype(BF16)
            k_t = pad_rows(k_low[j].astype(F32)).astype(BF16).T
            blocks, dks, dvs = [], [], []
            for pair in range(HEADS // 2):
                tile = slice((pair // 2) * LANE, (pair // 2 + 1) * LANE)
                d_pair = pair_rows(d_low, pair)
                dp = dot(v_low[j][:, tile], d_pair, NT)
                p = probs[j, pair, :n, :]
                ds = (p * (dp - jnp.sum(dp * p, axis=0, keepdims=True))).astype(BF16)
                dvs.append(dot(p.astype(BF16), d_pair))
                dks.append(dot(ds, pair_rows(q_pad[j], pair)))
                dq_t = dot(k_t[64 * pair : 64 * pair + 64, :n], ds)
                blocks += [dq_t[:STRIDE, :LANE], dq_t[STRIDE:, LANE:]]
            dq = jnp.concatenate(blocks, axis=0).T[:n] * scale
            dk = jnp.concatenate([dks[0] + dks[1], dks[2] + dks[3]], axis=1) * (1.0 / log2e)
            dv = jnp.concatenate([dvs[0] + dvs[1], dvs[2] + dvs[3]], axis=1)
            dqkv.append(jnp.concatenate([dq, dk, dv], axis=1))
        dqkv = jnp.concatenate(dqkv, axis=0).astype(BF16)
        acc_qkv[...] += dot(h1, dqkv, TN)
        dh1 = dot(dqkv, w_qkv_t[...])
        acc_small[24:32, :] += partial_sums(dh1 * hat1)
        acc_small[32:40, :] += partial_sums(dh1)
        dx = dy1 + norm_back(dh1, g1, hat1, inv1)
        for j in range(BATCH):
            xrow[pl.ds(at[j], n), :] = out[j * n : (j + 1) * n]
            crow[pl.ds(at[j], n), :] = dx[j * n : (j + 1) * n]

    def one_batch(step, carry):
        kind = group_ref[order[step * BATCH + BATCH - 1]]
        for member, n in enumerate((40, 72, 104)):
            pl.when(kind == member)(functools.partial(batch, step, n))
        return carry

    lax.fori_loop(0, samples // BATCH, one_batch, 0)

    def fold(tile, carry):
        at = pl.multiple_of(tile * LANE, LANE)
        y_ref[:, pl.ds(at, LANE)] = xrow[pl.ds(at, LANE), :].astype(BF16).T
        dx_ref[:, pl.ds(at, LANE)] = crow[pl.ds(at, LANE), :].T
        return carry

    lax.fori_loop(0, rows_all // LANE, fold, 0, unroll=4)

    def gather_heads(value):
        return lax.dot_general(
            value, spread.astype(F32), NT, precision=lax.Precision.HIGHEST,
            preferred_element_type=F32,
        )

    for member in range(3):
        g_attn_ref[member * width : (member + 1) * width, :] = gather_heads(
            acc_qkv[:width, member * pad : (member + 1) * pad]
        )
    g_attn_ref[3 * width :, :] = lax.dot_general(
        spread.astype(F32), acc_o[...], NN, precision=lax.Precision.HIGHEST,
        preferred_element_type=F32,
    )
    g_in_ref[...] = acc_in[:width, :].T
    g_out_ref[...] = acc_out[...]

    def small(member):
        return jnp.sum(acc_small[8 * member : 8 * member + 8, :], axis=0, keepdims=True)

    bias_rows = acc_qkv[width : width + 8, :]
    g_bq = gather_heads(bias_rows[:, :pad])[0:1]
    g_bv = gather_heads(bias_rows[:, 2 * pad :])[0:1]
    g_bo = acc_o[SPARE : SPARE + 8, :][0:1]
    flat = jnp.concatenate(
        [small(3), small(4), small(1), small(2), g_bq, g_bv, g_bo, small(0),
         acc_in[width : width + 8, :][0:1]],
        axis=1,
    )
    for row in range(16):
        g_vec_ref[row : row + 1, :] = flat[:, row * LANE : (row + 1) * LANE]


def layer(group, counts, tokens_t, cotangent_t, attn, ffn_in, ffn_out, vec):
    width, rows = tokens_t.shape
    hidden = ffn_out.shape[0]
    pad = HEADS * STRIDE
    vmem = pl.BlockSpec(memory_space=pltpu.VMEM)
    smem = pl.BlockSpec(memory_space=pltpu.SMEM)
    return pl.pallas_call(
        layer_kernel,
        name="layer",
        out_shape=(
            jax.ShapeDtypeStruct((width, rows), BF16),
            jax.ShapeDtypeStruct((width, rows), F32),
            jax.ShapeDtypeStruct((4 * width, width), F32),
            jax.ShapeDtypeStruct((2 * hidden, width), F32),
            jax.ShapeDtypeStruct((hidden, width), F32),
            jax.ShapeDtypeStruct((16, LANE), F32),
        ),
        in_specs=[smem, smem] + [vmem] * 6,
        out_specs=[vmem] * 6,
        scratch_shapes=[
            pltpu.SMEM((group.shape[0],), jnp.int32),
            pltpu.SMEM((4,), jnp.int32),
            pltpu.VMEM((rows, width), F32),
            pltpu.VMEM((rows, width), F32),
            pltpu.VMEM((pad, 3 * pad), BF16),
            pltpu.VMEM((3 * pad, width), BF16),
            pltpu.VMEM((pad, width), BF16),
            pltpu.VMEM((width, pad), BF16),
            pltpu.VMEM((pad, 2 * hidden), BF16),
            pltpu.VMEM((width, hidden), BF16),
            pltpu.VMEM((BATCH, HEADS // 2, SLOT, 2 * LANE), F32),
            pltpu.VMEM((pad, 3 * pad), F32),
            pltpu.VMEM((pad, width), F32),
            pltpu.VMEM((pad, 2 * hidden), F32),
            pltpu.VMEM((hidden, width), F32),
            pltpu.VMEM((40, width), F32),
        ],
        compiler_params=pltpu.CompilerParams(vmem_limit_bytes=60 * 2**20),
    )(group, counts, tokens_t, cotangent_t, attn, ffn_in, ffn_out, vec)


def local(
    tokens,
    cotangent,
    group,
    counts,
    attn_w,
    ffn_in,
    ffn_out,
    vectors,
    attn_m,
    attn_v,
    in_m,
    in_v,
    out_m,
    out_v,
    vec_m,
    vec_v,
):
    masters = (attn_w, ffn_in, ffn_out, vectors)
    full = [
        lax.all_gather(value.astype(BF16), "wide", axis=0, tiled=True) for value in masters
    ]
    out_t, grad_t, *grads = layer(
        group, counts, tokens.T, cotangent.T, full[0], full[1], full[2],
        full[3].reshape(16, LANE),
    )
    grads[3] = grads[3].reshape(vectors.shape[0] * lax.axis_size("wide"))
    owned = [lax.psum_scatter(g, "wide", scatter_dimension=0, tiled=True) for g in grads]
    owned = lax.psum(tuple(owned), "narrow")
    firsts = (attn_m, in_m, out_m, vec_m)
    seconds = (attn_v, in_v, out_v, vec_v)
    results = []
    for member in range(4):
        results += adamw_update(
            masters[member], owned[member], firsts[member], seconds[member]
        )
    return (out_t.T, grad_t.T, *results)


def solution(mesh):
    rows = P(("wide", "narrow"), None)
    samples = P(("wide", "narrow"))
    weight = P("wide", None)
    vector = P("wide")
    return jax.shard_map(
        local,
        mesh=mesh,
        in_specs=(rows, rows, samples, samples, weight, weight, weight, vector)
        + (weight,) * 6
        + (vector,) * 2,
        out_specs=(rows, rows) + (weight,) * 9 + (vector,) * 3,
        check_vma=False,
    )
```

```python
import functools
import math

import jax
import jax.numpy as jnp
from jax import lax
from jax.experimental import pallas as pl
from jax.experimental.pallas import tpu as pltpu
from jax.sharding import PartitionSpec as P

HEADS = 8
SLOT = 104
L1 = 40
L2 = 68
L3 = 100
STEP = 10

NORM_EPS = 1e-05
BETA_ONE = 0.9
BETA_TWO = 0.999
ADAM_EPS = 1e-08
LEARN_RATE = 0.1
WEIGHT_DECAY = 0.01
MASK_VALUE = -1e30

F32 = jnp.float32
BF16 = jnp.bfloat16
LANE = 128
MESH = pl.DeviceIdType.MESH
STRIDE = 32
NN = (((1,), (0,)), ((), ()))
NT = (((1,), (1,)), ((), ()))
TN = (((0,), (0,)), ((), ()))
BATCH = 4
SPARE = 24


def adamw_update(master, gradient, moment, square):
    moment_new = BETA_ONE * moment + (1.0 - BETA_ONE) * gradient
    square_new = BETA_TWO * square + (1.0 - BETA_TWO) * gradient * gradient
    moment_hat = moment_new / (1.0 - BETA_ONE**STEP)
    square_hat = square_new / (1.0 - BETA_TWO**STEP)
    master_new = master - LEARN_RATE * (
        moment_hat / (jnp.sqrt(square_hat) + ADAM_EPS) + WEIGHT_DECAY * master
    )
    return (master_new, moment_new, square_new)


def dot(a, b, dims=NN):
    return lax.dot_general(a, b, dims, preferred_element_type=F32)


def iota(shape, dim):
    return lax.broadcasted_iota(jnp.int32, shape, dim)


def partial_sums(value):
    rows, cols = value.shape
    return jnp.sum(value.reshape(rows // 8, 8, cols), axis=0)


def piece(vec, member, width):
    start = member * width
    parts, at = [], start
    while at < start + width:
        row, lane = divmod(at, LANE)
        take = min(LANE - lane, start + width - at)
        parts.append(vec[row : row + 1, lane : lane + take])
        at += take
    return jnp.concatenate(parts, axis=1)


def layer_kernel(
    group_ref,
    counts_ref,
    tok_ref,
    cot_ref,
    attn_ref,
    in_ref,
    out_ref,
    vec_ref,
    y_ref,
    dx_ref,
    g_attn_ref,
    g_in_ref,
    g_out_ref,
    g_vec_ref,
    order,
    slots,
    xrow,
    crow,
    w_qkv,
    w_qkv_t,
    w_o,
    w_o_t,
    w_in,
    w_out_t,
    probs,
    acc_qkv,
    acc_o,
    acc_in,
    acc_out,
    acc_small,
):
    width = attn_ref.shape[1]
    hidden = out_ref.shape[0]
    samples = group_ref.shape[0]
    rows_all = tok_ref.shape[1]
    head = width // HEADS
    pad = HEADS * STRIDE
    scale = 1.0 / math.sqrt(head)
    log2e = math.log2(math.e)
    q_scale = scale * log2e

    slots[0] = 0
    slots[1] = 0
    slots[2] = 0

    def count(s, carry):
        g = group_ref[s]
        slots[g] = slots[g] + 1
        return carry

    lax.fori_loop(0, samples, count, 0)
    first = slots[0]
    second = slots[1]
    slots[0] = 0
    slots[1] = first
    slots[2] = first + second

    def place(s, carry):
        g = group_ref[s]
        at = slots[g]
        order[at] = s
        slots[g] = at + 1
        return carry

    lax.fori_loop(0, samples, place, 0)

    spread_row = iota((width, pad), 0)
    spread_col = iota((width, pad), 1)
    within = spread_col & (STRIDE - 1)
    spread = jnp.where(
        (within < head) & (spread_row == (spread_col >> 5) * head + within), 1.0, 0.0
    ).astype(BF16)
    vec = jnp.concatenate([vec_ref[row] for row in range(vec_ref.shape[0])], axis=0)
    pieces = [piece(vec, member, width) for member in range(8)]
    g1, b1, g2, b2, bq, bv, bo, bf = pieces
    bi = jnp.concatenate([vec[row : row + 1] for row in range(12, 16)], axis=1)
    zero_rows = jnp.zeros((pad - width - 8, pad), F32)

    def first_row(row):
        return jnp.concatenate([row, jnp.zeros((7, row.shape[1]), F32)], axis=0)

    spare_lane = (iota((1, pad), 1) & (STRIDE - 1)) == SPARE
    for member in range(3):
        spread_w = dot(attn_ref[member * width : (member + 1) * width, :], spread)
        if member == 0:
            bias = dot(bq.astype(BF16), spread) + jnp.where(spare_lane, 1.0, 0.0)
        elif member == 1:
            bias = jnp.zeros((1, pad), F32)
        else:
            bias = dot(bv.astype(BF16), spread)
        w_qkv[:, member * pad : (member + 1) * pad] = jnp.concatenate(
            [spread_w, first_row(bias), zero_rows], axis=0
        ).astype(BF16)
        w_qkv_t[member * pad : (member + 1) * pad, :] = spread_w.T.astype(BF16)
    spread_o = dot(spread, attn_ref[3 * width :, :], TN)
    w_o_t[...] = spread_o.T.astype(BF16)
    w_o[...] = jnp.where(iota((pad, width), 0) == SPARE, bo, spread_o).astype(BF16)
    w_in[...] = jnp.concatenate(
        [
            in_ref[...].astype(F32).T,
            first_row(bi),
            jnp.zeros((pad - width - 8, 2 * hidden), F32),
        ],
        axis=0,
    ).astype(BF16)
    w_out_t[...] = out_ref[...].astype(F32).T.astype(BF16)

    acc_qkv[...] = jnp.zeros_like(acc_qkv)
    acc_o[...] = jnp.zeros_like(acc_o)
    acc_in[...] = jnp.zeros_like(acc_in)
    acc_out[...] = jnp.zeros_like(acc_out)
    acc_small[...] = jnp.zeros_like(acc_small)

    def unfold(tile, carry):
        at = pl.multiple_of(tile * LANE, LANE)
        xrow[pl.ds(at, LANE), :] = tok_ref[:, pl.ds(at, LANE)].T.astype(F32)
        crow[pl.ds(at, LANE), :] = cot_ref[:, pl.ds(at, LANE)].T.astype(F32)
        return carry

    lax.fori_loop(0, rows_all // LANE, unfold, 0, unroll=4)

    def norm_stats(x):
        centre = x - jnp.sum(x, -1, keepdims=True) * (1.0 / width)
        spread_sq = jnp.sum(centre * centre, -1, keepdims=True) * (1.0 / width)
        inv = lax.rsqrt(spread_sq + NORM_EPS)
        return centre * inv, inv

    def norm_back(grad, gain, hat, inv):
        scaled = grad * gain
        mean_one = jnp.sum(scaled, -1, keepdims=True) * (1.0 / width)
        mean_two = jnp.sum(scaled * hat, -1, keepdims=True) * (1.0 / width)
        return inv * (scaled - mean_one - hat * mean_two)

    def with_one(value):
        rows = value.shape[0]
        tail = jnp.where(iota((rows, pad - width), 1) == 0, 1.0, 0.0)
        return jnp.concatenate([value, tail], axis=1).astype(BF16)

    half = [
        (iota((1, LANE), 1) >> 5) == member for member in range(LANE // STRIDE)
    ]

    def pair_rows(block, pair):
        tile = block[:, (pair // 2) * LANE : (pair // 2 + 1) * LANE]
        at = 2 * (pair % 2)
        zero = jnp.zeros_like(tile)
        return jnp.concatenate(
            [jnp.where(half[at], tile, zero), jnp.where(half[at + 1], tile, zero)], axis=0
        )

    def pad_rows(value):
        rows = value.shape[0]
        return jnp.concatenate([value, jnp.zeros((LANE - rows, value.shape[1]), F32)], axis=0)

    def batch(step, n):
        at, kept, live = [], [], []
        for j in range(BATCH):
            s = order[step * BATCH + j]
            g = group_ref[s]
            limit = jnp.where(g == 0, L1, jnp.where(g == 1, L2, L3))
            at.append(pl.multiple_of(s * SLOT, 8))
            kept.append(jnp.where(iota((n, 1), 0) < limit, 1.0, 0.0))
            live.append(counts_ref[s])
        keep = jnp.concatenate(kept, axis=0)
        x = jnp.concatenate([xrow[pl.ds(a, n), :] for a in at], axis=0)
        c = jnp.concatenate([crow[pl.ds(a, n), :] for a in at], axis=0)

        hat1, inv1 = norm_stats(x)
        h1 = with_one(hat1 * g1 + b1)
        qkv = dot(h1, w_qkv[...])
        q_pad, k_low, v_low, mixed = [], [], [], []
        for j in range(BATCH):
            rows = slice(j * n, (j + 1) * n)
            q = pad_rows(qkv[rows, :pad] * q_scale).astype(BF16)
            dead = iota((n, 1), 0) >= live[j]
            k = jnp.where(
                dead & spare_lane, MASK_VALUE, qkv[rows, pad : 2 * pad]
            ).astype(BF16)
            v32 = qkv[rows, 2 * pad :]
            v = v32.astype(BF16)
            v_t = pad_rows(v32).astype(BF16).T
            q_pad.append(q)
            k_low.append(k)
            v_low.append(v)
            blocks = []
            for pair in range(HEADS // 2):
                tile = slice((pair // 2) * LANE, (pair // 2 + 1) * LANE)
                scores = dot(k[:, tile], pair_rows(q, pair), NT)
                top = jnp.max(scores, axis=0, keepdims=True)
                e = jnp.exp2(scores - top)
                p = e * (1.0 / jnp.sum(e, axis=0, keepdims=True))
                probs[j, pair, :n, :] = p
                o_t = dot(v_t[64 * pair : 64 * pair + 64, :n], p.astype(BF16))
                blocks += [o_t[:STRIDE, :LANE], o_t[STRIDE:, LANE:]]
            mixed.append(jnp.concatenate(blocks, axis=0).T[:n])
        mixed = jnp.concatenate(mixed, axis=0)
        o = jnp.where(iota((1, pad), 1) == SPARE, 1.0, mixed).astype(BF16)
        y1 = x + keep * dot(o, w_o[...])
        hat2, inv2 = norm_stats(y1)
        h2 = with_one(hat2 * g2 + b2)
        u = dot(h2, w_in[...])
        z, up = u[:, :hidden], u[:, hidden:]
        alpha, beta = 0.7978845608028654, 0.044715
        zz = z * z
        t = jnp.tanh(z * (alpha + (alpha * beta) * zz))
        half_t = 0.5 + 0.5 * t
        act = z * half_t
        slope = half_t + (z * (0.5 - 0.5 * t * t)) * (alpha + (3.0 * alpha * beta) * zz)
        hid = (act * up).astype(BF16)
        f = dot(hid, out_ref[...]) + bf
        out = y1 + keep * f
        df = keep * c
        df_low = df.astype(BF16)
        acc_small[0:8, :] += partial_sums(df)
        acc_out[...] += dot(hid, df_low, TN)
        dhid = dot(df_low, w_out_t[...])
        du = jnp.concatenate([dhid * up * slope, dhid * act], axis=1).astype(BF16)
        acc_in[...] += dot(h2, du, TN)
        dh2 = dot(du, in_ref[...])
        acc_small[8:16, :] += partial_sums(dh2 * hat2)
        acc_small[16:24, :] += partial_sums(dh2)
        dy1 = c + norm_back(dh2, g2, hat2, inv2)
        da = (keep * dy1).astype(BF16)
        acc_o[...] += dot(o, da, TN)
        do = dot(da, w_o_t[...])
        dqkv = []
        for j in range(BATCH):
            d_low = pad_rows(do[j * n : (j + 1) * n]).astype(BF16)
            k_t = pad_rows(k_low[j].astype(F32)).astype(BF16).T
            blocks, dks, dvs = [], [], []
            for pair in range(HEADS // 2):
                tile = slice((pair // 2) * LANE, (pair // 2 + 1) * LANE)
                d_pair = pair_rows(d_low, pair)
                dp = dot(v_low[j][:, tile], d_pair, NT)
                p = probs[j, pair, :n, :]
                ds = (p * (dp - jnp.sum(dp * p, axis=0, keepdims=True))).astype(BF16)
                dvs.append(dot(p.astype(BF16), d_pair))
                dks.append(dot(ds, pair_rows(q_pad[j], pair)))
                dq_t = dot(k_t[64 * pair : 64 * pair + 64, :n], ds)
                blocks += [dq_t[:STRIDE, :LANE], dq_t[STRIDE:, LANE:]]
            dq = jnp.concatenate(blocks, axis=0).T[:n] * scale
            dk = jnp.concatenate([dks[0] + dks[1], dks[2] + dks[3]], axis=1) * (1.0 / log2e)
            dv = jnp.concatenate([dvs[0] + dvs[1], dvs[2] + dvs[3]], axis=1)
            dqkv.append(jnp.concatenate([dq, dk, dv], axis=1))
        dqkv = jnp.concatenate(dqkv, axis=0).astype(BF16)
        acc_qkv[...] += dot(h1, dqkv, TN)
        dh1 = dot(dqkv, w_qkv_t[...])
        acc_small[24:32, :] += partial_sums(dh1 * hat1)
        acc_small[32:40, :] += partial_sums(dh1)
        dx = dy1 + norm_back(dh1, g1, hat1, inv1)
        for j in range(BATCH):
            xrow[pl.ds(at[j], n), :] = out[j * n : (j + 1) * n]
            crow[pl.ds(at[j], n), :] = dx[j * n : (j + 1) * n]

    def one_batch(step, carry):
        kind = group_ref[order[step * BATCH + BATCH - 1]]
        for member, n in enumerate((40, 72, 104)):
            pl.when(kind == member)(functools.partial(batch, step, n))
        return carry

    lax.fori_loop(0, samples // BATCH, one_batch, 0)

    def fold(tile, carry):
        at = pl.multiple_of(tile * LANE, LANE)
        y_ref[:, pl.ds(at, LANE)] = xrow[pl.ds(at, LANE), :].astype(BF16).T
        dx_ref[:, pl.ds(at, LANE)] = crow[pl.ds(at, LANE), :].T
        return carry

    lax.fori_loop(0, rows_all // LANE, fold, 0, unroll=4)

    def gather_heads(value):
        return lax.dot_general(
            value, spread.astype(F32), NT, precision=lax.Precision.HIGHEST,
            preferred_element_type=F32,
        )

    for member in range(3):
        g_attn_ref[member * width : (member + 1) * width, :] = gather_heads(
            acc_qkv[:width, member * pad : (member + 1) * pad]
        )
    g_attn_ref[3 * width :, :] = lax.dot_general(
        spread.astype(F32), acc_o[...], NN, precision=lax.Precision.HIGHEST,
        preferred_element_type=F32,
    )
    g_in_ref[...] = acc_in[:width, :].T
    g_out_ref[...] = acc_out[...]

    def small(member):
        return jnp.sum(acc_small[8 * member : 8 * member + 8, :], axis=0, keepdims=True)

    bias_rows = acc_qkv[width : width + 8, :]
    g_bq = gather_heads(bias_rows[:, :pad])[0:1]
    g_bv = gather_heads(bias_rows[:, 2 * pad :])[0:1]
    g_bo = acc_o[SPARE : SPARE + 8, :][0:1]
    flat = jnp.concatenate(
        [small(3), small(4), small(1), small(2), g_bq, g_bv, g_bo, small(0),
         acc_in[width : width + 8, :][0:1]],
        axis=1,
    )
    for row in range(16):
        g_vec_ref[row] = flat[:, row * LANE : (row + 1) * LANE]


def layer(group, counts, tokens_t, cotangent_t, attn, ffn_in, ffn_out, vec):
    width, rows = tokens_t.shape
    hidden = ffn_out.shape[0]
    pad = HEADS * STRIDE
    vmem = pl.BlockSpec(memory_space=pltpu.VMEM)
    smem = pl.BlockSpec(memory_space=pltpu.SMEM)
    return pl.pallas_call(
        layer_kernel,
        name="layer",
        out_shape=(
            jax.ShapeDtypeStruct((width, rows), BF16),
            jax.ShapeDtypeStruct((width, rows), F32),
            jax.ShapeDtypeStruct((4 * width, width), F32),
            jax.ShapeDtypeStruct((2 * hidden, width), F32),
            jax.ShapeDtypeStruct((hidden, width), F32),
            jax.ShapeDtypeStruct((16, 1, LANE), F32),
        ),
        in_specs=[smem, smem] + [vmem] * 6,
        out_specs=[vmem] * 6,
        scratch_shapes=[
            pltpu.SMEM((group.shape[0],), jnp.int32),
            pltpu.SMEM((4,), jnp.int32),
            pltpu.VMEM((rows, width), F32),
            pltpu.VMEM((rows, width), F32),
            pltpu.VMEM((pad, 3 * pad), BF16),
            pltpu.VMEM((3 * pad, width), BF16),
            pltpu.VMEM((pad, width), BF16),
            pltpu.VMEM((width, pad), BF16),
            pltpu.VMEM((pad, 2 * hidden), BF16),
            pltpu.VMEM((width, hidden), BF16),
            pltpu.VMEM((BATCH, HEADS // 2, SLOT, 2 * LANE), F32),
            pltpu.VMEM((pad, 3 * pad), F32),
            pltpu.VMEM((pad, width), F32),
            pltpu.VMEM((pad, 2 * hidden), F32),
            pltpu.VMEM((hidden, width), F32),
            pltpu.VMEM((40, width), F32),
        ],
        compiler_params=pltpu.CompilerParams(vmem_limit_bytes=60 * 2**20),
    )(group, counts, tokens_t, cotangent_t, attn, ffn_in, ffn_out, vec)


def greet(size, me, core):
    barrier = pltpu.get_barrier_semaphore()

    def signal(k, carry):
        pl.semaphore_signal(
            barrier, inc=1, device_id=(lax.rem(me + k, size), core), device_id_type=MESH
        )
        return carry

    lax.fori_loop(1, size, signal, 0)
    pl.semaphore_signal(barrier, inc=1, device_id=(me, 1 - core), device_id_type=MESH)
    pl.semaphore_wait(barrier, size)


def over(low, high, body):
    def step(k, carry):
        body(k)
        return carry

    lax.fori_loop(low, high, step, 0)


def gather_kernel(
    attn_ref, in_ref, out_ref, vec_ref,
    attn_all, in_all, out_all, vec_all,
    send_sem, recv_sem, pass_sem, got_sem,
):
    size = attn_all.shape[0]
    me, core = lax.axis_index("wide"), lax.axis_index("narrow")
    attn_all[me] = attn_ref[...].astype(BF16)
    in_all[me] = in_ref[...].astype(BF16)
    out_all[me] = out_ref[...].astype(BF16)
    vec_all[me] = vec_ref[...].astype(BF16).astype(F32)
    greet(size, me, core)

    def role(mine, theirs):
        def to_peer(ref, r, owner, k):
            return pltpu.make_async_remote_copy(
                src_ref=ref.at[owner],
                dst_ref=ref.at[owner],
                send_sem=send_sem.at[r, k],
                recv_sem=recv_sem.at[r, owner],
                device_id=(lax.rem(me + k, size), core),
                device_id_type=MESH,
            )

        def to_twin(ref, r, owner):
            return pltpu.make_async_remote_copy(
                src_ref=ref.at[owner],
                dst_ref=ref.at[owner],
                send_sem=pass_sem.at[r, owner],
                recv_sem=got_sem.at[r, owner],
                device_id=(me, 1 - core),
                device_id_type=MESH,
            )

        def start(k):
            for r, ref in enumerate(mine):
                to_peer(ref, r, me, k).start()

        def forward(k):
            owner = lax.rem(me + size - k, size)
            for r, ref in enumerate(mine):
                to_peer(ref, r, owner, k).wait_recv()
                to_twin(ref, r, owner).start()

        def finish(k):
            owner = lax.rem(me + size - k, size)
            for r, ref in enumerate(mine):
                to_peer(ref, r, me, k).wait_send()
                to_twin(ref, r, owner).wait_send()
            for r, ref in enumerate(theirs):
                to_twin(ref, r, owner).wait_recv()

        over(1, size, start)
        over(1, size, forward)
        over(1, size, finish)

    pl.when(core == 0)(lambda: role((attn_all, vec_all), (in_all, out_all)))
    pl.when(core != 0)(lambda: role((in_all, out_all), (attn_all, vec_all)))


def gather(size, attn, ffn_in, ffn_out, vec):
    vmem = pl.BlockSpec(memory_space=pltpu.VMEM)
    return pl.pallas_call(
        gather_kernel,
        name="gather",
        out_shape=tuple(
            jax.ShapeDtypeStruct((size, *value.shape), BF16)
            for value in (attn, ffn_in, ffn_out)
        )
        + (jax.ShapeDtypeStruct((size, *vec.shape), F32),),
        in_specs=[vmem] * 4,
        out_specs=[vmem] * 4,
        scratch_shapes=[pltpu.SemaphoreType.DMA((2, size))] * 4,
        compiler_params=pltpu.CompilerParams(
            collective_id=0, has_side_effects=True, vmem_limit_bytes=32 * 2**20
        ),
    )(attn, ffn_in, ffn_out, vec)


def reduce_kernel(
    g_attn, g_in, g_out, g_vec,
    s_attn, s_in, s_out, s_vec,
    stage_attn, stage_in, stage_out, stage_vec,
    twin_attn, twin_in, twin_out, twin_vec,
    both_attn, both_in, both_out, both_vec,
    peer_attn, peer_in, peer_out, peer_vec,
    pass_sem, got_sem, send_sem, recv_sem, last_send, last_recv,
):
    size = g_attn.shape[0]
    me, core = lax.axis_index("wide"), lax.axis_index("narrow")
    greet(size, me, core)

    def role(mine, theirs):
        def to_twin(pack, r, owner):
            return pltpu.make_async_remote_copy(
                src_ref=pack[2].at[owner],
                dst_ref=pack[3].at[owner],
                send_sem=pass_sem.at[r, owner],
                recv_sem=got_sem.at[r, owner],
                device_id=(me, 1 - core),
                device_id_type=MESH,
            )

        def to_peer(pack, r, k, source):
            return pltpu.make_async_remote_copy(
                src_ref=pack[4].at[lax.rem(me + k, size)],
                dst_ref=pack[5].at[source],
                send_sem=send_sem.at[r, k],
                recv_sem=recv_sem.at[r, source],
                device_id=(lax.rem(me + k, size), core),
                device_id_type=MESH,
            )

        def result(pack, r):
            return pltpu.make_async_remote_copy(
                src_ref=pack[1],
                dst_ref=pack[1],
                send_sem=last_send.at[r],
                recv_sem=last_recv.at[r],
                device_id=(me, 1 - core),
                device_id_type=MESH,
            )

        def give(k):
            owner = lax.rem(me + k, size)
            for r, pack in enumerate(theirs):
                pack[2][owner] = pack[0][owner].astype(pack[2].dtype)
                to_twin(pack, r, owner).start()

        def send(k):
            owner = lax.rem(me + k, size)
            for r, pack in enumerate(mine):
                to_twin(pack, r, owner).wait_recv()
                total = pack[0][owner] + pack[3][owner].astype(F32)
                pack[4][owner] = total.astype(pack[4].dtype)
                to_peer(pack, r, k, me).start()

        def take(k):
            source = lax.rem(me + size - k, size)
            for r, pack in enumerate(mine):
                to_peer(pack, r, k, source).wait_recv()
                pack[1][...] += pack[5][source].astype(F32)

        def finish(k):
            owner = lax.rem(me + k, size)
            for r, pack in enumerate(theirs):
                to_twin(pack, r, owner).wait_send()

        def finish_peer(k):
            for r, pack in enumerate(mine):
                to_peer(pack, r, k, me).wait_send()

        over(1, size + 1, give)
        over(1, size, send)
        for r, pack in enumerate(mine):
            to_twin(pack, r, me).wait_recv()
            pack[1][...] = pack[0][me] + pack[3][me].astype(F32)
        over(1, size, take)
        for r, pack in enumerate(mine):
            result(pack, r).start()
        over(1, size + 1, finish)
        over(1, size, finish_peer)
        for r, pack in enumerate(mine):
            result(pack, r).wait_send()
        for r, pack in enumerate(theirs):
            result(pack, r).wait_recv()

    attn = (g_attn, s_attn, stage_attn, twin_attn, both_attn, peer_attn)
    into = (g_in, s_in, stage_in, twin_in, both_in, peer_in)
    outof = (g_out, s_out, stage_out, twin_out, both_out, peer_out)
    vecs = (g_vec, s_vec, stage_vec, twin_vec, both_vec, peer_vec)
    pl.when(core == 0)(lambda: role((attn, vecs), (into, outof)))
    pl.when(core != 0)(lambda: role((into, outof), (attn, vecs)))


def reduce_scatter(g_attn, g_in, g_out, g_vec):
    grads = (g_attn, g_in, g_out, g_vec)
    size = g_attn.shape[0]
    vmem = pl.BlockSpec(memory_space=pltpu.VMEM)
    buffers = [
        pltpu.VMEM(value.shape, F32 if value is g_vec else BF16) for value in grads
    ]
    return pl.pallas_call(
        reduce_kernel,
        name="reduce",
        out_shape=tuple(jax.ShapeDtypeStruct(value.shape[1:], F32) for value in grads),
        in_specs=[vmem] * 4,
        out_specs=[vmem] * 4,
        scratch_shapes=buffers * 4
        + [pltpu.SemaphoreType.DMA((2, size))] * 4
        + [pltpu.SemaphoreType.DMA((2,))] * 2,
        compiler_params=pltpu.CompilerParams(
            collective_id=1, has_side_effects=True, vmem_limit_bytes=48 * 2**20
        ),
    )(*grads)


def adamw_kernel(*refs):
    for member in range(4):
        master, first, second, grad = (refs[4 * kind + member][...] for kind in range(4))
        results = adamw_update(master, grad, first, second)
        for kind in range(3):
            refs[16 + 3 * member + kind][...] = results[kind]


def adamw(masters, firsts, seconds, grads):
    vmem = pl.BlockSpec(memory_space=pltpu.VMEM)
    return pl.pallas_call(
        adamw_kernel,
        name="adamw",
        out_shape=tuple(
            jax.ShapeDtypeStruct(value.shape, F32) for value in masters for kind in range(3)
        ),
        in_specs=[vmem] * 16,
        out_specs=[vmem] * 12,
    )(*masters, *firsts, *seconds, *grads)


def local(
    tokens,
    cotangent,
    group,
    counts,
    attn_w,
    ffn_in,
    ffn_out,
    vectors,
    attn_m,
    attn_v,
    in_m,
    in_v,
    out_m,
    out_v,
    vec_m,
    vec_v,
):
    size = lax.axis_size("wide")
    width = tokens.shape[1]
    masters = (attn_w, ffn_in, ffn_out, vectors[None])
    attn, into, outof, vec = gather(size, *masters)
    out_t, grad_t, *grads = layer(
        group,
        counts,
        tokens.T,
        cotangent.T,
        attn.reshape(-1, width),
        into.reshape(-1, width),
        outof.reshape(-1, width),
        vec.reshape(-1, 1, LANE),
    )
    sums = reduce_scatter(
        *[g.reshape(size, -1, width) for g in grads[:3]], grads[3].reshape(size, 1, -1)
    )
    results = adamw(
        masters, (attn_m, in_m, out_m, vec_m[None]), (attn_v, in_v, out_v, vec_v[None]), sums
    )
    return (out_t.T, grad_t.T, *results[:9], *[value[0] for value in results[9:]])


def solution(mesh):
    rows = P(("wide", "narrow"), None)
    samples = P(("wide", "narrow"))
    weight = P("wide", None)
    vector = P("wide")
    return jax.shard_map(
        local,
        mesh=mesh,
        in_specs=(rows, rows, samples, samples, weight, weight, weight, vector)
        + (weight,) * 6
        + (vector,) * 2,
        out_specs=(rows, rows) + (weight,) * 9 + (vector,) * 3,
        check_vma=False,
    )
```

```python
import functools
import math

import jax
import jax.numpy as jnp
from jax import lax
from jax.experimental import pallas as pl
from jax.experimental.pallas import tpu as pltpu
from jax.sharding import PartitionSpec as P

HEADS = 8
SLOT = 104
L1 = 40
L2 = 68
L3 = 100
STEP = 10

NORM_EPS = 1e-05
BETA_ONE = 0.9
BETA_TWO = 0.999
ADAM_EPS = 1e-08
LEARN_RATE = 0.1
WEIGHT_DECAY = 0.01
MASK_VALUE = -1e30

F32 = jnp.float32
BF16 = jnp.bfloat16
LANE = 128
MESH = pl.DeviceIdType.MESH
STRIDE = 32
NN = (((1,), (0,)), ((), ()))
NT = (((1,), (1,)), ((), ()))
TN = (((0,), (0,)), ((), ()))
BATCH = 8
SPARE = 24


def adamw_update(master, gradient, moment, square):
    moment_new = BETA_ONE * moment + (1.0 - BETA_ONE) * gradient
    square_new = BETA_TWO * square + (1.0 - BETA_TWO) * gradient * gradient
    moment_hat = moment_new / (1.0 - BETA_ONE**STEP)
    square_hat = square_new / (1.0 - BETA_TWO**STEP)
    master_new = master - LEARN_RATE * (
        moment_hat / (jnp.sqrt(square_hat) + ADAM_EPS) + WEIGHT_DECAY * master
    )
    return (master_new, moment_new, square_new)


def dot(a, b, dims=NN):
    return lax.dot_general(a, b, dims, preferred_element_type=F32)


def iota(shape, dim):
    return lax.broadcasted_iota(jnp.int32, shape, dim)


def partial_sums(value):
    rows, cols = value.shape
    return jnp.sum(value.reshape(rows // 8, 8, cols), axis=0)


def piece(vec, member, width):
    start = member * width
    parts, at = [], start
    while at < start + width:
        row, lane = divmod(at, LANE)
        take = min(LANE - lane, start + width - at)
        parts.append(vec[row : row + 1, lane : lane + take])
        at += take
    return jnp.concatenate(parts, axis=1)


def layer_kernel(
    group_ref,
    counts_ref,
    tok_ref,
    cot_ref,
    attn_ref,
    in_ref,
    out_ref,
    vec_ref,
    y_ref,
    dx_ref,
    g_attn_ref,
    g_in_ref,
    g_out_ref,
    g_vec_ref,
    order,
    slots,
    xrow,
    crow,
    w_qkv,
    w_qkv_t,
    w_o,
    w_o_t,
    w_in,
    w_out_t,
    probs,
    probs_low,
    scores,
    ds_low,
    q_pairs,
    d_pairs,
    k_rows,
    v_rows,
    k_cols,
    v_cols,
    cols,
    acc_qkv,
    acc_o,
    acc_in,
    acc_out,
    acc_small,
):
    width = attn_ref.shape[1]
    hidden = out_ref.shape[0]
    samples = group_ref.shape[0]
    rows_all = tok_ref.shape[1]
    head = width // HEADS
    pad = HEADS * STRIDE
    scale = 1.0 / math.sqrt(head)
    log2e = math.log2(math.e)
    q_scale = scale * log2e

    slots[0] = 0
    slots[1] = 0
    slots[2] = 0

    def count(s, carry):
        g = group_ref[s]
        slots[g] = slots[g] + 1
        return carry

    lax.fori_loop(0, samples, count, 0)
    first = slots[0]
    second = slots[1]
    slots[0] = 0
    slots[1] = first
    slots[2] = first + second

    def place(s, carry):
        g = group_ref[s]
        at = slots[g]
        order[at] = s
        slots[g] = at + 1
        return carry

    lax.fori_loop(0, samples, place, 0)

    spread_row = iota((width, pad), 0)
    spread_col = iota((width, pad), 1)
    within = spread_col & (STRIDE - 1)
    spread = jnp.where(
        (within < head) & (spread_row == (spread_col >> 5) * head + within), 1.0, 0.0
    ).astype(BF16)
    vec = jnp.concatenate([vec_ref[row] for row in range(vec_ref.shape[0])], axis=0)
    pieces = [piece(vec, member, width) for member in range(8)]
    g1, b1, g2, b2, bq, bv, bo, bf = pieces
    bi = jnp.concatenate([vec[row : row + 1] for row in range(12, 16)], axis=1)
    zero_rows = jnp.zeros((pad - width - 8, pad), F32)

    def first_row(row):
        return jnp.concatenate([row, jnp.zeros((7, row.shape[1]), F32)], axis=0)

    spare_lane = (iota((1, pad), 1) & (STRIDE - 1)) == SPARE
    for member in range(3):
        spread_w = dot(attn_ref[member * width : (member + 1) * width, :], spread)
        if member == 0:
            bias = dot(bq.astype(BF16), spread) + jnp.where(spare_lane, 1.0, 0.0)
        elif member == 1:
            bias = jnp.zeros((1, pad), F32)
        else:
            bias = dot(bv.astype(BF16), spread)
        w_qkv[:, member * pad : (member + 1) * pad] = jnp.concatenate(
            [spread_w, first_row(bias), zero_rows], axis=0
        ).astype(BF16)
        w_qkv_t[member * pad : (member + 1) * pad, :] = spread_w.T.astype(BF16)
    spread_o = dot(spread, attn_ref[3 * width :, :], TN)
    w_o_t[...] = spread_o.T.astype(BF16)
    w_o[...] = jnp.where(iota((pad, width), 0) == SPARE, bo, spread_o).astype(BF16)
    w_in[...] = jnp.concatenate(
        [
            in_ref[...].astype(F32).T,
            first_row(bi),
            jnp.zeros((pad - width - 8, 2 * hidden), F32),
        ],
        axis=0,
    ).astype(BF16)
    w_out_t[...] = out_ref[...].astype(F32).T.astype(BF16)

    acc_qkv[...] = jnp.zeros_like(acc_qkv)
    acc_o[...] = jnp.zeros_like(acc_o)
    acc_in[...] = jnp.zeros_like(acc_in)
    acc_out[...] = jnp.zeros_like(acc_out)
    acc_small[...] = jnp.zeros_like(acc_small)

    def unfold(tile, carry):
        at = pl.multiple_of(tile * LANE, LANE)
        xrow[pl.ds(at, LANE), :] = tok_ref[:, pl.ds(at, LANE)].T.astype(F32)
        crow[pl.ds(at, LANE), :] = cot_ref[:, pl.ds(at, LANE)].T.astype(F32)
        return carry

    lax.fori_loop(0, rows_all // LANE, unfold, 0, unroll=4)

    def norm_stats(x):
        centre = x - jnp.sum(x, -1, keepdims=True) * (1.0 / width)
        spread_sq = jnp.sum(centre * centre, -1, keepdims=True) * (1.0 / width)
        inv = lax.rsqrt(spread_sq + NORM_EPS)
        return centre * inv, inv

    def norm_back(grad, gain, hat, inv):
        scaled = grad * gain
        mean_one = jnp.sum(scaled, -1, keepdims=True) * (1.0 / width)
        mean_two = jnp.sum(scaled * hat, -1, keepdims=True) * (1.0 / width)
        return inv * (scaled - mean_one - hat * mean_two)

    def with_one(value):
        rows = value.shape[0]
        tail = jnp.where(iota((rows, pad - width), 1) == 0, 1.0, 0.0)
        return jnp.concatenate([value, tail], axis=1).astype(BF16)

    half = [
        (iota((1, LANE), 1) >> 5) == member for member in range(LANE // STRIDE)
    ]

    def pair_rows(block, pair):
        tile = block[:, (pair // 2) * LANE : (pair // 2 + 1) * LANE]
        at = 2 * (pair % 2)
        zero = jnp.zeros_like(tile)
        return jnp.concatenate(
            [jnp.where(half[at], tile, zero), jnp.where(half[at + 1], tile, zero)], axis=0
        )

    def pad_rows(value):
        rows = value.shape[0]
        return jnp.concatenate([value, jnp.zeros((LANE - rows, value.shape[1]), F32)], axis=0)

    def batch(step, n):
        at, kept, live = [], [], []
        for j in range(BATCH):
            s = order[step * BATCH + j]
            g = group_ref[s]
            limit = jnp.where(g == 0, L1, jnp.where(g == 1, L2, L3))
            at.append(pl.multiple_of(s * SLOT, 8))
            kept.append(jnp.where(iota((n, 1), 0) < limit, 1.0, 0.0))
            live.append(counts_ref[s])
        keep = jnp.concatenate(kept, axis=0)
        x = jnp.concatenate([xrow[pl.ds(a, n), :] for a in at], axis=0)
        c = jnp.concatenate([crow[pl.ds(a, n), :] for a in at], axis=0)

        hat1, inv1 = norm_stats(x)
        h1 = with_one(hat1 * g1 + b1)
        qkv = dot(h1, w_qkv[...])
        pairs = HEADS // 2
        for j in range(BATCH):
            rows = slice(j * n, (j + 1) * n)
            q = pad_rows(qkv[rows, :pad] * q_scale).astype(BF16)
            dead = iota((n, 1), 0) >= live[j]
            k32 = jnp.where(dead & spare_lane, MASK_VALUE, qkv[rows, pad : 2 * pad])
            v32 = qkv[rows, 2 * pad :]
            for pair in range(pairs):
                q_pairs[j, pair] = pair_rows(q, pair)
            k_rows[j, :n] = k32.astype(BF16)
            v_rows[j, :n] = v32.astype(BF16)
            k_cols[j] = pad_rows(k32).astype(BF16).T
            v_cols[j] = pad_rows(v32).astype(BF16).T
        every = [(j, pair) for j in range(BATCH) for pair in range(pairs)]

        def tile(pair):
            return slice((pair // 2) * LANE, (pair // 2 + 1) * LANE)

        def heads(pair):
            return slice(2 * STRIDE * pair, 2 * STRIDE * (pair + 1))

        for j, pair in every:
            scores[j, pair, :n] = dot(k_rows[j, :n, tile(pair)], q_pairs[j, pair], NT)
        for j, pair in every:
            score = scores[j, pair, :n]
            e = jnp.exp2(score - jnp.max(score, axis=0, keepdims=True))
            p = e * (1.0 / jnp.sum(e, axis=0, keepdims=True))
            probs[j, pair, :n] = p
            probs_low[j, pair, :n] = p.astype(BF16)
        for j, pair in every:
            o_t = dot(v_cols[j, heads(pair), :n], probs_low[j, pair, :n])
            cols[j, 2 * pair] = o_t[:STRIDE, :LANE]
            cols[j, 2 * pair + 1] = o_t[STRIDE:, LANE:]
        mixed = jnp.concatenate(
            [cols[j].reshape(pad, LANE).T[:n] for j in range(BATCH)], axis=0
        )
        o = jnp.where(iota((1, pad), 1) == SPARE, 1.0, mixed).astype(BF16)
        y1 = x + keep * dot(o, w_o[...])
        hat2, inv2 = norm_stats(y1)
        h2 = with_one(hat2 * g2 + b2)
        u = dot(h2, w_in[...])
        z, up = u[:, :hidden], u[:, hidden:]
        alpha, beta = 0.7978845608028654, 0.044715
        zz = z * z
        t = jnp.tanh(z * (alpha + (alpha * beta) * zz))
        half_t = 0.5 + 0.5 * t
        act = z * half_t
        slope = half_t + (z * (0.5 - 0.5 * t * t)) * (alpha + (3.0 * alpha * beta) * zz)
        hid = (act * up).astype(BF16)
        f = dot(hid, out_ref[...]) + bf
        out = y1 + keep * f
        df = keep * c
        df_low = df.astype(BF16)
        acc_small[0:8, :] += partial_sums(df)
        acc_out[...] += dot(hid, df_low, TN)
        dhid = dot(df_low, w_out_t[...])
        du = jnp.concatenate([dhid * up * slope, dhid * act], axis=1).astype(BF16)
        acc_in[...] += dot(h2, du, TN)
        dh2 = dot(du, in_ref[...])
        acc_small[8:16, :] += partial_sums(dh2 * hat2)
        acc_small[16:24, :] += partial_sums(dh2)
        dy1 = c + norm_back(dh2, g2, hat2, inv2)
        da = (keep * dy1).astype(BF16)
        acc_o[...] += dot(o, da, TN)
        do = dot(da, w_o_t[...])
        for j in range(BATCH):
            d_low = pad_rows(do[j * n : (j + 1) * n]).astype(BF16)
            for pair in range(pairs):
                d_pairs[j, pair] = pair_rows(d_low, pair)
        for j, pair in every:
            scores[j, pair, :n] = dot(v_rows[j, :n, tile(pair)], d_pairs[j, pair], NT)
        for j, pair in every:
            dp = scores[j, pair, :n]
            p = probs[j, pair, :n]
            ds_low[j, pair, :n] = (
                p * (dp - jnp.sum(dp * p, axis=0, keepdims=True))
            ).astype(BF16)
        for j, pair in every:
            dq_t = dot(k_cols[j, heads(pair), :n], ds_low[j, pair, :n])
            cols[j, 2 * pair] = dq_t[:STRIDE, :LANE]
            cols[j, 2 * pair + 1] = dq_t[STRIDE:, LANE:]
        parts = []
        for j in range(BATCH):
            dvs = [dot(probs_low[j, p, :n], d_pairs[j, p]) for p in range(pairs)]
            dks = [dot(ds_low[j, p, :n], q_pairs[j, p]) for p in range(pairs)]
            dq = cols[j].reshape(pad, LANE).T[:n] * scale
            parts.append(
                jnp.concatenate(
                    [
                        dq,
                        (dks[0] + dks[1]) * (1.0 / log2e),
                        (dks[2] + dks[3]) * (1.0 / log2e),
                        dvs[0] + dvs[1],
                        dvs[2] + dvs[3],
                    ],
                    axis=1,
                )
            )
        dqkv = jnp.concatenate(parts, axis=0).astype(BF16)
        acc_qkv[...] += dot(h1, dqkv, TN)
        dh1 = dot(dqkv, w_qkv_t[...])
        acc_small[24:32, :] += partial_sums(dh1 * hat1)
        acc_small[32:40, :] += partial_sums(dh1)
        dx = dy1 + norm_back(dh1, g1, hat1, inv1)
        for j in range(BATCH):
            xrow[pl.ds(at[j], n), :] = out[j * n : (j + 1) * n]
            crow[pl.ds(at[j], n), :] = dx[j * n : (j + 1) * n]

    def one_batch(step, carry):
        kind = group_ref[order[step * BATCH + BATCH - 1]]
        for member, n in enumerate((40, 72, 104)):
            pl.when(kind == member)(functools.partial(batch, step, n))
        return carry

    lax.fori_loop(0, samples // BATCH, one_batch, 0)

    def fold(tile, carry):
        at = pl.multiple_of(tile * LANE, LANE)
        y_ref[:, pl.ds(at, LANE)] = xrow[pl.ds(at, LANE), :].astype(BF16).T
        dx_ref[:, pl.ds(at, LANE)] = crow[pl.ds(at, LANE), :].T
        return carry

    lax.fori_loop(0, rows_all // LANE, fold, 0, unroll=4)

    def gather_heads(value):
        return lax.dot_general(
            value, spread.astype(F32), NT, precision=lax.Precision.HIGHEST,
            preferred_element_type=F32,
        )

    for member in range(3):
        g_attn_ref[member * width : (member + 1) * width, :] = gather_heads(
            acc_qkv[:width, member * pad : (member + 1) * pad]
        )
    g_attn_ref[3 * width :, :] = lax.dot_general(
        spread.astype(F32), acc_o[...], NN, precision=lax.Precision.HIGHEST,
        preferred_element_type=F32,
    )
    g_in_ref[...] = acc_in[:width, :].T
    g_out_ref[...] = acc_out[...]

    def small(member):
        return jnp.sum(acc_small[8 * member : 8 * member + 8, :], axis=0, keepdims=True)

    bias_rows = acc_qkv[width : width + 8, :]
    g_bq = gather_heads(bias_rows[:, :pad])[0:1]
    g_bv = gather_heads(bias_rows[:, 2 * pad :])[0:1]
    g_bo = acc_o[SPARE : SPARE + 8, :][0:1]
    flat = jnp.concatenate(
        [small(3), small(4), small(1), small(2), g_bq, g_bv, g_bo, small(0),
         acc_in[width : width + 8, :][0:1]],
        axis=1,
    )
    for row in range(16):
        g_vec_ref[row] = flat[:, row * LANE : (row + 1) * LANE]


def layer(group, counts, tokens_t, cotangent_t, attn, ffn_in, ffn_out, vec):
    width, rows = tokens_t.shape
    hidden = ffn_out.shape[0]
    pad = HEADS * STRIDE
    vmem = pl.BlockSpec(memory_space=pltpu.VMEM)
    smem = pl.BlockSpec(memory_space=pltpu.SMEM)
    return pl.pallas_call(
        layer_kernel,
        name="layer",
        out_shape=(
            jax.ShapeDtypeStruct((width, rows), BF16),
            jax.ShapeDtypeStruct((width, rows), F32),
            jax.ShapeDtypeStruct((4 * width, width), F32),
            jax.ShapeDtypeStruct((2 * hidden, width), F32),
            jax.ShapeDtypeStruct((hidden, width), F32),
            jax.ShapeDtypeStruct((16, 1, LANE), F32),
        ),
        in_specs=[smem, smem] + [vmem] * 6,
        out_specs=[vmem] * 6,
        scratch_shapes=[
            pltpu.SMEM((group.shape[0],), jnp.int32),
            pltpu.SMEM((4,), jnp.int32),
            pltpu.VMEM((rows, width), F32),
            pltpu.VMEM((rows, width), F32),
            pltpu.VMEM((pad, 3 * pad), BF16),
            pltpu.VMEM((3 * pad, width), BF16),
            pltpu.VMEM((pad, width), BF16),
            pltpu.VMEM((width, pad), BF16),
            pltpu.VMEM((pad, 2 * hidden), BF16),
            pltpu.VMEM((width, hidden), BF16),
            pltpu.VMEM((BATCH, HEADS // 2, SLOT, 2 * LANE), F32),
            pltpu.VMEM((BATCH, HEADS // 2, SLOT, 2 * LANE), BF16),
            pltpu.VMEM((BATCH, HEADS // 2, SLOT, 2 * LANE), F32),
            pltpu.VMEM((BATCH, HEADS // 2, SLOT, 2 * LANE), BF16),
            pltpu.VMEM((BATCH, HEADS // 2, 2 * LANE, LANE), BF16),
            pltpu.VMEM((BATCH, HEADS // 2, 2 * LANE, LANE), BF16),
            pltpu.VMEM((BATCH, SLOT, pad), BF16),
            pltpu.VMEM((BATCH, SLOT, pad), BF16),
            pltpu.VMEM((BATCH, pad, LANE), BF16),
            pltpu.VMEM((BATCH, pad, LANE), BF16),
            pltpu.VMEM((BATCH, HEADS, STRIDE, LANE), F32),
            pltpu.VMEM((pad, 3 * pad), F32),
            pltpu.VMEM((pad, width), F32),
            pltpu.VMEM((pad, 2 * hidden), F32),
            pltpu.VMEM((hidden, width), F32),
            pltpu.VMEM((40, width), F32),
        ],
        compiler_params=pltpu.CompilerParams(vmem_limit_bytes=60 * 2**20),
    )(group, counts, tokens_t, cotangent_t, attn, ffn_in, ffn_out, vec)


def greet(size, me, core):
    barrier = pltpu.get_barrier_semaphore()

    def signal(k, carry):
        pl.semaphore_signal(
            barrier, inc=1, device_id=(lax.rem(me + k, size), core), device_id_type=MESH
        )
        return carry

    lax.fori_loop(1, size, signal, 0)
    pl.semaphore_signal(barrier, inc=1, device_id=(me, 1 - core), device_id_type=MESH)
    pl.semaphore_wait(barrier, size)


def over(low, high, body):
    def step(k, carry):
        body(k)
        return carry

    lax.fori_loop(low, high, step, 0)


def gather_kernel(
    attn_ref, in_ref, out_ref, vec_ref,
    attn_all, in_all, out_all, vec_all,
    send_sem, recv_sem, pass_sem, got_sem,
):
    size = attn_all.shape[0]
    me, core = lax.axis_index("wide"), lax.axis_index("narrow")
    attn_all[me] = attn_ref[...].astype(BF16)
    in_all[me] = in_ref[...].astype(BF16)
    out_all[me] = out_ref[...].astype(BF16)
    vec_all[me] = vec_ref[...].astype(BF16).astype(F32)
    greet(size, me, core)

    def role(mine, theirs):
        def to_peer(ref, r, owner, k):
            return pltpu.make_async_remote_copy(
                src_ref=ref.at[owner],
                dst_ref=ref.at[owner],
                send_sem=send_sem.at[r, k],
                recv_sem=recv_sem.at[r, owner],
                device_id=(lax.rem(me + k, size), core),
                device_id_type=MESH,
            )

        def to_twin(ref, r, owner):
            return pltpu.make_async_remote_copy(
                src_ref=ref.at[owner],
                dst_ref=ref.at[owner],
                send_sem=pass_sem.at[r, owner],
                recv_sem=got_sem.at[r, owner],
                device_id=(me, 1 - core),
                device_id_type=MESH,
            )

        def start(k):
            for r, ref in enumerate(mine):
                to_peer(ref, r, me, k).start()

        def forward(k):
            owner = lax.rem(me + size - k, size)
            for r, ref in enumerate(mine):
                to_peer(ref, r, owner, k).wait_recv()
                to_twin(ref, r, owner).start()

        def finish(k):
            owner = lax.rem(me + size - k, size)
            for r, ref in enumerate(mine):
                to_peer(ref, r, me, k).wait_send()
                to_twin(ref, r, owner).wait_send()
            for r, ref in enumerate(theirs):
                to_twin(ref, r, owner).wait_recv()

        over(1, size, start)
        over(1, size, forward)
        over(1, size, finish)

    pl.when(core == 0)(lambda: role((attn_all, vec_all), (in_all, out_all)))
    pl.when(core != 0)(lambda: role((in_all, out_all), (attn_all, vec_all)))


def gather(size, attn, ffn_in, ffn_out, vec):
    vmem = pl.BlockSpec(memory_space=pltpu.VMEM)
    return pl.pallas_call(
        gather_kernel,
        name="gather",
        out_shape=tuple(
            jax.ShapeDtypeStruct((size, *value.shape), BF16)
            for value in (attn, ffn_in, ffn_out)
        )
        + (jax.ShapeDtypeStruct((size, *vec.shape), F32),),
        in_specs=[vmem] * 4,
        out_specs=[vmem] * 4,
        scratch_shapes=[pltpu.SemaphoreType.DMA((2, size))] * 4,
        compiler_params=pltpu.CompilerParams(
            collective_id=0, has_side_effects=True, vmem_limit_bytes=32 * 2**20
        ),
    )(attn, ffn_in, ffn_out, vec)


def reduce_kernel(
    g_attn, g_in, g_out, g_vec,
    s_attn, s_in, s_out, s_vec,
    stage_attn, stage_in, stage_out, stage_vec,
    twin_attn, twin_in, twin_out, twin_vec,
    both_attn, both_in, both_out, both_vec,
    peer_attn, peer_in, peer_out, peer_vec,
    pass_sem, got_sem, send_sem, recv_sem, last_send, last_recv,
):
    size = g_attn.shape[0]
    me, core = lax.axis_index("wide"), lax.axis_index("narrow")
    greet(size, me, core)

    def role(mine, theirs):
        def to_twin(pack, r, owner):
            return pltpu.make_async_remote_copy(
                src_ref=pack[2].at[owner],
                dst_ref=pack[3].at[owner],
                send_sem=pass_sem.at[r, owner],
                recv_sem=got_sem.at[r, owner],
                device_id=(me, 1 - core),
                device_id_type=MESH,
            )

        def to_peer(pack, r, k, source):
            return pltpu.make_async_remote_copy(
                src_ref=pack[4].at[lax.rem(me + k, size)],
                dst_ref=pack[5].at[source],
                send_sem=send_sem.at[r, k],
                recv_sem=recv_sem.at[r, source],
                device_id=(lax.rem(me + k, size), core),
                device_id_type=MESH,
            )

        def result(pack, r):
            return pltpu.make_async_remote_copy(
                src_ref=pack[1],
                dst_ref=pack[1],
                send_sem=last_send.at[r],
                recv_sem=last_recv.at[r],
                device_id=(me, 1 - core),
                device_id_type=MESH,
            )

        def give(k):
            owner = lax.rem(me + k, size)
            for r, pack in enumerate(theirs):
                pack[2][owner] = pack[0][owner].astype(pack[2].dtype)
                to_twin(pack, r, owner).start()

        def send(k):
            owner = lax.rem(me + k, size)
            for r, pack in enumerate(mine):
                to_twin(pack, r, owner).wait_recv()
                total = pack[0][owner] + pack[3][owner].astype(F32)
                pack[4][owner] = total.astype(pack[4].dtype)
                to_peer(pack, r, k, me).start()

        def take(k):
            source = lax.rem(me + size - k, size)
            for r, pack in enumerate(mine):
                to_peer(pack, r, k, source).wait_recv()
                pack[1][...] += pack[5][source].astype(F32)

        def finish(k):
            owner = lax.rem(me + k, size)
            for r, pack in enumerate(theirs):
                to_twin(pack, r, owner).wait_send()

        def finish_peer(k):
            for r, pack in enumerate(mine):
                to_peer(pack, r, k, me).wait_send()

        over(1, size + 1, give)
        over(1, size, send)
        for r, pack in enumerate(mine):
            to_twin(pack, r, me).wait_recv()
            pack[1][...] = pack[0][me] + pack[3][me].astype(F32)
        over(1, size, take)
        for r, pack in enumerate(mine):
            result(pack, r).start()
        over(1, size + 1, finish)
        over(1, size, finish_peer)
        for r, pack in enumerate(mine):
            result(pack, r).wait_send()
        for r, pack in enumerate(theirs):
            result(pack, r).wait_recv()

    attn = (g_attn, s_attn, stage_attn, twin_attn, both_attn, peer_attn)
    into = (g_in, s_in, stage_in, twin_in, both_in, peer_in)
    outof = (g_out, s_out, stage_out, twin_out, both_out, peer_out)
    vecs = (g_vec, s_vec, stage_vec, twin_vec, both_vec, peer_vec)
    pl.when(core == 0)(lambda: role((attn, vecs), (into, outof)))
    pl.when(core != 0)(lambda: role((into, outof), (attn, vecs)))


def reduce_scatter(g_attn, g_in, g_out, g_vec):
    grads = (g_attn, g_in, g_out, g_vec)
    size = g_attn.shape[0]
    vmem = pl.BlockSpec(memory_space=pltpu.VMEM)
    buffers = [
        pltpu.VMEM(value.shape, F32 if value is g_vec else BF16) for value in grads
    ]
    return pl.pallas_call(
        reduce_kernel,
        name="reduce",
        out_shape=tuple(jax.ShapeDtypeStruct(value.shape[1:], F32) for value in grads),
        in_specs=[vmem] * 4,
        out_specs=[vmem] * 4,
        scratch_shapes=buffers * 4
        + [pltpu.SemaphoreType.DMA((2, size))] * 4
        + [pltpu.SemaphoreType.DMA((2,))] * 2,
        compiler_params=pltpu.CompilerParams(
            collective_id=1, has_side_effects=True, vmem_limit_bytes=48 * 2**20
        ),
    )(*grads)


def adamw_kernel(*refs):
    for member in range(4):
        master, first, second, grad = (refs[4 * kind + member][...] for kind in range(4))
        results = adamw_update(master, grad, first, second)
        for kind in range(3):
            refs[16 + 3 * member + kind][...] = results[kind]


def adamw(masters, firsts, seconds, grads):
    vmem = pl.BlockSpec(memory_space=pltpu.VMEM)
    return pl.pallas_call(
        adamw_kernel,
        name="adamw",
        out_shape=tuple(
            jax.ShapeDtypeStruct(value.shape, F32) for value in masters for kind in range(3)
        ),
        in_specs=[vmem] * 16,
        out_specs=[vmem] * 12,
    )(*masters, *firsts, *seconds, *grads)


def local(
    tokens,
    cotangent,
    group,
    counts,
    attn_w,
    ffn_in,
    ffn_out,
    vectors,
    attn_m,
    attn_v,
    in_m,
    in_v,
    out_m,
    out_v,
    vec_m,
    vec_v,
):
    size = lax.axis_size("wide")
    width = tokens.shape[1]
    masters = (attn_w, ffn_in, ffn_out, vectors[None])
    attn, into, outof, vec = gather(size, *masters)
    out_t, grad_t, *grads = layer(
        group,
        counts,
        tokens.T,
        cotangent.T,
        attn.reshape(-1, width),
        into.reshape(-1, width),
        outof.reshape(-1, width),
        vec.reshape(-1, 1, LANE),
    )
    sums = reduce_scatter(
        *[g.reshape(size, -1, width) for g in grads[:3]], grads[3].reshape(size, 1, -1)
    )
    results = adamw(
        masters, (attn_m, in_m, out_m, vec_m[None]), (attn_v, in_v, out_v, vec_v[None]), sums
    )
    return (out_t.T, grad_t.T, *results[:9], *[value[0] for value in results[9:]])


def solution(mesh):
    rows = P(("wide", "narrow"), None)
    samples = P(("wide", "narrow"))
    weight = P("wide", None)
    vector = P("wide")
    return jax.shard_map(
        local,
        mesh=mesh,
        in_specs=(rows, rows, samples, samples, weight, weight, weight, vector)
        + (weight,) * 6
        + (vector,) * 2,
        out_specs=(rows, rows) + (weight,) * 9 + (vector,) * 3,
        check_vma=False,
    )
```

```python
import functools
import math

import jax
import jax.numpy as jnp
from jax import lax
from jax.experimental import pallas as pl
from jax.experimental.pallas import tpu as pltpu
from jax.sharding import PartitionSpec as P

HEADS = 8
SLOT = 104
L1 = 40
L2 = 68
L3 = 100
STEP = 10

NORM_EPS = 1e-05
BETA_ONE = 0.9
BETA_TWO = 0.999
ADAM_EPS = 1e-08
LEARN_RATE = 0.1
WEIGHT_DECAY = 0.01
MASK_VALUE = -1e30

F32 = jnp.float32
BF16 = jnp.bfloat16
LANE = 128
MESH = pl.DeviceIdType.MESH
STRIDE = 32
NN = (((1,), (0,)), ((), ()))
NT = (((1,), (1,)), ((), ()))
TN = (((0,), (0,)), ((), ()))
BATCH = 4
SPARE = 24


def adamw_update(master, gradient, moment, square):
    moment_new = BETA_ONE * moment + (1.0 - BETA_ONE) * gradient
    square_new = BETA_TWO * square + (1.0 - BETA_TWO) * gradient * gradient
    moment_hat = moment_new / (1.0 - BETA_ONE**STEP)
    square_hat = square_new / (1.0 - BETA_TWO**STEP)
    master_new = master - LEARN_RATE * (
        moment_hat / (jnp.sqrt(square_hat) + ADAM_EPS) + WEIGHT_DECAY * master
    )
    return (master_new, moment_new, square_new)


def dot(a, b, dims=NN):
    return lax.dot_general(a, b, dims, preferred_element_type=F32)


def iota(shape, dim):
    return lax.broadcasted_iota(jnp.int32, shape, dim)


def partial_sums(value):
    rows, cols = value.shape
    return jnp.sum(value.reshape(rows // 8, 8, cols), axis=0)


def piece(vec, member, width):
    start = member * width
    parts, at = [], start
    while at < start + width:
        row, lane = divmod(at, LANE)
        take = min(LANE - lane, start + width - at)
        parts.append(vec[row : row + 1, lane : lane + take])
        at += take
    return jnp.concatenate(parts, axis=1)


def layer_kernel(
    group_ref,
    counts_ref,
    order,
    x_hbm,
    c_hbm,
    attn_ref,
    in_ref,
    out_ref,
    vec_ref,
    y_ref,
    dx_ref,
    g_attn_ref,
    g_in_ref,
    g_out_ref,
    g_vec_ref,
    xrow,
    crow,
    y_cols,
    dx_cols,
    row_sem,
    col_sem,
    w_qkv,
    w_qkv_t,
    w_o,
    w_o_t,
    w_in,
    w_in_t,
    w_out,
    w_out_t,
    probs,
    scores,
    k_rows,
    v_rows,
    v_cols,
    cols,
    acc_qkv,
    acc_o,
    acc_in,
    acc_out,
    acc_small,
    *carried,
):
    width = attn_ref.shape[1]
    hidden = out_ref.shape[0]
    samples = group_ref.shape[0]
    rows_all = x_hbm.shape[0]
    head = width // HEADS
    pad = HEADS * STRIDE
    scale = 1.0 / math.sqrt(head)
    log2e = math.log2(math.e)
    q_scale = scale * log2e

    steps = samples // (2 * BATCH)

    def fetch(step):
        for j in range(2 * BATCH):
            rows = pl.ds(pl.multiple_of(order[step * 2 * BATCH + j] * SLOT, 8), SLOT)
            for ref, held in ((x_hbm, xrow), (c_hbm, crow)):
                pltpu.make_async_copy(ref.at[rows], held.at[rows], row_sem.at[step]).start()

    def fetched(step):
        rows = pl.ds(0, 2 * BATCH * SLOT)
        for ref, held in ((x_hbm, xrow), (c_hbm, crow)):
            pltpu.make_async_copy(ref.at[rows], held.at[rows], row_sem.at[step]).wait()

    fetch(0)
    fetch(1)

    spread_row = iota((width, pad), 0)
    spread_col = iota((width, pad), 1)
    within = spread_col & (STRIDE - 1)
    spread = jnp.where(
        (within < head) & (spread_row == (spread_col >> 5) * head + within), 1.0, 0.0
    ).astype(BF16)
    vec = jnp.concatenate([vec_ref[row] for row in range(vec_ref.shape[0])], axis=0)
    bi = jnp.concatenate([vec[row : row + 1] for row in range(12, 16)], axis=1)

    def widen(value, fill=0.0):
        rows = value.shape[0]
        tail = jnp.where(iota((rows, pad - width), 1) == 0, fill, 0.0)
        return jnp.concatenate([value, tail], axis=1)

    def lengthen(value, row=None):
        cols = value.shape[1]
        if row is None:
            row = jnp.zeros((1, cols), F32)
        tail = jnp.concatenate([row, jnp.zeros((pad - width - 1, cols), F32)], axis=0)
        return jnp.concatenate([value, tail], axis=0)

    g1, b1, g2, b2, bq, bv, bo, bf = (piece(vec, member, width) for member in range(8))
    g1, b1, g2, b2 = widen(g1), widen(b1, 1.0), widen(g2), widen(b2, 1.0)
    bf = widen(bf)
    spare_lane = (iota((1, pad), 1) & (STRIDE - 1)) == SPARE
    for member in range(3):
        spread_w = dot(attn_ref[member * width : (member + 1) * width, :], spread)
        if member == 0:
            bias = dot(bq.astype(BF16), spread) + jnp.where(spare_lane, 1.0, 0.0)
        elif member == 1:
            bias = None
        else:
            bias = dot(bv.astype(BF16), spread)
        w_qkv[:, member * pad : (member + 1) * pad] = lengthen(spread_w, bias).astype(BF16)
        w_qkv_t[member * pad : (member + 1) * pad, :] = widen(spread_w.T).astype(BF16)
    spread_o = widen(dot(spread, attn_ref[3 * width :, :], TN))
    w_o_t[...] = spread_o.T.astype(BF16)
    w_o[...] = jnp.where(iota((pad, pad), 0) == SPARE, widen(bo), spread_o).astype(BF16)
    in_wide = widen(in_ref[...].astype(F32))
    out_wide = widen(out_ref[...].astype(F32))
    w_in_t[...] = in_wide.astype(BF16)
    w_in[...] = lengthen(in_wide[:, :width].T, bi).astype(BF16)
    w_out[...] = out_wide.astype(BF16)
    w_out_t[...] = out_wide.T.astype(BF16)

    for ref in (acc_qkv, acc_o, acc_in, acc_out, acc_small, *carried):
        ref[...] = jnp.zeros_like(ref)
    names = ("q_rows", "d_rows", "probs_low", "ds_low", "k_cols", "dq_cols", "hat", "inv")
    names += ("h2", "du", "hid", "df", "o", "da")
    kept = [
        dict(zip(names, carried[side * len(names) : (side + 1) * len(names)]))
        for side in range(2)
    ]

    features = iota((1, pad), 1) < width

    def norm_stats(x):
        mean = jnp.sum(x, -1, keepdims=True) * (1.0 / width)
        centre = jnp.where(features, x - mean, 0.0)
        spread_sq = jnp.sum(centre * centre, -1, keepdims=True) * (1.0 / width)
        inv = lax.rsqrt(spread_sq + NORM_EPS)
        return centre * inv, inv

    def norm_back(scaled, crossed, hat, inv):
        mean_one = jnp.sum(scaled, -1, keepdims=True) * (1.0 / width)
        mean_two = jnp.sum(crossed, -1, keepdims=True) * (1.0 / width)
        return inv * (scaled - mean_one - hat * mean_two)

    half = [
        (iota((1, LANE), 1) >> 5) == member for member in range(LANE // STRIDE)
    ]

    def group_rows(block, group, per):
        first = group * per
        lanes = block[:, first // 4 * LANE : (first // 4 + 1) * LANE]
        zero = jnp.zeros_like(lanes)
        return jnp.concatenate(
            [jnp.where(half[(first + i) % 4], lanes, zero) for i in range(per)], axis=0
        )

    def pad_rows(value, size=LANE):
        rows = value.shape[0]
        return jnp.concatenate([value, jnp.zeros((size - rows, value.shape[1]), F32)], axis=0)

    lead = width + 8

    def grouping(n):
        per = 4 if n <= 64 else 2
        groups = HEADS // per
        return per, groups, [(j, group) for j in range(BATCH) for group in range(groups)]

    def tile(group, per):
        first = group * per // 4
        return slice(first * LANE, (first + 1) * LANE)

    def heads(group, per):
        return slice(per * STRIDE * group, per * STRIDE * (group + 1))

    def keep_own(ref, j, group, per, product):
        size = 2 * LANE // per
        for i in range(per):
            block = product[i * STRIDE : (i + 1) * STRIDE]
            at = i * size // LANE
            block = block[:, at * LANE : (at + 1) * LANE]
            if i * size % LANE:
                block = pltpu.roll(block, LANE - i * size % LANE, 1)
            ref[j, per * group + i] = block

    def bases(first):
        return [pl.multiple_of(order[first + j] * SLOT, 8) for j in range(BATCH)]

    def stack(values):
        return jnp.concatenate(values, axis=0)

    def front(box, first, n):
        cuts = {40: (0, 40), 72: (0, 40, 72), 104: (0, 32, 64, 104)}[n]
        chunks = [
            (j, lo, hi) for j in range(BATCH) for lo, hi in zip(cuts[:-1], cuts[1:])
        ]
        at = bases(first)
        limits, live = [], []
        for j in range(BATCH):
            s = order[first + j]
            g = group_ref[s]
            limits.append(jnp.where(g == 0, L1, jnp.where(g == 1, L2, L3)))
            live.append(counts_ref[s])

        per, groups, every = grouping(n)

        def keep(j, lo, hi):
            return jnp.where(iota((hi - lo, 1), 0) + lo < limits[j], 1.0, 0.0)

        def rows_of(ref, j, lo, hi):
            return ref[pl.ds(at[j] + lo, hi - lo), :]

        def flat(j, lo, hi):
            return slice(j * n + lo, j * n + hi)

        h1 = []
        for j, lo, hi in chunks:
            hat1, inv1 = norm_stats(rows_of(xrow, j, lo, hi))
            box["hat"][j, lo:hi] = hat1
            box["inv"][j, lo:hi] = inv1
            h1.append(hat1 * g1 + b1)
        yield
        qkv = dot(stack(h1).astype(BF16), w_qkv[...])
        for j in range(BATCH):
            rows = slice(j * n, (j + 1) * n)
            q = pad_rows(qkv[rows, :pad] * q_scale, 2 * LANE // per).astype(BF16)
            dead = iota((n, 1), 0) >= live[j]
            k32 = jnp.where(dead & spare_lane, MASK_VALUE, qkv[rows, pad : 2 * pad])
            v32 = qkv[rows, 2 * pad :]
            for group in range(groups):
                box["q_rows"][j, group] = group_rows(q, group, per)
            k_rows[j, :n] = k32.astype(BF16)
            v_rows[j, :n] = v32.astype(BF16)
            box["k_cols"][j] = pad_rows(k32).astype(BF16).T
            v_cols[j] = pad_rows(v32).astype(BF16).T
            yield
        for j, group in every:
            scores[j, group, :n] = dot(
                k_rows[j, :n, tile(group, per)], box["q_rows"][j, group], NT
            )
        yield
        for j, group in every:
            score = scores[j, group, :n]
            e = jnp.exp2(score - jnp.max(score, axis=0, keepdims=True))
            p = e * (1.0 / jnp.sum(e, axis=0, keepdims=True))
            probs[j, group, :n] = p
            box["probs_low"][j, group, :n] = p.astype(BF16)
            if group == groups - 1:
                yield
        for j, group in every:
            o_t = dot(v_cols[j, heads(group, per), :n], box["probs_low"][j, group, :n])
            keep_own(cols, j, group, per, o_t)
        yield
        mixed = stack([cols[j].reshape(pad, LANE).T[:n] for j in range(BATCH)])
        o = jnp.where(iota((1, pad), 1) == SPARE, 1.0, mixed).astype(BF16)
        box["o"][: BATCH * n] = o
        yield
        a = dot(o, w_o[...])
        y1, hat2, inv2, h2 = [], [], [], []
        for c in chunks:
            y = rows_of(xrow, *c) + keep(*c) * a[flat(*c)]
            hat, inv = norm_stats(y)
            y1.append(y)
            hat2.append(hat)
            inv2.append(inv)
            h2.append(hat * g2 + b2)
        h2 = stack(h2).astype(BF16)
        box["h2"][: BATCH * n] = h2
        yield
        u = dot(h2, w_in[...])
        df = stack([keep(*c) * rows_of(crow, *c) for c in chunks])
        df_low = df.astype(BF16)
        box["df"][: BATCH * n] = df_low
        acc_small[0:8, :] += partial_sums(df)
        dhid = dot(df_low, w_out_t[...])
        yield
        hid, du = [], []
        alpha, beta = 0.7978845608028654, 0.044715
        for c in chunks:
            z, up = u[flat(*c), :hidden], u[flat(*c), hidden:]
            dh = dhid[flat(*c)]
            inner = alpha + (alpha * beta) * (z * z)
            gate = 0.5 + 0.5 * jnp.tanh(z * inner)
            act = z * gate
            slope = gate + (act * (1.0 - gate)) * (6.0 * inner - 4.0 * alpha)
            hid.append(act * up)
            du.append(jnp.concatenate([dh * up * slope, dh * act], axis=1))
            if c[1] == 0:
                yield
        hid = stack(hid).astype(BF16)
        box["hid"][: BATCH * n] = hid
        du = stack(du).astype(BF16)
        box["du"][: BATCH * n] = du
        yield
        f = dot(hid, w_out[...])
        dh2 = dot(du, w_in_t[...])
        yield
        da = []
        gain = jnp.zeros((8, pad), F32)
        for i, c in enumerate(chunks):
            j, lo, hi = c
            xrow[pl.ds(at[j] + lo, hi - lo), :] = y1[i] + keep(*c) * (f[flat(*c)] + bf)
            grad = dh2[flat(*c)]
            crossed = grad * hat2[i]
            gain += partial_sums(crossed)
            dy1 = rows_of(crow, *c) + norm_back(grad * g2, crossed * g2, hat2[i], inv2[i])
            crow[pl.ds(at[j] + lo, hi - lo), :] = dy1
            da.append(keep(*c) * dy1)
        acc_small[8:16, :] += gain
        da = stack(da).astype(BF16)
        box["da"][: BATCH * n] = da
        yield
        do = dot(da, w_o_t[...])
        for j in range(BATCH):
            d_low = pad_rows(do[j * n : (j + 1) * n], 2 * LANE // per).astype(BF16)
            for group in range(groups):
                box["d_rows"][j, group] = group_rows(d_low, group, per)
        yield
        for j, group in every:
            scores[j, group, :n] = dot(
                v_rows[j, :n, tile(group, per)], box["d_rows"][j, group], NT
            )
        yield
        for j, group in every:
            dp = scores[j, group, :n]
            p = probs[j, group, :n]
            box["ds_low"][j, group, :n] = (
                p * (dp - jnp.sum(dp * p, axis=0, keepdims=True))
            ).astype(BF16)
            if group == groups - 1:
                yield

    def back(box, first, n, layout):
        per, groups, every = grouping(layout)
        rows = slice(0, BATCH * n)
        at = bases(first)
        for j, group in every:
            dq_t = dot(box["k_cols"][j, heads(group, per), :n], box["ds_low"][j, group, :n])
            keep_own(box["dq_cols"], j, group, per, dq_t)
            if group == groups - 1:
                yield
        parts = []
        for j in range(BATCH):
            dvs = [
                dot(box["probs_low"][j, group, :n], box["d_rows"][j, group])
                for group in range(groups)
            ]
            yield
            dks = [
                dot(box["ds_low"][j, group, :n], box["q_rows"][j, group])
                for group in range(groups)
            ]
            if per == 2:
                dvs = [dvs[0] + dvs[1], dvs[2] + dvs[3]]
                dks = [dks[0] + dks[1], dks[2] + dks[3]]
            dq = box["dq_cols"][j].reshape(pad, LANE).T[:n] * scale
            dks = [value * (1.0 / log2e) for value in dks]
            parts.append(jnp.concatenate([dq, *dks, *dvs], axis=1))
            yield
        dqkv = stack(parts).astype(BF16)
        dh1 = dot(dqkv, w_qkv_t[...])
        yield
        acc_out[...] += dot(box["df"][rows, :width], box["hid"][rows], TN)
        yield
        acc_o[...] += dot(box["da"][rows, :width], box["o"][rows], TN)
        yield
        acc_in[...] += dot(box["h2"][rows, :lead], box["du"][rows], TN)
        yield
        h1 = []
        gain = jnp.zeros((8, pad), F32)
        for j in range(BATCH):
            hat = box["hat"][j, :n]
            grad = dh1[j * n : (j + 1) * n]
            crossed = grad * hat
            gain += partial_sums(crossed)
            crow[pl.ds(at[j], n), :] += norm_back(
                grad * g1, crossed * g1, hat, box["inv"][j, :n]
            )
            h1.append(hat * g1 + b1)
            if j % 2:
                yield
        acc_small[16:24, :] += gain
        h1 = stack(h1).astype(BF16)
        acc_qkv[...] += dot(h1[:, :lead], dqkv, TN)

    def together(first, second):
        going = [first, second]
        while going:
            for part in list(going):
                if next(part, going) is going:
                    going.remove(part)

    def double(step, n):
        even = step * 2 * BATCH
        before = jnp.maximum(even - BATCH, 0)
        together(back(kept[1], before, n, n), front(kept[0], even, n))
        together(back(kept[0], even, n, n), front(kept[1], even + BATCH, n))

    lengths = (40, 72, 104)
    def kind_of(step):
        return group_ref[order[(step + 1) * 2 * BATCH - 1]]

    def finish_short(step):
        together(back(kept[1], step * 2 * BATCH - BATCH, 40, 40), iter(()))
        for name in ("ds_low", "d_rows", "du", "df", "da"):
            kept[1][name][...] = jnp.zeros_like(kept[1][name])

    def one_step(step, carry):
        kind = kind_of(jnp.minimum(step, steps - 1))
        last = kind_of(jnp.maximum(step - 1, 0))
        pl.when((step > 0) & (last == 0) & ((step == steps) | (kind != 0)))(
            functools.partial(finish_short, step)
        )
        pl.when(step < steps)(lambda: fetched(step))
        pl.when(step + 2 < steps)(lambda: fetch(step + 2))
        for member, n in enumerate(lengths):
            pl.when((step < steps) & (kind == member))(functools.partial(double, step, n))
        return carry

    lax.fori_loop(0, steps + 1, one_step, 0)
    together(back(kept[1], samples - BATCH, SLOT, SLOT), iter(()))

    cut = 4 * LANE

    def col_copies(part):
        lanes = pl.ds(pl.multiple_of(part * cut, cut), cut)
        return [
            pltpu.make_async_copy(held.at[:, lanes], ref.at[:, lanes], col_sem.at[i, part])
            for i, (held, ref) in enumerate(((y_cols, y_ref), (dx_cols, dx_ref)))
        ]

    def fold(part, carry):
        for member in range(4):
            at = pl.multiple_of(part * cut + member * LANE, LANE)
            y_cols[:, pl.ds(at, LANE)] = xrow[pl.ds(at, LANE), :width].astype(BF16).T
            dx_cols[:, pl.ds(at, LANE)] = crow[pl.ds(at, LANE), :width].T
        for copy in col_copies(part):
            copy.start()
        return carry

    lax.fori_loop(0, rows_all // cut, fold, 0)

    def gather_heads(value):
        return lax.dot_general(
            value, spread.astype(F32), NT, precision=lax.Precision.HIGHEST,
            preferred_element_type=F32,
        )

    for member in range(3):
        g_attn_ref[member * width : (member + 1) * width, :] = gather_heads(
            acc_qkv[:width, member * pad : (member + 1) * pad]
        )
    g_attn_ref[3 * width :, :] = lax.dot_general(
        spread.astype(F32), acc_o[...], NT, precision=lax.Precision.HIGHEST,
        preferred_element_type=F32,
    )
    g_in_ref[...] = acc_in[:width, :].T
    g_out_ref[...] = acc_out[...].T

    def small(member):
        block = acc_small[8 * member : 8 * member + 8, :width]
        return jnp.sum(block, axis=0, keepdims=True)

    def exact(a, b):
        return lax.dot_general(
            a, b.astype(F32), NN, precision=lax.Precision.HIGHEST, preferred_element_type=F32
        )[0:1]

    qkv_sums = acc_qkv[width : width + 8, :]
    in_sums = acc_in[width : width + 8, :]
    g_b1 = exact(qkv_sums, w_qkv_t[...])[:, :width]
    g_b2 = exact(in_sums, w_in_t[...])[:, :width]
    g_bq = gather_heads(qkv_sums[:, :pad])[0:1]
    g_bv = gather_heads(qkv_sums[:, 2 * pad :])[0:1]
    g_bo = acc_o[...].T[SPARE : SPARE + 1]
    flat = jnp.concatenate(
        [small(2), g_b1, small(1), g_b2, g_bq, g_bv, g_bo, small(0), in_sums[0:1]], axis=1
    )
    for row in range(16):
        g_vec_ref[row] = flat[:, row * LANE : (row + 1) * LANE]

    def folded(part, carry):
        for copy in col_copies(part):
            copy.wait()
        return carry

    lax.fori_loop(0, rows_all // cut, folded, 0)


def layer(group, counts, order, x_rows, c_rows, attn, ffn_in, ffn_out, vec):
    rows, width = x_rows.shape[0], attn.shape[1]
    hidden = ffn_out.shape[0]
    pad = HEADS * STRIDE
    vmem = pl.BlockSpec(memory_space=pltpu.VMEM)
    smem = pl.BlockSpec(memory_space=pltpu.SMEM)
    whole = pl.BlockSpec(memory_space=pl.ANY)
    return pl.pallas_call(
        layer_kernel,
        name="layer",
        out_shape=(
            jax.ShapeDtypeStruct((width, rows), BF16),
            jax.ShapeDtypeStruct((width, rows), F32),
            jax.ShapeDtypeStruct((4 * width, width), F32),
            jax.ShapeDtypeStruct((2 * hidden, width), F32),
            jax.ShapeDtypeStruct((hidden, width), F32),
            jax.ShapeDtypeStruct((16, 1, LANE), F32),
        ),
        in_specs=[smem] * 3 + [whole] * 2 + [vmem] * 4,
        out_specs=[whole] * 2 + [vmem] * 4,
        scratch_shapes=[
            pltpu.VMEM((rows, pad), F32),
            pltpu.VMEM((rows, pad), F32),
            pltpu.VMEM((width, rows), BF16),
            pltpu.VMEM((width, rows), F32),
            pltpu.SemaphoreType.DMA((group.shape[0] // (2 * BATCH),)),
            pltpu.SemaphoreType.DMA((2, rows // (4 * LANE))),
            pltpu.VMEM((pad, 3 * pad), BF16),
            pltpu.VMEM((3 * pad, pad), BF16),
            pltpu.VMEM((pad, pad), BF16),
            pltpu.VMEM((pad, pad), BF16),
            pltpu.VMEM((pad, 2 * hidden), BF16),
            pltpu.VMEM((2 * hidden, pad), BF16),
            pltpu.VMEM((hidden, pad), BF16),
            pltpu.VMEM((pad, hidden), BF16),
            pltpu.VMEM((BATCH, HEADS // 2, SLOT, 2 * LANE), F32),
            pltpu.VMEM((BATCH, HEADS // 2, SLOT, 2 * LANE), F32),
            pltpu.VMEM((BATCH, SLOT, pad), BF16),
            pltpu.VMEM((BATCH, SLOT, pad), BF16),
            pltpu.VMEM((BATCH, pad, LANE), BF16),
            pltpu.VMEM((BATCH, HEADS, STRIDE, LANE), F32),
            pltpu.VMEM((width + 8, 3 * pad), F32),
            pltpu.VMEM((width, pad), F32),
            pltpu.VMEM((width + 8, 2 * hidden), F32),
            pltpu.VMEM((width, hidden), F32),
            pltpu.VMEM((24, pad), F32),
        ]
        + [
            pltpu.VMEM((BATCH, HEADS // 2, 2 * LANE, LANE), BF16),
            pltpu.VMEM((BATCH, HEADS // 2, 2 * LANE, LANE), BF16),
            pltpu.VMEM((BATCH, HEADS // 2, SLOT, 2 * LANE), BF16),
            pltpu.VMEM((BATCH, HEADS // 2, SLOT, 2 * LANE), BF16),
            pltpu.VMEM((BATCH, pad, LANE), BF16),
            pltpu.VMEM((BATCH, HEADS, STRIDE, LANE), F32),
            pltpu.VMEM((BATCH, SLOT, pad), F32),
            pltpu.VMEM((BATCH, SLOT, 1), F32),
            pltpu.VMEM((BATCH * SLOT, pad), BF16),
            pltpu.VMEM((BATCH * SLOT, 2 * hidden), BF16),
            pltpu.VMEM((BATCH * SLOT, hidden), BF16),
            pltpu.VMEM((BATCH * SLOT, pad), BF16),
            pltpu.VMEM((BATCH * SLOT, pad), BF16),
            pltpu.VMEM((BATCH * SLOT, pad), BF16),
        ]
        * 2,
        compiler_params=pltpu.CompilerParams(vmem_limit_bytes=60 * 2**20),
    )(group, counts, order, x_rows, c_rows, attn, ffn_in, ffn_out, vec)


def signal_all(size, me, core):
    barrier = pltpu.get_barrier_semaphore()

    def signal(k):
        pl.semaphore_signal(
            barrier, inc=1, device_id=(lax.rem(me + k, size), core), device_id_type=MESH
        )

    over(1, size, signal)
    pl.semaphore_signal(barrier, inc=1, device_id=(me, 1 - core), device_id_type=MESH)


def wait_all(size):
    pl.semaphore_wait(pltpu.get_barrier_semaphore(), size)


def over(low, high, body):
    def step(k, carry):
        body(k)
        return carry

    lax.fori_loop(low, high, step, 0)


def packed_rows(share):
    return (share + share // 2 + 1 + 15) // 16 * 16


def pack(value, vec):
    share, width = value.shape
    tail = value[:, LANE:]
    tail = jnp.concatenate([tail[: share // 2], tail[share // 2 :]], axis=1)
    if vec.shape[1] < LANE:
        vec = jnp.concatenate([vec, jnp.zeros((1, LANE - vec.shape[1]), F32)], axis=1)
    rest = packed_rows(share) - share - share // 2 - 1
    return jnp.concatenate([value[:, :LANE], tail, vec, jnp.zeros((rest, LANE), F32)], axis=0)


def unpack(block, share):
    at = share + share // 2
    tail = block[share:at]
    tail = jnp.concatenate([tail[:, : LANE // 2], tail[:, LANE // 2 :]], axis=0)
    return jnp.concatenate([block[:share], tail], axis=1), block[at : at + 1]


def gather_kernel(
    group_ref, attn_ref, in_ref, out_ref, vec_ref, tok_hbm, cot_hbm,
    attn_all, in_all, out_all, vec_all, order_ref, x_hbm, c_hbm,
    blocks, tok, cot, xrow, crow, in_sem, row_sem, send_sem, recv_sem, pass_sem, got_sem,
):
    size = attn_all.shape[0]
    share, width = attn_ref.shape
    split = in_ref.shape[0]
    me, core = lax.axis_index("wide"), lax.axis_index("narrow")
    cut = 4 * LANE
    parts = tok_hbm.shape[1] // cut
    pad = xrow.shape[1]

    def lanes(part):
        return pl.ds(pl.multiple_of(part * cut, cut), cut)

    def col_copies(part):
        return [
            pltpu.make_async_copy(ref.at[:, lanes(part)], held.at[:, lanes(part)], in_sem.at[i, part])
            for i, (ref, held) in enumerate(((tok_hbm, tok), (cot_hbm, cot)))
        ]

    def row_copies(part):
        return [
            pltpu.make_async_copy(held.at[lanes(part)], ref.at[lanes(part)], row_sem.at[i, part])
            for i, (held, ref) in enumerate(((xrow, x_hbm), (crow, c_hbm)))
        ]

    signal_all(size, me, core)

    def begin(part):
        for copy in col_copies(part):
            copy.start()

    over(0, parts, begin)
    vec = vec_ref[...]
    blocks[0, me] = pack(attn_ref[...], vec).astype(BF16)
    both = jnp.concatenate([in_ref[...], out_ref[...]], axis=0)
    blocks[1, me] = pack(both, vec).astype(BF16)
    wait_all(size)

    def to_peer(owner, k):
        return pltpu.make_async_remote_copy(
            src_ref=blocks.at[core, owner],
            dst_ref=blocks.at[core, owner],
            send_sem=send_sem.at[k],
            recv_sem=recv_sem.at[owner],
            device_id=(lax.rem(me + k, size), core),
            device_id_type=MESH,
        )

    def to_twin(owner, whose):
        return pltpu.make_async_remote_copy(
            src_ref=blocks.at[whose, owner],
            dst_ref=blocks.at[whose, owner],
            send_sem=pass_sem.at[owner],
            recv_sem=got_sem.at[owner],
            device_id=(me, 1 - core),
            device_id_type=MESH,
        )

    over(1, size, lambda k: to_peer(me, k).start())

    samples = group_ref.shape[1]
    key = group_ref[...] * samples + iota((1, samples), 1)
    wide = jnp.broadcast_to(key.astype(F32), (samples, samples))
    rank = jnp.sum(jnp.where(wide < wide.T, 1.0, 0.0), axis=1, keepdims=True)
    here = rank == iota((samples, samples), 1).astype(F32)
    found = jnp.where(here, iota((samples, samples), 0).astype(F32), 0.0)
    order_ref[...] = jnp.sum(found, axis=0, keepdims=True).astype(jnp.int32)

    zero = jnp.zeros((LANE, pad - width), F32)

    def unfold(part):
        for copy in col_copies(part):
            copy.wait()
        for member in range(4):
            at = pl.multiple_of(part * cut + member * LANE, LANE)
            for held, rows in ((tok, xrow), (cot, crow)):
                value = held[:, pl.ds(at, LANE)].T.astype(F32)
                rows[pl.ds(at, LANE), :] = jnp.concatenate([value, zero], axis=1)
        for copy in row_copies(part):
            copy.start()

    over(0, parts, unfold)

    def forward(k):
        owner = lax.rem(me + size - k, size)
        to_peer(owner, k).wait_recv()
        to_twin(owner, core).start()

    def finish(k):
        owner = lax.rem(me + size - k, size)
        to_peer(me, k).wait_send()
        to_twin(owner, core).wait_send()
        to_twin(owner, 1 - core).wait_recv()

    def end(part):
        for copy in row_copies(part):
            copy.wait()

    def spread_out(owner):
        value, last = unpack(blocks[0, owner].astype(F32), share)
        attn_all[owner] = value.astype(BF16)
        vec_all[owner] = last[:, : vec_all.shape[2]]
        value, _ = unpack(blocks[1, owner].astype(F32), share)
        in_all[owner] = value[:split].astype(BF16)
        out_all[owner] = value[split:].astype(BF16)

    over(1, size, forward)
    over(1, size, finish)
    over(0, size, spread_out)
    over(0, parts, end)


def gather(size, group, attn, ffn_in, ffn_out, vec, tokens_t, cotangent_t):
    vmem = pl.BlockSpec(memory_space=pltpu.VMEM)
    whole = pl.BlockSpec(memory_space=pl.ANY)
    width, rows = tokens_t.shape
    pad = HEADS * STRIDE
    parts = rows // (4 * LANE)
    return pl.pallas_call(
        gather_kernel,
        name="gather",
        out_shape=tuple(
            jax.ShapeDtypeStruct((size, *value.shape), BF16)
            for value in (attn, ffn_in, ffn_out)
        )
        + (
            jax.ShapeDtypeStruct((size, *vec.shape), F32),
            jax.ShapeDtypeStruct(group.shape, jnp.int32),
            jax.ShapeDtypeStruct((rows, pad), F32),
            jax.ShapeDtypeStruct((rows, pad), F32),
        ),
        in_specs=[vmem] * 5 + [whole] * 2,
        out_specs=[vmem] * 5 + [whole] * 2,
        scratch_shapes=[
            pltpu.VMEM((2, size, packed_rows(attn.shape[0]), LANE), BF16),
            pltpu.VMEM((width, rows), BF16),
            pltpu.VMEM((width, rows), BF16),
            pltpu.VMEM((rows, pad), F32),
            pltpu.VMEM((rows, pad), F32),
            pltpu.SemaphoreType.DMA((2, parts)),
            pltpu.SemaphoreType.DMA((2, parts)),
        ]
        + [pltpu.SemaphoreType.DMA((size,))] * 4,
        compiler_params=pltpu.CompilerParams(
            collective_id=0, has_side_effects=True, vmem_limit_bytes=60 * 2**20
        ),
    )(group, attn, ffn_in, ffn_out, vec, tokens_t, cotangent_t)


def reduce_kernel(
    g_attn, g_in, g_out, g_vec,
    s_attn, s_in, s_out, s_vec,
    own, stage, twin, chip, peer, total,
    pass_sem, got_sem, send_sem, recv_sem, last_sem,
):
    size, share = g_attn.shape[:2]
    split = g_in.shape[1]
    me, core = lax.axis_index("wide"), lax.axis_index("narrow")
    signal_all(size, me, core)

    def prepare(owner):
        own[0, owner] = pack(g_attn[owner], g_vec[owner])
        both = jnp.concatenate([g_in[owner], g_out[owner]], axis=0)
        own[1, owner] = pack(both, jnp.zeros((1, LANE), F32))
        stage[owner] = own[1 - core, owner].astype(BF16)

    over(0, size, prepare)
    wait_all(size)

    def to_twin(owner):
        return pltpu.make_async_remote_copy(
            src_ref=stage.at[owner],
            dst_ref=twin.at[owner],
            send_sem=pass_sem.at[owner],
            recv_sem=got_sem.at[owner],
            device_id=(me, 1 - core),
            device_id_type=MESH,
        )

    def to_peer(k, source):
        return pltpu.make_async_remote_copy(
            src_ref=chip.at[lax.rem(me + k, size)],
            dst_ref=peer.at[source],
            send_sem=send_sem.at[k],
            recv_sem=recv_sem.at[source],
            device_id=(lax.rem(me + k, size), core),
            device_id_type=MESH,
        )

    def result(whose):
        return pltpu.make_async_remote_copy(
            src_ref=total.at[whose],
            dst_ref=total.at[whose],
            send_sem=last_sem.at[0],
            recv_sem=last_sem.at[1],
            device_id=(me, 1 - core),
            device_id_type=MESH,
        )

    def send(k):
        owner = lax.rem(me + k, size)
        to_twin(owner).wait_recv()
        chip[owner] = (own[core, owner] + twin[owner].astype(F32)).astype(BF16)
        to_peer(k, me).start()

    def take(k):
        source = lax.rem(me + size - k, size)
        to_peer(k, source).wait_recv()
        total[core] += peer[source].astype(F32)

    def finish(k):
        to_peer(k, me).wait_send()

    over(1, size + 1, lambda k: to_twin(lax.rem(me + k, size)).start())
    over(1, size, send)
    to_twin(me).wait_recv()
    total[core] = own[core, me] + twin[me].astype(F32)
    over(1, size, take)
    result(core).start()
    over(1, size, finish)
    over(0, size, lambda owner: to_twin(owner).wait_send())
    result(core).wait_send()
    result(1 - core).wait_recv()
    value, last = unpack(total[0], share)
    s_attn[...] = value
    s_vec[...] = last[:, : s_vec.shape[1]]
    value, _ = unpack(total[1], share)
    s_in[...] = value[:split]
    s_out[...] = value[split:]


def reduce_scatter(g_attn, g_in, g_out, g_vec):
    grads = (g_attn, g_in, g_out, g_vec)
    size, share = g_attn.shape[:2]
    vmem = pl.BlockSpec(memory_space=pltpu.VMEM)
    block = (packed_rows(share), LANE)
    return pl.pallas_call(
        reduce_kernel,
        name="reduce",
        out_shape=tuple(jax.ShapeDtypeStruct(value.shape[1:], F32) for value in grads),
        in_specs=[vmem] * 4,
        out_specs=[vmem] * 4,
        scratch_shapes=[pltpu.VMEM((2, size, *block), F32)]
        + [pltpu.VMEM((size, *block), BF16)] * 4
        + [pltpu.VMEM((2, *block), F32)]
        + [pltpu.SemaphoreType.DMA((size,))] * 4
        + [pltpu.SemaphoreType.DMA((2,))],
        compiler_params=pltpu.CompilerParams(
            collective_id=1, has_side_effects=True, vmem_limit_bytes=60 * 2**20
        ),
    )(*grads)


def adamw_kernel(*refs):
    for member in range(4):
        master, first, second, grad = (refs[4 * kind + member][...] for kind in range(4))
        results = adamw_update(master, grad, first, second)
        for kind in range(3):
            refs[16 + 3 * member + kind][...] = results[kind]


def adamw(masters, firsts, seconds, grads):
    vmem = pl.BlockSpec(memory_space=pltpu.VMEM)
    return pl.pallas_call(
        adamw_kernel,
        name="adamw",
        out_shape=tuple(
            jax.ShapeDtypeStruct(value.shape, F32) for value in masters for kind in range(3)
        ),
        in_specs=[vmem] * 16,
        out_specs=[vmem] * 12,
        compiler_params=pltpu.CompilerParams(vmem_limit_bytes=60 * 2**20),
    )(*masters, *firsts, *seconds, *grads)


def local(
    tokens,
    cotangent,
    group,
    counts,
    attn_w,
    ffn_in,
    ffn_out,
    vectors,
    attn_m,
    attn_v,
    in_m,
    in_v,
    out_m,
    out_v,
    vec_m,
    vec_v,
):
    size = lax.axis_size("wide")
    width = tokens.shape[1]
    masters = (attn_w, ffn_in, ffn_out, vectors[None])
    attn, into, outof, vec, order, x_rows, c_rows = gather(
        size, group[None], *masters, tokens.T, cotangent.T
    )
    out_t, grad_t, *grads = layer(
        group,
        counts,
        order[0],
        x_rows,
        c_rows,
        attn.reshape(-1, width),
        into.reshape(-1, width),
        outof.reshape(-1, width),
        vec.reshape(-1, 1, LANE),
    )
    sums = reduce_scatter(
        *[g.reshape(size, -1, width) for g in grads[:3]], grads[3].reshape(size, 1, -1)
    )
    results = adamw(
        masters, (attn_m, in_m, out_m, vec_m[None]), (attn_v, in_v, out_v, vec_v[None]), sums
    )
    return (out_t.T, grad_t.T, *results[:9], *[value[0] for value in results[9:]])


def solution(mesh):
    rows = P(("wide", "narrow"), None)
    samples = P(("wide", "narrow"))
    weight = P("wide", None)
    vector = P("wide")
    return jax.shard_map(
        local,
        mesh=mesh,
        in_specs=(rows, rows, samples, samples, weight, weight, weight, vector)
        + (weight,) * 6
        + (vector,) * 2,
        out_specs=(rows, rows) + (weight,) * 9 + (vector,) * 3,
        check_vma=False,
    )
```

```python
import functools
import math

import jax
import jax.numpy as jnp
from jax import lax
from jax.experimental import pallas as pl
from jax.experimental.pallas import tpu as pltpu
from jax.sharding import PartitionSpec as P

HEADS = 8
SLOT = 104
L1 = 40
L2 = 68
L3 = 100
STEP = 10

NORM_EPS = 1e-05
BETA_ONE = 0.9
BETA_TWO = 0.999
ADAM_EPS = 1e-08
LEARN_RATE = 0.1
WEIGHT_DECAY = 0.01
MASK_VALUE = -1e30

F32 = jnp.float32
BF16 = jnp.bfloat16
LANE = 128
MESH = pl.DeviceIdType.MESH
STRIDE = 32
NN = (((1,), (0,)), ((), ()))
NT = (((1,), (1,)), ((), ()))
TN = (((0,), (0,)), ((), ()))
BATCH = 4
SPARE = 24


def adamw_update(master, gradient, moment, square):
    moment_new = BETA_ONE * moment + (1.0 - BETA_ONE) * gradient
    square_new = BETA_TWO * square + (1.0 - BETA_TWO) * gradient * gradient
    moment_hat = moment_new / (1.0 - BETA_ONE**STEP)
    square_hat = square_new / (1.0 - BETA_TWO**STEP)
    master_new = master - LEARN_RATE * (
        moment_hat / (jnp.sqrt(square_hat) + ADAM_EPS) + WEIGHT_DECAY * master
    )
    return (master_new, moment_new, square_new)


def dot(a, b, dims=NN):
    return lax.dot_general(a, b, dims, preferred_element_type=F32)


def iota(shape, dim):
    return lax.broadcasted_iota(jnp.int32, shape, dim)


def partial_sums(value):
    rows, cols = value.shape
    return jnp.sum(value.reshape(rows // 8, 8, cols), axis=0)


def piece(vec, member, width):
    start = member * width
    parts, at = [], start
    while at < start + width:
        row, lane = divmod(at, LANE)
        take = min(LANE - lane, start + width - at)
        parts.append(vec[row : row + 1, lane : lane + take])
        at += take
    return jnp.concatenate(parts, axis=1)


def layer_kernel(
    group_ref,
    counts_ref,
    order,
    x_hbm,
    c_hbm,
    attn_ref,
    in_ref,
    out_ref,
    vec_ref,
    y_ref,
    dx_ref,
    g_attn_ref,
    g_in_ref,
    g_out_ref,
    g_vec_ref,
    xrow,
    crow,
    y_cols,
    dx_cols,
    row_sem,
    col_sem,
    w_qkv,
    w_qkv_t,
    w_o,
    w_o_t,
    w_in,
    w_in_t,
    w_out,
    w_out_t,
    probs,
    scores,
    k_rows,
    v_rows,
    v_cols,
    cols,
    acc_qkv,
    acc_o,
    acc_in,
    acc_out,
    acc_small,
    *carried,
):
    width = attn_ref.shape[1]
    hidden = out_ref.shape[0]
    samples = group_ref.shape[0]
    rows_all = x_hbm.shape[0]
    head = width // HEADS
    pad = HEADS * STRIDE
    scale = 1.0 / math.sqrt(head)
    log2e = math.log2(math.e)
    q_scale = scale * log2e

    steps = samples // (2 * BATCH)

    def fetch(step):
        for j in range(2 * BATCH):
            rows = pl.ds(pl.multiple_of(order[step * 2 * BATCH + j] * SLOT, 8), SLOT)
            for ref, held in ((x_hbm, xrow), (c_hbm, crow)):
                pltpu.make_async_copy(ref.at[rows], held.at[rows], row_sem.at[step]).start()

    def fetched(step):
        rows = pl.ds(0, 2 * BATCH * SLOT)
        for ref, held in ((x_hbm, xrow), (c_hbm, crow)):
            pltpu.make_async_copy(ref.at[rows], held.at[rows], row_sem.at[step]).wait()

    fetch(0)
    fetch(1)

    spread_row = iota((width, pad), 0)
    spread_col = iota((width, pad), 1)
    within = spread_col & (STRIDE - 1)
    spread = jnp.where(
        (within < head) & (spread_row == (spread_col >> 5) * head + within), 1.0, 0.0
    ).astype(BF16)
    vec = jnp.concatenate([vec_ref[row] for row in range(vec_ref.shape[0])], axis=0)
    bi = jnp.concatenate([vec[row : row + 1] for row in range(12, 16)], axis=1)

    def widen(value, fill=0.0):
        rows = value.shape[0]
        tail = jnp.where(iota((rows, pad - width), 1) == 0, fill, 0.0)
        return jnp.concatenate([value, tail], axis=1)

    def lengthen(value, row=None):
        cols = value.shape[1]
        if row is None:
            row = jnp.zeros((1, cols), F32)
        tail = jnp.concatenate([row, jnp.zeros((pad - width - 1, cols), F32)], axis=0)
        return jnp.concatenate([value, tail], axis=0)

    g1, b1, g2, b2, bq, bv, bo, bf = (piece(vec, member, width) for member in range(8))
    g1, b1, g2, b2 = widen(g1), widen(b1, 1.0), widen(g2), widen(b2, 1.0)
    bf = widen(bf)
    spare_lane = (iota((1, pad), 1) & (STRIDE - 1)) == SPARE
    for member in range(3):
        spread_w = dot(attn_ref[member * width : (member + 1) * width, :], spread)
        if member == 0:
            bias = dot(bq.astype(BF16), spread) + jnp.where(spare_lane, 1.0, 0.0)
        elif member == 1:
            bias = None
        else:
            bias = dot(bv.astype(BF16), spread)
        w_qkv[:, member * pad : (member + 1) * pad] = lengthen(spread_w, bias).astype(BF16)
        w_qkv_t[member * pad : (member + 1) * pad, :] = widen(spread_w.T).astype(BF16)
    spread_o = widen(dot(spread, attn_ref[3 * width :, :], TN))
    w_o_t[...] = spread_o.T.astype(BF16)
    w_o[...] = jnp.where(iota((pad, pad), 0) == SPARE, widen(bo), spread_o).astype(BF16)
    in_wide = widen(in_ref[...].astype(F32))
    out_wide = widen(out_ref[...].astype(F32))
    w_in_t[...] = in_wide.astype(BF16)
    w_in[...] = lengthen(in_wide[:, :width].T, bi).astype(BF16)
    w_out[...] = out_wide.astype(BF16)
    w_out_t[...] = out_wide.T.astype(BF16)

    for ref in (acc_qkv, acc_o, acc_in, acc_out, acc_small, *carried):
        ref[...] = jnp.zeros_like(ref)
    names = ("q_rows", "d_rows", "probs_low", "ds_low", "k_cols", "dq_cols", "hat", "inv")
    names += ("h2", "du", "hid", "df", "o", "da")
    kept = [
        dict(zip(names, carried[side * len(names) : (side + 1) * len(names)]))
        for side in range(2)
    ]

    features = iota((1, pad), 1) < width

    def norm_stats(x):
        mean = jnp.sum(x, -1, keepdims=True) * (1.0 / width)
        centre = jnp.where(features, x - mean, 0.0)
        spread_sq = jnp.sum(centre * centre, -1, keepdims=True) * (1.0 / width)
        inv = lax.rsqrt(spread_sq + NORM_EPS)
        return centre * inv, inv

    def norm_back(scaled, crossed, hat, inv):
        mean_one = jnp.sum(scaled, -1, keepdims=True) * (1.0 / width)
        mean_two = jnp.sum(crossed, -1, keepdims=True) * (1.0 / width)
        return inv * (scaled - mean_one - hat * mean_two)

    half = [
        (iota((1, LANE), 1) >> 5) == member for member in range(LANE // STRIDE)
    ]

    def group_rows(block, group, per):
        first = group * per
        lanes = block[:, first // 4 * LANE : (first // 4 + 1) * LANE]
        zero = jnp.zeros_like(lanes)
        return jnp.concatenate(
            [jnp.where(half[(first + i) % 4], lanes, zero) for i in range(per)], axis=0
        )

    def pad_rows(value, size=LANE):
        rows = value.shape[0]
        return jnp.concatenate([value, jnp.zeros((size - rows, value.shape[1]), F32)], axis=0)

    lead = width + 8

    def grouping(n):
        per = 4 if n <= 64 else 2
        groups = HEADS // per
        return per, groups, [(j, group) for j in range(BATCH) for group in range(groups)]

    def tile(group, per):
        first = group * per // 4
        return slice(first * LANE, (first + 1) * LANE)

    def heads(group, per):
        return slice(per * STRIDE * group, per * STRIDE * (group + 1))

    def keep_own(ref, j, group, per, product):
        size = 2 * LANE // per
        for i in range(per):
            block = product[i * STRIDE : (i + 1) * STRIDE]
            at = i * size // LANE
            block = block[:, at * LANE : (at + 1) * LANE]
            if i * size % LANE:
                block = pltpu.roll(block, LANE - i * size % LANE, 1)
            ref[j, per * group + i] = block

    def bases(first):
        return [pl.multiple_of(order[first + j] * SLOT, 8) for j in range(BATCH)]

    def stack(values):
        return jnp.concatenate(values, axis=0)

    def front(box, first, n):
        cuts = {40: (0, 40), 72: (0, 40, 72), 104: (0, 32, 64, 104)}[n]
        chunks = [
            (j, lo, hi) for j in range(BATCH) for lo, hi in zip(cuts[:-1], cuts[1:])
        ]
        at = bases(first)
        limits, live = [], []
        for j in range(BATCH):
            s = order[first + j]
            g = group_ref[s]
            limits.append(jnp.where(g == 0, L1, jnp.where(g == 1, L2, L3)))
            live.append(counts_ref[s])

        per, groups, every = grouping(n)

        def keep(j, lo, hi):
            return jnp.where(iota((hi - lo, 1), 0) + lo < limits[j], 1.0, 0.0)

        def rows_of(ref, j, lo, hi):
            return ref[pl.ds(at[j] + lo, hi - lo), :]

        def flat(j, lo, hi):
            return slice(j * n + lo, j * n + hi)

        h1 = []
        for j, lo, hi in chunks:
            hat1, inv1 = norm_stats(rows_of(xrow, j, lo, hi))
            box["hat"][j, lo:hi] = hat1
            box["inv"][j, lo:hi] = inv1
            h1.append(hat1 * g1 + b1)
        yield
        qkv = dot(stack(h1).astype(BF16), w_qkv[...])
        for j in range(BATCH):
            rows = slice(j * n, (j + 1) * n)
            q = pad_rows(qkv[rows, :pad] * q_scale, 2 * LANE // per).astype(BF16)
            dead = iota((n, 1), 0) >= live[j]
            k32 = jnp.where(dead & spare_lane, MASK_VALUE, qkv[rows, pad : 2 * pad])
            v32 = qkv[rows, 2 * pad :]
            for group in range(groups):
                box["q_rows"][j, group] = group_rows(q, group, per)
            k_rows[j, :n] = k32.astype(BF16)
            v_rows[j, :n] = v32.astype(BF16)
            box["k_cols"][j] = pad_rows(k32).astype(BF16).T
            v_cols[j] = pad_rows(v32).astype(BF16).T
            yield
        for j, group in every:
            scores[j, group, :n] = dot(
                k_rows[j, :n, tile(group, per)], box["q_rows"][j, group], NT
            )
        yield
        for j, group in every:
            score = scores[j, group, :n]
            e = jnp.exp2(score - jnp.max(score, axis=0, keepdims=True))
            p = e * (1.0 / jnp.sum(e, axis=0, keepdims=True))
            probs[j, group, :n] = p
            box["probs_low"][j, group, :n] = p.astype(BF16)
            if group == groups - 1:
                yield
        for j, group in every:
            o_t = dot(v_cols[j, heads(group, per), :n], box["probs_low"][j, group, :n])
            keep_own(cols, j, group, per, o_t)
        yield
        mixed = stack([cols[j].reshape(pad, LANE).T[:n] for j in range(BATCH)])
        o = jnp.where(iota((1, pad), 1) == SPARE, 1.0, mixed).astype(BF16)
        box["o"][: BATCH * n] = o
        yield
        a = dot(o, w_o[...])
        y1, hat2, inv2, h2 = [], [], [], []
        for c in chunks:
            y = rows_of(xrow, *c) + keep(*c) * a[flat(*c)]
            hat, inv = norm_stats(y)
            y1.append(y)
            hat2.append(hat)
            inv2.append(inv)
            h2.append(hat * g2 + b2)
        h2 = stack(h2).astype(BF16)
        box["h2"][: BATCH * n] = h2
        yield
        u = dot(h2, w_in[...])
        df = stack([keep(*c) * rows_of(crow, *c) for c in chunks])
        df_low = df.astype(BF16)
        box["df"][: BATCH * n] = df_low
        acc_small[0:8, :] += partial_sums(df)
        dhid = dot(df_low, w_out_t[...])
        yield
        hid, du = [], []
        alpha, beta = 0.7978845608028654, 0.044715
        for c in chunks:
            z, up = u[flat(*c), :hidden], u[flat(*c), hidden:]
            dh = dhid[flat(*c)]
            inner = alpha + (alpha * beta) * (z * z)
            gate = 0.5 + 0.5 * jnp.tanh(z * inner)
            act = z * gate
            slope = gate + (act * (1.0 - gate)) * (6.0 * inner - 4.0 * alpha)
            hid.append(act * up)
            du.append(jnp.concatenate([dh * up * slope, dh * act], axis=1))
            if c[1] == 0:
                yield
        hid = stack(hid).astype(BF16)
        box["hid"][: BATCH * n] = hid
        du = stack(du).astype(BF16)
        box["du"][: BATCH * n] = du
        yield
        f = dot(hid, w_out[...])
        dh2 = dot(du, w_in_t[...])
        yield
        da = []
        gain = jnp.zeros((8, pad), F32)
        for i, c in enumerate(chunks):
            j, lo, hi = c
            xrow[pl.ds(at[j] + lo, hi - lo), :] = y1[i] + keep(*c) * (f[flat(*c)] + bf)
            grad = dh2[flat(*c)]
            crossed = grad * hat2[i]
            gain += partial_sums(crossed)
            dy1 = rows_of(crow, *c) + norm_back(grad * g2, crossed * g2, hat2[i], inv2[i])
            crow[pl.ds(at[j] + lo, hi - lo), :] = dy1
            da.append(keep(*c) * dy1)
        acc_small[8:16, :] += gain
        da = stack(da).astype(BF16)
        box["da"][: BATCH * n] = da
        yield
        do = dot(da, w_o_t[...])
        for j in range(BATCH):
            d_low = pad_rows(do[j * n : (j + 1) * n], 2 * LANE // per).astype(BF16)
            for group in range(groups):
                box["d_rows"][j, group] = group_rows(d_low, group, per)
        yield
        for j, group in every:
            scores[j, group, :n] = dot(
                v_rows[j, :n, tile(group, per)], box["d_rows"][j, group], NT
            )
        yield
        for j, group in every:
            dp = scores[j, group, :n]
            p = probs[j, group, :n]
            box["ds_low"][j, group, :n] = (
                p * (dp - jnp.sum(dp * p, axis=0, keepdims=True))
            ).astype(BF16)
            if group == groups - 1:
                yield

    def back(box, first, n, layout):
        per, groups, every = grouping(layout)
        rows = slice(0, BATCH * n)
        at = bases(first)
        for j, group in every:
            dq_t = dot(box["k_cols"][j, heads(group, per), :n], box["ds_low"][j, group, :n])
            keep_own(box["dq_cols"], j, group, per, dq_t)
            if group == groups - 1:
                yield
        parts = []
        for j in range(BATCH):
            dvs = [
                dot(box["probs_low"][j, group, :n], box["d_rows"][j, group])
                for group in range(groups)
            ]
            yield
            dks = [
                dot(box["ds_low"][j, group, :n], box["q_rows"][j, group])
                for group in range(groups)
            ]
            if per == 2:
                dvs = [dvs[0] + dvs[1], dvs[2] + dvs[3]]
                dks = [dks[0] + dks[1], dks[2] + dks[3]]
            dq = box["dq_cols"][j].reshape(pad, LANE).T[:n] * scale
            dks = [value * (1.0 / log2e) for value in dks]
            parts.append(jnp.concatenate([dq, *dks, *dvs], axis=1))
            yield
        dqkv = stack(parts).astype(BF16)
        dh1 = dot(dqkv, w_qkv_t[...])
        yield
        acc_out[...] += dot(box["df"][rows, :width], box["hid"][rows], TN)
        yield
        acc_o[...] += dot(box["da"][rows, :width], box["o"][rows], TN)
        yield
        acc_in[...] += dot(box["h2"][rows, :lead], box["du"][rows], TN)
        yield
        h1 = []
        gain = jnp.zeros((8, pad), F32)
        for j in range(BATCH):
            hat = box["hat"][j, :n]
            grad = dh1[j * n : (j + 1) * n]
            crossed = grad * hat
            gain += partial_sums(crossed)
            crow[pl.ds(at[j], n), :] += norm_back(
                grad * g1, crossed * g1, hat, box["inv"][j, :n]
            )
            h1.append(hat * g1 + b1)
            if j % 2:
                yield
        acc_small[16:24, :] += gain
        h1 = stack(h1).astype(BF16)
        acc_qkv[...] += dot(h1[:, :lead], dqkv, TN)

    def together(first, second):
        going = [first, second]
        while going:
            for part in list(going):
                if next(part, going) is going:
                    going.remove(part)

    def double(step, n):
        even = step * 2 * BATCH
        before = jnp.maximum(even - BATCH, 0)
        together(back(kept[1], before, n, n), front(kept[0], even, n))
        together(back(kept[0], even, n, n), front(kept[1], even + BATCH, n))

    lengths = (40, 72, 104)
    def kind_of(step):
        return group_ref[order[(step + 1) * 2 * BATCH - 1]]

    def finish_short(step):
        together(back(kept[1], step * 2 * BATCH - BATCH, 40, 40), iter(()))
        for name in ("ds_low", "d_rows", "du", "df", "da"):
            kept[1][name][...] = jnp.zeros_like(kept[1][name])

    def one_step(step, carry):
        kind = kind_of(jnp.minimum(step, steps - 1))
        last = kind_of(jnp.maximum(step - 1, 0))
        pl.when((step > 0) & (last == 0) & ((step == steps) | (kind != 0)))(
            functools.partial(finish_short, step)
        )
        pl.when(step < steps)(lambda: fetched(step))
        pl.when(step + 2 < steps)(lambda: fetch(step + 2))
        for member, n in enumerate(lengths):
            pl.when((step < steps) & (kind == member))(functools.partial(double, step, n))
        return carry

    lax.fori_loop(0, steps + 1, one_step, 0)
    together(back(kept[1], samples - BATCH, SLOT, SLOT), iter(()))

    cut = 4 * LANE

    def col_copies(part):
        lanes = pl.ds(pl.multiple_of(part * cut, cut), cut)
        return [
            pltpu.make_async_copy(held.at[:, lanes], ref.at[:, lanes], col_sem.at[i, part])
            for i, (held, ref) in enumerate(((y_cols, y_ref), (dx_cols, dx_ref)))
        ]

    def fold(part, carry):
        for member in range(4):
            at = pl.multiple_of(part * cut + member * LANE, LANE)
            y_cols[:, pl.ds(at, LANE)] = xrow[pl.ds(at, LANE), :width].astype(BF16).T
            dx_cols[:, pl.ds(at, LANE)] = crow[pl.ds(at, LANE), :width].T
        for copy in col_copies(part):
            copy.start()
        return carry

    lax.fori_loop(0, rows_all // cut, fold, 0)

    def gather_heads(value):
        return lax.dot_general(
            value, spread.astype(F32), NT, precision=lax.Precision.HIGHEST,
            preferred_element_type=F32,
        )

    for member in range(3):
        g_attn_ref[member * width : (member + 1) * width, :] = gather_heads(
            acc_qkv[:width, member * pad : (member + 1) * pad]
        )
    g_attn_ref[3 * width :, :] = lax.dot_general(
        spread.astype(F32), acc_o[...], NT, precision=lax.Precision.HIGHEST,
        preferred_element_type=F32,
    )
    g_in_ref[...] = acc_in[:width, :].T
    g_out_ref[...] = acc_out[...].T

    def small(member):
        block = acc_small[8 * member : 8 * member + 8, :width]
        return jnp.sum(block, axis=0, keepdims=True)

    def exact(a, b):
        return lax.dot_general(
            a, b.astype(F32), NN, precision=lax.Precision.HIGHEST, preferred_element_type=F32
        )[0:1]

    qkv_sums = acc_qkv[width : width + 8, :]
    in_sums = acc_in[width : width + 8, :]
    g_b1 = exact(qkv_sums, w_qkv_t[...])[:, :width]
    g_b2 = exact(in_sums, w_in_t[...])[:, :width]
    g_bq = gather_heads(qkv_sums[:, :pad])[0:1]
    g_bv = gather_heads(qkv_sums[:, 2 * pad :])[0:1]
    g_bo = acc_o[...].T[SPARE : SPARE + 1]
    flat = jnp.concatenate(
        [small(2), g_b1, small(1), g_b2, g_bq, g_bv, g_bo, small(0), in_sums[0:1]], axis=1
    )
    for row in range(16):
        g_vec_ref[row] = flat[:, row * LANE : (row + 1) * LANE]

    def folded(part, carry):
        for copy in col_copies(part):
            copy.wait()
        return carry

    lax.fori_loop(0, rows_all // cut, folded, 0)


def layer(group, counts, order, x_rows, c_rows, attn, ffn_in, ffn_out, vec):
    rows, width = x_rows.shape[0], attn.shape[1]
    hidden = ffn_out.shape[0]
    pad = HEADS * STRIDE
    vmem = pl.BlockSpec(memory_space=pltpu.VMEM)
    smem = pl.BlockSpec(memory_space=pltpu.SMEM)
    whole = pl.BlockSpec(memory_space=pl.ANY)
    return pl.pallas_call(
        layer_kernel,
        name="layer",
        out_shape=(
            jax.ShapeDtypeStruct((width, rows), BF16),
            jax.ShapeDtypeStruct((width, rows), F32),
            jax.ShapeDtypeStruct((4 * width, width), F32),
            jax.ShapeDtypeStruct((2 * hidden, width), F32),
            jax.ShapeDtypeStruct((hidden, width), F32),
            jax.ShapeDtypeStruct((16, 1, LANE), F32),
        ),
        in_specs=[smem] * 3 + [whole] * 2 + [vmem] * 4,
        out_specs=[whole] * 2 + [vmem] * 4,
        scratch_shapes=[
            pltpu.VMEM((rows, pad), F32),
            pltpu.VMEM((rows, pad), F32),
            pltpu.VMEM((width, rows), BF16),
            pltpu.VMEM((width, rows), F32),
            pltpu.SemaphoreType.DMA((group.shape[0] // (2 * BATCH),)),
            pltpu.SemaphoreType.DMA((2, rows // (4 * LANE))),
            pltpu.VMEM((pad, 3 * pad), BF16),
            pltpu.VMEM((3 * pad, pad), BF16),
            pltpu.VMEM((pad, pad), BF16),
            pltpu.VMEM((pad, pad), BF16),
            pltpu.VMEM((pad, 2 * hidden), BF16),
            pltpu.VMEM((2 * hidden, pad), BF16),
            pltpu.VMEM((hidden, pad), BF16),
            pltpu.VMEM((pad, hidden), BF16),
            pltpu.VMEM((BATCH, HEADS // 2, SLOT, 2 * LANE), F32),
            pltpu.VMEM((BATCH, HEADS // 2, SLOT, 2 * LANE), F32),
            pltpu.VMEM((BATCH, SLOT, pad), BF16),
            pltpu.VMEM((BATCH, SLOT, pad), BF16),
            pltpu.VMEM((BATCH, pad, LANE), BF16),
            pltpu.VMEM((BATCH, HEADS, STRIDE, LANE), F32),
            pltpu.VMEM((width + 8, 3 * pad), F32),
            pltpu.VMEM((width, pad), F32),
            pltpu.VMEM((width + 8, 2 * hidden), F32),
            pltpu.VMEM((width, hidden), F32),
            pltpu.VMEM((24, pad), F32),
        ]
        + [
            pltpu.VMEM((BATCH, HEADS // 2, 2 * LANE, LANE), BF16),
            pltpu.VMEM((BATCH, HEADS // 2, 2 * LANE, LANE), BF16),
            pltpu.VMEM((BATCH, HEADS // 2, SLOT, 2 * LANE), BF16),
            pltpu.VMEM((BATCH, HEADS // 2, SLOT, 2 * LANE), BF16),
            pltpu.VMEM((BATCH, pad, LANE), BF16),
            pltpu.VMEM((BATCH, HEADS, STRIDE, LANE), F32),
            pltpu.VMEM((BATCH, SLOT, pad), F32),
            pltpu.VMEM((BATCH, SLOT, 1), F32),
            pltpu.VMEM((BATCH * SLOT, pad), BF16),
            pltpu.VMEM((BATCH * SLOT, 2 * hidden), BF16),
            pltpu.VMEM((BATCH * SLOT, hidden), BF16),
            pltpu.VMEM((BATCH * SLOT, pad), BF16),
            pltpu.VMEM((BATCH * SLOT, pad), BF16),
            pltpu.VMEM((BATCH * SLOT, pad), BF16),
        ]
        * 2,
        compiler_params=pltpu.CompilerParams(vmem_limit_bytes=60 * 2**20),
    )(group, counts, order, x_rows, c_rows, attn, ffn_in, ffn_out, vec)


class Place:
    def __init__(self, size):
        side = 1
        while 2 * (2 * side) ** 3 <= size:
            side *= 2
        self.size, self.spots = size, side * side
        self.layers = size // self.spots
        me, self.core = lax.axis_index("wide"), lax.axis_index("narrow")
        self.me = me
        self.layer, self.spot = me // self.spots, lax.rem(me, self.spots)

    def at(self, layer, spot):
        layer = lax.rem(self.layer + layer + self.layers, self.layers)
        return layer * self.spots + lax.rem(self.spot + spot + self.spots, self.spots)

    def signal(self):
        barrier = pltpu.get_barrier_semaphore()

        def tell(index, core):
            pl.semaphore_signal(
                barrier, inc=1, device_id=(index, core), device_id_type=MESH
            )

        over(1, self.layers, lambda k: tell(self.at(k, 0), self.core))
        over(1, self.spots, lambda k: tell(self.at(0, k), self.core))
        tell(self.me, 1 - self.core)

    def wait(self):
        pl.semaphore_wait(
            pltpu.get_barrier_semaphore(), self.layers + self.spots - 1
        )


def over(low, high, body):
    def step(k, carry):
        body(k)
        return carry

    lax.fori_loop(low, high, step, 0)


def packed_rows(share):
    return (share + share // 2 + 1 + 15) // 16 * 16


def pack(value, vec):
    share, width = value.shape
    tail = value[:, LANE:]
    tail = jnp.concatenate([tail[: share // 2], tail[share // 2 :]], axis=1)
    if vec.shape[1] < LANE:
        vec = jnp.concatenate([vec, jnp.zeros((1, LANE - vec.shape[1]), F32)], axis=1)
    rest = packed_rows(share) - share - share // 2 - 1
    return jnp.concatenate([value[:, :LANE], tail, vec, jnp.zeros((rest, LANE), F32)], axis=0)


def unpack(block, share):
    at = share + share // 2
    tail = block[share:at]
    tail = jnp.concatenate([tail[:, : LANE // 2], tail[:, LANE // 2 :]], axis=0)
    return jnp.concatenate([block[:share], tail], axis=1), block[at : at + 1]


def gather_kernel(
    group_ref, attn_ref, in_ref, out_ref, vec_ref, tok_hbm, cot_hbm,
    attn_all, in_all, out_all, vec_all, order_ref, x_hbm, c_hbm,
    blocks, tok, cot, xrow, crow, in_sem, row_sem, send_sem, recv_sem, pass_sem, got_sem,
):
    size = attn_all.shape[0]
    share, width = attn_ref.shape
    split = in_ref.shape[0]
    place = Place(size)
    me, core, layers, spots = place.me, place.core, place.layers, place.spots
    cut = 4 * LANE
    parts = tok_hbm.shape[1] // cut
    pad = xrow.shape[1]

    def lanes(part):
        return pl.ds(pl.multiple_of(part * cut, cut), cut)

    def col_copies(part):
        return [
            pltpu.make_async_copy(ref.at[:, lanes(part)], held.at[:, lanes(part)], in_sem.at[i, part])
            for i, (ref, held) in enumerate(((tok_hbm, tok), (cot_hbm, cot)))
        ]

    def row_copies(part):
        return [
            pltpu.make_async_copy(held.at[lanes(part)], ref.at[lanes(part)], row_sem.at[i, part])
            for i, (held, ref) in enumerate(((xrow, x_hbm), (crow, c_hbm)))
        ]

    place.signal()

    def begin(part):
        for copy in col_copies(part):
            copy.start()

    over(0, parts, begin)
    vec = vec_ref[...]
    blocks[0, me] = pack(attn_ref[...], vec).astype(BF16)
    both = jnp.concatenate([in_ref[...], out_ref[...]], axis=0)
    blocks[1, me] = pack(both, vec).astype(BF16)
    place.wait()

    def to_peer(owner, target, slot):
        return pltpu.make_async_remote_copy(
            src_ref=blocks.at[core, owner],
            dst_ref=blocks.at[core, owner],
            send_sem=send_sem.at[slot],
            recv_sem=recv_sem.at[owner],
            device_id=(target, core),
            device_id_type=MESH,
        )

    def to_twin(owner, whose):
        return pltpu.make_async_remote_copy(
            src_ref=blocks.at[whose, owner],
            dst_ref=blocks.at[whose, owner],
            send_sem=pass_sem.at[owner],
            recv_sem=got_sem.at[owner],
            device_id=(me, 1 - core),
            device_id_type=MESH,
        )

    def along(k):
        return to_peer(me, place.at(k, 0), layers * (spots - 1) + k - 1)

    def within(layer, k):
        owner = place.at(-layer, 0)
        return to_peer(owner, place.at(0, k), layer * (spots - 1) + k - 1)

    over(1, layers, lambda k: along(k).start())
    over(1, spots, lambda k: within(0, k).start())

    samples = group_ref.shape[1]
    key = group_ref[...] * samples + iota((1, samples), 1)
    wide = jnp.broadcast_to(key.astype(F32), (samples, samples))
    rank = jnp.sum(jnp.where(wide < wide.T, 1.0, 0.0), axis=1, keepdims=True)
    here = rank == iota((samples, samples), 1).astype(F32)
    found = jnp.where(here, iota((samples, samples), 0).astype(F32), 0.0)
    order_ref[...] = jnp.sum(found, axis=0, keepdims=True).astype(jnp.int32)

    zero = jnp.zeros((LANE, pad - width), F32)

    def unfold(part):
        for copy in col_copies(part):
            copy.wait()
        for member in range(4):
            at = pl.multiple_of(part * cut + member * LANE, LANE)
            for held, rows in ((tok, xrow), (cot, crow)):
                value = held[:, pl.ds(at, LANE)].T.astype(F32)
                rows[pl.ds(at, LANE), :] = jnp.concatenate([value, zero], axis=1)
        for copy in row_copies(part):
            copy.start()

    def arrived(owner):
        to_peer(owner, me, 0).wait_recv()
        to_twin(owner, core).start()

    def forward(layer):
        to_peer(place.at(-layer, 0), me, 0).wait_recv()
        over(1, spots, lambda k: within(layer, k).start())
        to_twin(place.at(-layer, 0), core).start()

    early = min(3, parts)
    over(0, early, unfold)
    over(1, layers, forward)
    over(early, parts, unfold)
    over(1, spots, lambda k: over(0, layers, lambda layer: arrived(place.at(-layer, -k))))

    def finish(owner):
        to_twin(owner, core).wait_send()
        to_twin(owner, 1 - core).wait_recv()

    over(1, layers, lambda k: along(k).wait_send())
    over(0, layers, lambda layer: over(1, spots, lambda k: within(layer, k).wait_send()))
    over(1, size, lambda k: finish(lax.rem(me + k, size)))

    def end(part):
        for copy in row_copies(part):
            copy.wait()

    def spread_out(owner):
        value, last = unpack(blocks[0, owner].astype(F32), share)
        attn_all[owner] = value.astype(BF16)
        vec_all[owner] = last[:, : vec_all.shape[2]]
        value, _ = unpack(blocks[1, owner].astype(F32), share)
        in_all[owner] = value[:split].astype(BF16)
        out_all[owner] = value[split:].astype(BF16)

    over(0, size, spread_out)
    over(0, parts, end)


def gather(size, group, attn, ffn_in, ffn_out, vec, tokens_t, cotangent_t):
    vmem = pl.BlockSpec(memory_space=pltpu.VMEM)
    whole = pl.BlockSpec(memory_space=pl.ANY)
    width, rows = tokens_t.shape
    pad = HEADS * STRIDE
    parts = rows // (4 * LANE)
    return pl.pallas_call(
        gather_kernel,
        name="gather",
        out_shape=tuple(
            jax.ShapeDtypeStruct((size, *value.shape), BF16)
            for value in (attn, ffn_in, ffn_out)
        )
        + (
            jax.ShapeDtypeStruct((size, *vec.shape), F32),
            jax.ShapeDtypeStruct(group.shape, jnp.int32),
            jax.ShapeDtypeStruct((rows, pad), F32),
            jax.ShapeDtypeStruct((rows, pad), F32),
        ),
        in_specs=[vmem] * 5 + [whole] * 2,
        out_specs=[vmem] * 5 + [whole] * 2,
        scratch_shapes=[
            pltpu.VMEM((2, size, packed_rows(attn.shape[0]), LANE), BF16),
            pltpu.VMEM((width, rows), BF16),
            pltpu.VMEM((width, rows), BF16),
            pltpu.VMEM((rows, pad), F32),
            pltpu.VMEM((rows, pad), F32),
            pltpu.SemaphoreType.DMA((2, parts)),
            pltpu.SemaphoreType.DMA((2, parts)),
        ]
        + [pltpu.SemaphoreType.DMA((size,))] * 4,
        compiler_params=pltpu.CompilerParams(
            collective_id=0, has_side_effects=True, vmem_limit_bytes=60 * 2**20
        ),
    )(group, attn, ffn_in, ffn_out, vec, tokens_t, cotangent_t)


def reduce_kernel(
    g_attn, g_in, g_out, g_vec,
    s_attn, s_in, s_out, s_vec,
    own, stage, twin, chip, near, relay, far, total,
    pass_sem, got_sem, near_send, near_recv, far_send, far_recv, last_sem,
):
    size, share = g_attn.shape[:2]
    split = g_in.shape[1]
    place = Place(size)
    me, core, layers, spots = place.me, place.core, place.layers, place.spots
    place.signal()

    def prepare(owner):
        own[0, owner] = pack(g_attn[owner], g_vec[owner])
        both = jnp.concatenate([g_in[owner], g_out[owner]], axis=0)
        own[1, owner] = pack(both, jnp.zeros((1, LANE), F32))
        stage[owner] = own[1 - core, owner].astype(BF16)

    over(0, size, prepare)
    place.wait()

    def to_twin(owner):
        return pltpu.make_async_remote_copy(
            src_ref=stage.at[owner],
            dst_ref=twin.at[owner],
            send_sem=pass_sem.at[owner],
            recv_sem=got_sem.at[owner],
            device_id=(me, 1 - core),
            device_id_type=MESH,
        )

    def within(layer, k, spot, owner_layer):
        owner = place.at(layer, k)
        slot = spot * layers + owner_layer
        return pltpu.make_async_remote_copy(
            src_ref=chip.at[owner],
            dst_ref=near.at[slot],
            send_sem=near_send.at[owner],
            recv_sem=near_recv.at[slot],
            device_id=(place.at(0, k), core),
            device_id_type=MESH,
        )

    def along(layer, sender):
        target = lax.rem(place.layer + layer, layers)
        return pltpu.make_async_remote_copy(
            src_ref=relay.at[target],
            dst_ref=far.at[sender],
            send_sem=far_send.at[target],
            recv_sem=far_recv.at[sender],
            device_id=(place.at(layer, 0), core),
            device_id_type=MESH,
        )

    def result(whose):
        return pltpu.make_async_remote_copy(
            src_ref=total.at[whose],
            dst_ref=total.at[whose],
            send_sem=last_sem.at[0],
            recv_sem=last_sem.at[1],
            device_id=(me, 1 - core),
            device_id_type=MESH,
        )

    def layer_of(layer):
        return lax.rem(place.layer + layer, layers)

    def send(k, layer):
        owner = place.at(layer, k)
        to_twin(owner).wait_recv()
        chip[owner] = (own[core, owner] + twin[owner].astype(F32)).astype(BF16)
        within(layer, k, place.spot, layer_of(layer)).start()

    def spot_sum(layer):
        owner = place.at(layer, 0)
        to_twin(owner).wait_recv()
        total[core] = own[core, owner] + twin[owner].astype(F32)

        def add(k):
            spot = lax.rem(place.spot + k, spots)
            within(layer, k, spot, layer_of(layer)).wait_recv()
            total[core] += near[spot * layers + layer_of(layer)].astype(F32)

        over(1, spots, add)

    def pass_on(layer):
        spot_sum(layer)
        relay[layer_of(layer)] = total[core].astype(BF16)
        along(layer, place.layer).start()

    def take(layer):
        sender = layer_of(layer)
        along(layer, sender).wait_recv()
        total[core] += far[sender].astype(F32)

    over(1, spots, lambda k: over(1, layers, lambda layer: to_twin(place.at(layer, k)).start()))
    over(1, layers, lambda layer: to_twin(place.at(layer, 0)).start())
    over(0, spots, lambda k: to_twin(place.at(0, k)).start())
    over(1, spots, lambda k: over(1, layers, lambda layer: send(k, layer)))
    over(1, spots, lambda k: send(k, 0))
    over(1, layers, pass_on)
    spot_sum(0)
    over(1, layers, take)
    result(core).start()
    over(1, spots, lambda k: over(
        0, layers, lambda layer: within(layer, k, place.spot, layer_of(layer)).wait_send()
    ))
    over(1, layers, lambda layer: along(layer, place.layer).wait_send())
    over(0, size, lambda owner: to_twin(owner).wait_send())
    result(core).wait_send()
    result(1 - core).wait_recv()
    value, last = unpack(total[0], share)
    s_attn[...] = value
    s_vec[...] = last[:, : s_vec.shape[1]]
    value, _ = unpack(total[1], share)
    s_in[...] = value[:split]
    s_out[...] = value[split:]


def reduce_scatter(g_attn, g_in, g_out, g_vec):
    grads = (g_attn, g_in, g_out, g_vec)
    size, share = g_attn.shape[:2]
    vmem = pl.BlockSpec(memory_space=pltpu.VMEM)
    block = (packed_rows(share), LANE)
    return pl.pallas_call(
        reduce_kernel,
        name="reduce",
        out_shape=tuple(jax.ShapeDtypeStruct(value.shape[1:], F32) for value in grads),
        in_specs=[vmem] * 4,
        out_specs=[vmem] * 4,
        scratch_shapes=[pltpu.VMEM((2, size, *block), F32)]
        + [pltpu.VMEM((size, *block), BF16)] * 6
        + [pltpu.VMEM((2, *block), F32)]
        + [pltpu.SemaphoreType.DMA((size,))] * 6
        + [pltpu.SemaphoreType.DMA((2,))],
        compiler_params=pltpu.CompilerParams(
            collective_id=1, has_side_effects=True, vmem_limit_bytes=60 * 2**20
        ),
    )(*grads)


def adamw_kernel(*refs):
    for member in range(4):
        master, first, second, grad = (refs[4 * kind + member][...] for kind in range(4))
        results = adamw_update(master, grad, first, second)
        for kind in range(3):
            refs[16 + 3 * member + kind][...] = results[kind]


def adamw(masters, firsts, seconds, grads):
    vmem = pl.BlockSpec(memory_space=pltpu.VMEM)
    return pl.pallas_call(
        adamw_kernel,
        name="adamw",
        out_shape=tuple(
            jax.ShapeDtypeStruct(value.shape, F32) for value in masters for kind in range(3)
        ),
        in_specs=[vmem] * 16,
        out_specs=[vmem] * 12,
        compiler_params=pltpu.CompilerParams(vmem_limit_bytes=60 * 2**20),
    )(*masters, *firsts, *seconds, *grads)


def local(
    tokens,
    cotangent,
    group,
    counts,
    attn_w,
    ffn_in,
    ffn_out,
    vectors,
    attn_m,
    attn_v,
    in_m,
    in_v,
    out_m,
    out_v,
    vec_m,
    vec_v,
):
    size = lax.axis_size("wide")
    width = tokens.shape[1]
    masters = (attn_w, ffn_in, ffn_out, vectors[None])
    attn, into, outof, vec, order, x_rows, c_rows = gather(
        size, group[None], *masters, tokens.T, cotangent.T
    )
    out_t, grad_t, *grads = layer(
        group,
        counts,
        order[0],
        x_rows,
        c_rows,
        attn.reshape(-1, width),
        into.reshape(-1, width),
        outof.reshape(-1, width),
        vec.reshape(-1, 1, LANE),
    )
    sums = reduce_scatter(
        *[g.reshape(size, -1, width) for g in grads[:3]], grads[3].reshape(size, 1, -1)
    )
    results = adamw(
        masters, (attn_m, in_m, out_m, vec_m[None]), (attn_v, in_v, out_v, vec_v[None]), sums
    )
    return (out_t.T, grad_t.T, *results[:9], *[value[0] for value in results[9:]])


def solution(mesh):
    rows = P(("wide", "narrow"), None)
    samples = P(("wide", "narrow"))
    weight = P("wide", None)
    vector = P("wide")
    return jax.shard_map(
        local,
        mesh=mesh,
        in_specs=(rows, rows, samples, samples, weight, weight, weight, vector)
        + (weight,) * 6
        + (vector,) * 2,
        out_specs=(rows, rows) + (weight,) * 9 + (vector,) * 3,
        check_vma=False,
    )
```

```python
import functools
import math

import jax
import jax.numpy as jnp
from jax import lax
from jax.experimental import pallas as pl
from jax.experimental.pallas import tpu as pltpu
from jax.sharding import PartitionSpec as P

HEADS = 8
SLOT = 104
L1 = 40
L2 = 68
L3 = 100
STEP = 10

NORM_EPS = 1e-05
BETA_ONE = 0.9
BETA_TWO = 0.999
ADAM_EPS = 1e-08
LEARN_RATE = 0.1
WEIGHT_DECAY = 0.01
MASK_VALUE = -1e30

F32 = jnp.float32
BF16 = jnp.bfloat16
LANE = 128
MESH = pl.DeviceIdType.MESH
STRIDE = 32
NN = (((1,), (0,)), ((), ()))
NT = (((1,), (1,)), ((), ()))
TN = (((0,), (0,)), ((), ()))
BATCH = 4
SPARE = 24


def adamw_update(master, gradient, moment, square):
    moment_new = BETA_ONE * moment + (1.0 - BETA_ONE) * gradient
    square_new = BETA_TWO * square + (1.0 - BETA_TWO) * gradient * gradient
    moment_hat = moment_new / (1.0 - BETA_ONE**STEP)
    square_hat = square_new / (1.0 - BETA_TWO**STEP)
    master_new = master - LEARN_RATE * (
        moment_hat / (jnp.sqrt(square_hat) + ADAM_EPS) + WEIGHT_DECAY * master
    )
    return (master_new, moment_new, square_new)


def dot(a, b, dims=NN):
    return lax.dot_general(a, b, dims, preferred_element_type=F32)


def iota(shape, dim):
    return lax.broadcasted_iota(jnp.int32, shape, dim)


def partial_sums(value):
    rows, cols = value.shape
    return jnp.sum(value.reshape(rows // 8, 8, cols), axis=0)


def piece(vec, member, width):
    start = member * width
    parts, at = [], start
    while at < start + width:
        row, lane = divmod(at, LANE)
        take = min(LANE - lane, start + width - at)
        parts.append(vec[row : row + 1, lane : lane + take])
        at += take
    return jnp.concatenate(parts, axis=1)


def layer_kernel(
    group_ref,
    counts_ref,
    order,
    x_hbm,
    c_hbm,
    attn_ref,
    in_ref,
    out_ref,
    vec_ref,
    y_ref,
    dx_ref,
    g_attn_ref,
    g_in_ref,
    g_out_ref,
    g_vec_ref,
    xrow,
    crow,
    y_cols,
    dx_cols,
    row_sem,
    col_sem,
    w_qkv,
    w_qkv_t,
    w_o,
    w_o_t,
    w_in,
    w_in_t,
    w_out,
    w_out_t,
    probs,
    scores,
    k_rows,
    v_rows,
    v_cols,
    cols,
    acc_qkv,
    acc_o,
    acc_in,
    acc_out,
    acc_small,
    *carried,
):
    width = attn_ref.shape[1]
    hidden = out_ref.shape[0]
    samples = group_ref.shape[0]
    rows_all = x_hbm.shape[0]
    head = width // HEADS
    pad = HEADS * STRIDE
    scale = 1.0 / math.sqrt(head)
    log2e = math.log2(math.e)
    q_scale = scale * log2e

    steps = samples // (2 * BATCH)

    def fetch(step):
        for j in range(2 * BATCH):
            rows = pl.ds(pl.multiple_of(order[step * 2 * BATCH + j] * SLOT, 8), SLOT)
            for ref, held in ((x_hbm, xrow), (c_hbm, crow)):
                pltpu.make_async_copy(ref.at[rows], held.at[rows], row_sem.at[step]).start()

    def fetched(step):
        rows = pl.ds(0, 2 * BATCH * SLOT)
        for ref, held in ((x_hbm, xrow), (c_hbm, crow)):
            pltpu.make_async_copy(ref.at[rows], held.at[rows], row_sem.at[step]).wait()

    fetch(0)
    fetch(1)

    spread_row = iota((width, pad), 0)
    spread_col = iota((width, pad), 1)
    within = spread_col & (STRIDE - 1)
    spread = jnp.where(
        (within < head) & (spread_row == (spread_col >> 5) * head + within), 1.0, 0.0
    ).astype(BF16)
    vec = jnp.concatenate([vec_ref[row] for row in range(vec_ref.shape[0])], axis=0)
    bi = jnp.concatenate([vec[row : row + 1] for row in range(12, 16)], axis=1)

    def widen(value, fill=0.0):
        rows = value.shape[0]
        tail = jnp.where(iota((rows, pad - width), 1) == 0, fill, 0.0)
        return jnp.concatenate([value, tail], axis=1)

    def lengthen(value, row=None):
        cols = value.shape[1]
        if row is None:
            row = jnp.zeros((1, cols), F32)
        tail = jnp.concatenate([row, jnp.zeros((pad - width - 1, cols), F32)], axis=0)
        return jnp.concatenate([value, tail], axis=0)

    g1, b1, g2, b2, bq, bv, bo, bf = (piece(vec, member, width) for member in range(8))
    g1, b1, g2, b2 = widen(g1), widen(b1, 1.0), widen(g2), widen(b2, 1.0)
    bf = widen(bf)
    spare_lane = (iota((1, pad), 1) & (STRIDE - 1)) == SPARE
    for member in range(3):
        spread_w = dot(attn_ref[member * width : (member + 1) * width, :], spread)
        if member == 0:
            bias = dot(bq.astype(BF16), spread) + jnp.where(spare_lane, 1.0, 0.0)
        elif member == 1:
            bias = None
        else:
            bias = dot(bv.astype(BF16), spread)
        w_qkv[:, member * pad : (member + 1) * pad] = lengthen(spread_w, bias).astype(BF16)
        w_qkv_t[member * pad : (member + 1) * pad, :] = widen(spread_w.T).astype(BF16)
    spread_o = widen(dot(spread, attn_ref[3 * width :, :], TN))
    w_o_t[...] = spread_o.T.astype(BF16)
    w_o[...] = jnp.where(iota((pad, pad), 0) == SPARE, widen(bo), spread_o).astype(BF16)
    in_wide = widen(in_ref[...].astype(F32))
    out_wide = widen(out_ref[...].astype(F32))
    w_in_t[...] = in_wide.astype(BF16)
    w_in[...] = lengthen(in_wide[:, :width].T, bi).astype(BF16)
    w_out[...] = out_wide.astype(BF16)
    w_out_t[...] = out_wide.T.astype(BF16)

    for ref in (acc_qkv, acc_o, acc_in, acc_out, acc_small, *carried):
        ref[...] = jnp.zeros_like(ref)
    names = ("q_cols", "d_cols", "probs_low", "ds_low", "k_cols", "dq_cols", "hat", "inv")
    names += ("h2", "du", "hid", "df", "o", "da")
    kept = [
        dict(zip(names, carried[side * len(names) : (side + 1) * len(names)]))
        for side in range(2)
    ]

    features = iota((1, pad), 1) < width

    def norm_stats(x):
        mean = jnp.sum(x, -1, keepdims=True) * (1.0 / width)
        centre = jnp.where(features, x - mean, 0.0)
        spread_sq = jnp.sum(centre * centre, -1, keepdims=True) * (1.0 / width)
        inv = lax.rsqrt(spread_sq + NORM_EPS)
        return centre * inv, inv

    def norm_back(scaled, crossed, hat, inv):
        mean_one = jnp.sum(scaled, -1, keepdims=True) * (1.0 / width)
        mean_two = jnp.sum(crossed, -1, keepdims=True) * (1.0 / width)
        return inv * (scaled - mean_one - hat * mean_two)

    def pad_rows(value, size=LANE):
        rows = value.shape[0]
        return jnp.concatenate([value, jnp.zeros((size - rows, value.shape[1]), F32)], axis=0)

    lead = width + 8

    def grouping(n):
        per = 4 if n <= 64 else 2
        groups = HEADS // per
        return per, groups, [(j, group) for j in range(BATCH) for group in range(groups)]

    def tile(group, per):
        first = group * per // 4
        return slice(first * LANE, (first + 1) * LANE)

    def heads(group, per):
        return slice(per * STRIDE * group, per * STRIDE * (group + 1))

    def put_own(ref, j, per, value):
        size = 2 * LANE // per
        value = pad_rows(value, size)
        cols = stack([value] * (LANE // size)).astype(BF16).T
        for head_at in range(HEADS):
            group, i = divmod(head_at, per)
            rows = slice(head_at % 4 * STRIDE, (head_at % 4 + 1) * STRIDE)
            lanes = slice(i * size % LANE, i * size % LANE + size)
            ref[j, group, rows, i * size : (i + 1) * size] = cols[
                head_at * STRIDE : (head_at + 1) * STRIDE, lanes
            ]

    def own_rows(group, per):
        return slice(group * per % 4 * STRIDE, (group * per % 4 + per) * STRIDE)

    def keep_own(ref, j, group, per, product):
        size = 2 * LANE // per
        for i in range(per):
            block = product[i * STRIDE : (i + 1) * STRIDE]
            at = i * size // LANE
            block = block[:, at * LANE : (at + 1) * LANE]
            if i * size % LANE:
                block = pltpu.roll(block, LANE - i * size % LANE, 1)
            ref[j, per * group + i] = block

    def bases(first):
        return [pl.multiple_of(order[first + j] * SLOT, 8) for j in range(BATCH)]

    def stack(values):
        return jnp.concatenate(values, axis=0)

    def front(box, first, n):
        cuts = {40: (0, 40), 72: (0, 40, 72), 104: (0, 32, 64, 104)}[n]
        chunks = [
            (j, lo, hi) for j in range(BATCH) for lo, hi in zip(cuts[:-1], cuts[1:])
        ]
        at = bases(first)
        limits, live = [], []
        for j in range(BATCH):
            s = order[first + j]
            g = group_ref[s]
            limits.append(jnp.where(g == 0, L1, jnp.where(g == 1, L2, L3)))
            live.append(counts_ref[s])

        per, groups, every = grouping(n)

        def keep(j, lo, hi):
            return jnp.where(iota((hi - lo, 1), 0) + lo < limits[j], 1.0, 0.0)

        def rows_of(ref, j, lo, hi):
            return ref[pl.ds(at[j] + lo, hi - lo), :]

        def flat(j, lo, hi):
            return slice(j * n + lo, j * n + hi)

        h1 = []
        for j, lo, hi in chunks:
            hat1, inv1 = norm_stats(rows_of(xrow, j, lo, hi))
            box["hat"][j, lo:hi] = hat1
            box["inv"][j, lo:hi] = inv1
            h1.append(hat1 * g1 + b1)
        yield 0
        qkv = dot(stack(h1).astype(BF16), w_qkv[...])
        yield 4
        for j in range(BATCH):
            rows = slice(j * n, (j + 1) * n)
            put_own(box["q_cols"], j, per, qkv[rows, :pad] * q_scale)
            dead = iota((n, 1), 0) >= live[j]
            k32 = jnp.where(dead & spare_lane, MASK_VALUE, qkv[rows, pad : 2 * pad])
            v32 = qkv[rows, 2 * pad :]
            k_rows[j, :n] = k32.astype(BF16)
            v_rows[j, :n] = v32.astype(BF16)
            box["k_cols"][j] = pad_rows(k32).astype(BF16).T
            v_cols[j] = pad_rows(v32).astype(BF16).T
            yield 0
        for j, group in every:
            scores[j, group, :n] = dot(
                k_rows[j, :n, tile(group, per)], box["q_cols"][j, group]
            )
        yield 2
        for j, group in every:
            score = scores[j, group, :n]
            e = jnp.exp2(score - jnp.max(score, axis=0, keepdims=True))
            p = e * (1.0 / jnp.sum(e, axis=0, keepdims=True))
            probs[j, group, :n] = p
            box["probs_low"][j, group, :n] = p.astype(BF16)
            if group == groups - 1:
                yield 0
        for j, group in every:
            o_t = dot(v_cols[j, heads(group, per), :n], box["probs_low"][j, group, :n])
            keep_own(cols, j, group, per, o_t)
        yield 2
        mixed = stack([cols[j].reshape(pad, LANE).T[:n] for j in range(BATCH)])
        o = jnp.where(iota((1, pad), 1) == SPARE, 1.0, mixed).astype(BF16)
        box["o"][: BATCH * n] = o
        yield 0
        a = dot(o, w_o[...])
        yield 4
        y1, hat2, inv2, h2 = [], [], [], []
        for c in chunks:
            y = rows_of(xrow, *c) + keep(*c) * a[flat(*c)]
            hat, inv = norm_stats(y)
            y1.append(y)
            hat2.append(hat)
            inv2.append(inv)
            h2.append(hat * g2 + b2)
        h2 = stack(h2).astype(BF16)
        box["h2"][: BATCH * n] = h2
        yield 0
        u = dot(h2, w_in[...])
        df = stack([keep(*c) * rows_of(crow, *c) for c in chunks])
        df_low = df.astype(BF16)
        box["df"][: BATCH * n] = df_low
        acc_small[0:8, :] += partial_sums(df)
        dhid = dot(df_low, w_out_t[...])
        yield 3
        hid, du = [], []
        alpha, beta = 0.7978845608028654, 0.044715
        for c in chunks:
            z, up = u[flat(*c), :hidden], u[flat(*c), hidden:]
            dh = dhid[flat(*c)]
            inner = alpha + (alpha * beta) * (z * z)
            gate = 0.5 + 0.5 * jnp.tanh(z * inner)
            act = z * gate
            slope = gate + (act * (1.0 - gate)) * (6.0 * inner - 4.0 * alpha)
            hid.append(act * up)
            du.append(jnp.concatenate([dh * up * slope, dh * act], axis=1))
            if c[1] == 0:
                yield 0
        hid = stack(hid).astype(BF16)
        box["hid"][: BATCH * n] = hid
        du = stack(du).astype(BF16)
        box["du"][: BATCH * n] = du
        yield 0
        f = dot(hid, w_out[...])
        dh2 = dot(du, w_in_t[...])
        yield 3
        da = []
        gain = jnp.zeros((8, pad), F32)
        for i, c in enumerate(chunks):
            j, lo, hi = c
            xrow[pl.ds(at[j] + lo, hi - lo), :] = y1[i] + keep(*c) * (f[flat(*c)] + bf)
            grad = dh2[flat(*c)]
            crossed = grad * hat2[i]
            gain += partial_sums(crossed)
            dy1 = rows_of(crow, *c) + norm_back(grad * g2, crossed * g2, hat2[i], inv2[i])
            crow[pl.ds(at[j] + lo, hi - lo), :] = dy1
            da.append(keep(*c) * dy1)
        acc_small[8:16, :] += gain
        da = stack(da).astype(BF16)
        box["da"][: BATCH * n] = da
        yield 0
        do = dot(da, w_o_t[...])
        yield 4
        for j in range(BATCH):
            put_own(box["d_cols"], j, per, do[j * n : (j + 1) * n])
        yield 0
        for j, group in every:
            scores[j, group, :n] = dot(
                v_rows[j, :n, tile(group, per)], box["d_cols"][j, group]
            )
        yield 4
        for j, group in every:
            dp = scores[j, group, :n]
            p = probs[j, group, :n]
            box["ds_low"][j, group, :n] = (
                p * (dp - jnp.sum(dp * p, axis=0, keepdims=True))
            ).astype(BF16)
            if group == groups - 1:
                yield 0

    def back(box, first, n, layout):
        per, groups, every = grouping(layout)
        rows = slice(0, BATCH * n)
        at = bases(first)
        for j, group in every:
            dq_t = dot(box["k_cols"][j, heads(group, per), :n], box["ds_low"][j, group, :n])
            keep_own(box["dq_cols"], j, group, per, dq_t)
            if group == groups - 1:
                yield
        parts = []
        for j in range(BATCH):
            dv_t, dk_t = [], []
            for group in range(groups):
                own = own_rows(group, per)
                dv_t.append(
                    dot(box["d_cols"][j, group, own], box["probs_low"][j, group, :n], NT)
                )
            yield
            for group in range(groups):
                own = own_rows(group, per)
                dk_t.append(dot(box["q_cols"][j, group, own], box["ds_low"][j, group, :n], NT))
            dq = (box["dq_cols"][j].reshape(pad, LANE) * scale).astype(BF16).T[:n]
            dk = (stack(dk_t) * (1.0 / log2e)).astype(BF16).T
            parts.append(jnp.concatenate([dq, dk, stack(dv_t).astype(BF16).T], axis=1))
            yield
        dqkv = stack(parts)
        dh1 = dot(dqkv, w_qkv_t[...])
        yield
        acc_out[...] += dot(box["df"][rows, :width], box["hid"][rows], TN)
        yield
        acc_o[...] += dot(box["da"][rows, :width], box["o"][rows], TN)
        yield
        h2 = box["h2"][rows, :lead]
        for part in range(2 * hidden // pad):
            lanes = slice(part * pad, (part + 1) * pad)
            acc_in[:, lanes] += dot(h2, box["du"][rows, lanes], TN)
            yield
        h1 = []
        gain = jnp.zeros((8, pad), F32)
        for j in range(BATCH):
            hat = box["hat"][j, :n]
            grad = dh1[j * n : (j + 1) * n]
            crossed = grad * hat
            gain += partial_sums(crossed)
            crow[pl.ds(at[j], n), :] += norm_back(
                grad * g1, crossed * g1, hat, box["inv"][j, :n]
            )
            h1.append(hat * g1 + b1)
            if j % 2:
                yield
        acc_small[16:24, :] += gain
        h1 = stack(h1).astype(BF16)[:, :lead]
        for part in range(3):
            lanes = slice(part * pad, (part + 1) * pad)
            acc_qkv[:, lanes] += dot(h1, dqkv[:, lanes], TN)
            yield

    def together(fill, main):
        for steps_of in main:
            for _ in range(steps_of):
                next(fill, None)
        for _ in fill:
            pass

    def double(step, n):
        even = step * 2 * BATCH
        before = jnp.maximum(even - BATCH, 0)
        together(back(kept[1], before, n, n), front(kept[0], even, n))
        together(back(kept[0], even, n, n), front(kept[1], even + BATCH, n))

    lengths = (40, 72, 104)
    def kind_of(step):
        return group_ref[order[(step + 1) * 2 * BATCH - 1]]

    def finish_short(step):
        together(back(kept[1], step * 2 * BATCH - BATCH, 40, 40), iter(()))
        for name in ("ds_low", "du", "df", "da"):
            kept[1][name][...] = jnp.zeros_like(kept[1][name])
        for box in kept:
            for name in ("q_cols", "d_cols"):
                box[name][...] = jnp.zeros_like(box[name])

    def one_step(step, carry):
        kind = kind_of(jnp.minimum(step, steps - 1))
        last = kind_of(jnp.maximum(step - 1, 0))
        pl.when((step > 0) & (last == 0) & ((step == steps) | (kind != 0)))(
            functools.partial(finish_short, step)
        )
        pl.when(step < steps)(lambda: fetched(step))
        pl.when(step + 2 < steps)(lambda: fetch(step + 2))
        for member, n in enumerate(lengths):
            pl.when((step < steps) & (kind == member))(functools.partial(double, step, n))
        return carry

    lax.fori_loop(0, steps + 1, one_step, 0)

    cut = 4 * LANE

    def col_copies(part):
        lanes = pl.ds(pl.multiple_of(part * cut, cut), cut)
        return [
            pltpu.make_async_copy(held.at[:, lanes], ref.at[:, lanes], col_sem.at[i, part])
            for i, (held, ref) in enumerate(((y_cols, y_ref), (dx_cols, dx_ref)))
        ]

    def fold_y():
        for part in range(rows_all // cut):
            for member in range(4):
                at = slice(part * cut + member * LANE, part * cut + (member + 1) * LANE)
                y_cols[:, at] = xrow[at, :width].astype(BF16).T
                yield
            col_copies(part)[0].start()

    folding = fold_y()
    for _ in back(kept[1], samples - BATCH, SLOT, SLOT):
        for _ in range(3):
            next(folding, None)
    for _ in folding:
        pass

    def fold_dx(part, carry):
        for member in range(4):
            at = pl.multiple_of(part * cut + member * LANE, LANE)
            dx_cols[:, pl.ds(at, LANE)] = crow[pl.ds(at, LANE), :width].T
        col_copies(part)[1].start()
        return carry

    lax.fori_loop(0, rows_all // cut, fold_dx, 0)

    def gather_heads(value):
        return lax.dot_general(
            value, spread.astype(F32), NT, precision=lax.Precision.HIGHEST,
            preferred_element_type=F32,
        )

    for member in range(3):
        g_attn_ref[member * width : (member + 1) * width, :] = gather_heads(
            acc_qkv[:width, member * pad : (member + 1) * pad]
        )
    g_attn_ref[3 * width :, :] = lax.dot_general(
        spread.astype(F32), acc_o[...], NT, precision=lax.Precision.HIGHEST,
        preferred_element_type=F32,
    )
    g_in_ref[...] = acc_in[:width, :].T
    g_out_ref[...] = acc_out[...].T

    def small(member):
        block = acc_small[8 * member : 8 * member + 8, :width]
        return jnp.sum(block, axis=0, keepdims=True)

    def exact(a, b):
        return lax.dot_general(
            a, b.astype(F32), NN, precision=lax.Precision.HIGHEST, preferred_element_type=F32
        )[0:1]

    qkv_sums = acc_qkv[width : width + 8, :]
    in_sums = acc_in[width : width + 8, :]
    g_b1 = exact(qkv_sums, w_qkv_t[...])[:, :width]
    g_b2 = exact(in_sums, w_in_t[...])[:, :width]
    g_bq = gather_heads(qkv_sums[:, :pad])[0:1]
    g_bv = gather_heads(qkv_sums[:, 2 * pad :])[0:1]
    g_bo = acc_o[...].T[SPARE : SPARE + 1]
    flat = jnp.concatenate(
        [small(2), g_b1, small(1), g_b2, g_bq, g_bv, g_bo, small(0), in_sums[0:1]], axis=1
    )
    for row in range(16):
        g_vec_ref[row] = flat[:, row * LANE : (row + 1) * LANE]

    def folded(part, carry):
        for copy in col_copies(part):
            copy.wait()
        return carry

    lax.fori_loop(0, rows_all // cut, folded, 0)


def layer(group, counts, order, x_rows, c_rows, attn, ffn_in, ffn_out, vec):
    rows, width = x_rows.shape[0], attn.shape[1]
    hidden = ffn_out.shape[0]
    pad = HEADS * STRIDE
    vmem = pl.BlockSpec(memory_space=pltpu.VMEM)
    smem = pl.BlockSpec(memory_space=pltpu.SMEM)
    whole = pl.BlockSpec(memory_space=pl.ANY)
    return pl.pallas_call(
        layer_kernel,
        name="layer",
        out_shape=(
            jax.ShapeDtypeStruct((width, rows), BF16),
            jax.ShapeDtypeStruct((width, rows), F32),
            jax.ShapeDtypeStruct((4 * width, width), F32),
            jax.ShapeDtypeStruct((2 * hidden, width), F32),
            jax.ShapeDtypeStruct((hidden, width), F32),
            jax.ShapeDtypeStruct((16, 1, LANE), F32),
        ),
        in_specs=[smem] * 3 + [whole] * 2 + [vmem] * 4,
        out_specs=[whole] * 2 + [vmem] * 4,
        scratch_shapes=[
            pltpu.VMEM((rows, pad), F32),
            pltpu.VMEM((rows, pad), F32),
            pltpu.VMEM((width, rows), BF16),
            pltpu.VMEM((width, rows), F32),
            pltpu.SemaphoreType.DMA((group.shape[0] // (2 * BATCH),)),
            pltpu.SemaphoreType.DMA((2, rows // (4 * LANE))),
            pltpu.VMEM((pad, 3 * pad), BF16),
            pltpu.VMEM((3 * pad, pad), BF16),
            pltpu.VMEM((pad, pad), BF16),
            pltpu.VMEM((pad, pad), BF16),
            pltpu.VMEM((pad, 2 * hidden), BF16),
            pltpu.VMEM((2 * hidden, pad), BF16),
            pltpu.VMEM((hidden, pad), BF16),
            pltpu.VMEM((pad, hidden), BF16),
            pltpu.VMEM((BATCH, HEADS // 2, SLOT, 2 * LANE), F32),
            pltpu.VMEM((BATCH, HEADS // 2, SLOT, 2 * LANE), F32),
            pltpu.VMEM((BATCH, SLOT, pad), BF16),
            pltpu.VMEM((BATCH, SLOT, pad), BF16),
            pltpu.VMEM((BATCH, pad, LANE), BF16),
            pltpu.VMEM((BATCH, HEADS, STRIDE, LANE), F32),
            pltpu.VMEM((width + 8, 3 * pad), F32),
            pltpu.VMEM((width, pad), F32),
            pltpu.VMEM((width + 8, 2 * hidden), F32),
            pltpu.VMEM((width, hidden), F32),
            pltpu.VMEM((24, pad), F32),
        ]
        + [
            pltpu.VMEM((BATCH, HEADS // 2, LANE, 2 * LANE), BF16),
            pltpu.VMEM((BATCH, HEADS // 2, LANE, 2 * LANE), BF16),
            pltpu.VMEM((BATCH, HEADS // 2, SLOT, 2 * LANE), BF16),
            pltpu.VMEM((BATCH, HEADS // 2, SLOT, 2 * LANE), BF16),
            pltpu.VMEM((BATCH, pad, LANE), BF16),
            pltpu.VMEM((BATCH, HEADS, STRIDE, LANE), F32),
            pltpu.VMEM((BATCH, SLOT, pad), F32),
            pltpu.VMEM((BATCH, SLOT, 1), F32),
            pltpu.VMEM((BATCH * SLOT, pad), BF16),
            pltpu.VMEM((BATCH * SLOT, 2 * hidden), BF16),
            pltpu.VMEM((BATCH * SLOT, hidden), BF16),
            pltpu.VMEM((BATCH * SLOT, pad), BF16),
            pltpu.VMEM((BATCH * SLOT, pad), BF16),
            pltpu.VMEM((BATCH * SLOT, pad), BF16),
        ]
        * 2,
        compiler_params=pltpu.CompilerParams(vmem_limit_bytes=60 * 2**20),
    )(group, counts, order, x_rows, c_rows, attn, ffn_in, ffn_out, vec)


class Place:
    def __init__(self, size):
        side = 1
        while 2 * (2 * side) ** 3 <= size:
            side *= 2
        self.size, self.spots = size, side * side
        self.layers = size // self.spots
        me, self.core = lax.axis_index("wide"), lax.axis_index("narrow")
        self.me = me
        self.layer, self.spot = me // self.spots, lax.rem(me, self.spots)

    def at(self, layer, spot):
        layer = lax.rem(self.layer + layer + self.layers, self.layers)
        return layer * self.spots + lax.rem(self.spot + spot + self.spots, self.spots)

    def signal(self):
        barrier = pltpu.get_barrier_semaphore()

        def tell(index, core):
            pl.semaphore_signal(
                barrier, inc=1, device_id=(index, core), device_id_type=MESH
            )

        over(1, self.layers, lambda k: tell(self.at(k, 0), self.core))
        over(1, self.spots, lambda k: tell(self.at(0, k), self.core))
        tell(self.me, 1 - self.core)

    def wait(self):
        pl.semaphore_wait(
            pltpu.get_barrier_semaphore(), self.layers + self.spots - 1
        )


def over(low, high, body):
    def step(k, carry):
        body(k)
        return carry

    lax.fori_loop(low, high, step, 0)


def packed_rows(share):
    return (share + share // 2 + 1 + 15) // 16 * 16


def pack(value, vec):
    share, width = value.shape
    tail = value[:, LANE:]
    tail = jnp.concatenate([tail[: share // 2], tail[share // 2 :]], axis=1)
    if vec.shape[1] < LANE:
        vec = jnp.concatenate([vec, jnp.zeros((1, LANE - vec.shape[1]), F32)], axis=1)
    rest = packed_rows(share) - share - share // 2 - 1
    return jnp.concatenate([value[:, :LANE], tail, vec, jnp.zeros((rest, LANE), F32)], axis=0)


def unpack(block, share):
    at = share + share // 2
    tail = block[share:at]
    tail = jnp.concatenate([tail[:, : LANE // 2], tail[:, LANE // 2 :]], axis=0)
    return jnp.concatenate([block[:share], tail], axis=1), block[at : at + 1]


def gather_kernel(
    group_ref, attn_ref, in_ref, out_ref, vec_ref, tok_hbm, cot_hbm,
    attn_all, in_all, out_all, vec_all, order_ref, x_hbm, c_hbm,
    blocks, tok, cot, xrow, crow, in_sem, row_sem, send_sem, recv_sem, pass_sem, got_sem,
):
    size = attn_all.shape[0]
    share, width = attn_ref.shape
    split = in_ref.shape[0]
    place = Place(size)
    me, core, layers, spots = place.me, place.core, place.layers, place.spots
    cut = 4 * LANE
    parts = tok_hbm.shape[1] // cut
    pad = xrow.shape[1]

    def lanes(part):
        return pl.ds(pl.multiple_of(part * cut, cut), cut)

    def col_copies(part):
        return [
            pltpu.make_async_copy(ref.at[:, lanes(part)], held.at[:, lanes(part)], in_sem.at[i, part])
            for i, (ref, held) in enumerate(((tok_hbm, tok), (cot_hbm, cot)))
        ]

    def row_copies(part):
        return [
            pltpu.make_async_copy(held.at[lanes(part)], ref.at[lanes(part)], row_sem.at[i, part])
            for i, (held, ref) in enumerate(((xrow, x_hbm), (crow, c_hbm)))
        ]

    place.signal()

    def begin(part):
        for copy in col_copies(part):
            copy.start()

    over(0, parts, begin)
    vec = vec_ref[...]
    blocks[0, me] = pack(attn_ref[...], vec).astype(BF16)
    both = jnp.concatenate([in_ref[...], out_ref[...]], axis=0)
    blocks[1, me] = pack(both, vec).astype(BF16)
    place.wait()

    def to_peer(owner, target, slot):
        return pltpu.make_async_remote_copy(
            src_ref=blocks.at[core, owner],
            dst_ref=blocks.at[core, owner],
            send_sem=send_sem.at[slot],
            recv_sem=recv_sem.at[owner],
            device_id=(target, core),
            device_id_type=MESH,
        )

    def to_twin(owner, whose):
        return pltpu.make_async_remote_copy(
            src_ref=blocks.at[whose, owner],
            dst_ref=blocks.at[whose, owner],
            send_sem=pass_sem.at[owner],
            recv_sem=got_sem.at[owner],
            device_id=(me, 1 - core),
            device_id_type=MESH,
        )

    def along(k):
        return to_peer(me, place.at(k, 0), layers * (spots - 1) + k - 1)

    def within(layer, k):
        owner = place.at(-layer, 0)
        return to_peer(owner, place.at(0, k), layer * (spots - 1) + k - 1)

    over(1, layers, lambda k: along(k).start())
    over(1, spots, lambda k: within(0, k).start())

    samples = group_ref.shape[1]
    key = group_ref[...] * samples + iota((1, samples), 1)
    wide = jnp.broadcast_to(key.astype(F32), (samples, samples))
    rank = jnp.sum(jnp.where(wide < wide.T, 1.0, 0.0), axis=1, keepdims=True)
    here = rank == iota((samples, samples), 1).astype(F32)
    found = jnp.where(here, iota((samples, samples), 0).astype(F32), 0.0)
    order_ref[...] = jnp.sum(found, axis=0, keepdims=True).astype(jnp.int32)

    zero = jnp.zeros((LANE, pad - width), F32)

    def unfold(part):
        for copy in col_copies(part):
            copy.wait()
        for member in range(4):
            at = pl.multiple_of(part * cut + member * LANE, LANE)
            for held, rows in ((tok, xrow), (cot, crow)):
                value = held[:, pl.ds(at, LANE)].T.astype(F32)
                rows[pl.ds(at, LANE), :] = jnp.concatenate([value, zero], axis=1)
        for copy in row_copies(part):
            copy.start()

    def arrived(owner):
        to_peer(owner, me, 0).wait_recv()
        to_twin(owner, core).start()

    def forward(layer):
        to_peer(place.at(-layer, 0), me, 0).wait_recv()
        over(1, spots, lambda k: within(layer, k).start())
        to_twin(place.at(-layer, 0), core).start()

    early = min(3, parts)
    over(0, early, unfold)
    over(1, layers, forward)
    over(early, parts, unfold)
    over(1, spots, lambda k: over(0, layers, lambda layer: arrived(place.at(-layer, -k))))

    def end(part):
        for copy in row_copies(part):
            copy.wait()

    def spread_out(owner):
        value, last = unpack(blocks[0, owner].astype(F32), share)
        attn_all[owner] = value.astype(BF16)
        vec_all[owner] = last[:, : vec_all.shape[2]]
        value, _ = unpack(blocks[1, owner].astype(F32), share)
        in_all[owner] = value[:split].astype(BF16)
        out_all[owner] = value[split:].astype(BF16)

    def finish(layer, k):
        owner = place.at(-layer, -k)
        to_twin(owner, 1 - core).wait_recv()
        spread_out(owner)

    spread_out(me)
    over(1, layers, lambda layer: finish(layer, 0))
    over(1, spots, lambda k: over(0, layers, lambda layer: finish(layer, k)))
    over(1, layers, lambda k: along(k).wait_send())
    over(0, layers, lambda layer: over(1, spots, lambda k: within(layer, k).wait_send()))
    over(1, size, lambda k: to_twin(lax.rem(me + k, size), core).wait_send())
    over(0, parts, end)


def gather(size, group, attn, ffn_in, ffn_out, vec, tokens_t, cotangent_t):
    vmem = pl.BlockSpec(memory_space=pltpu.VMEM)
    whole = pl.BlockSpec(memory_space=pl.ANY)
    width, rows = tokens_t.shape
    pad = HEADS * STRIDE
    parts = rows // (4 * LANE)
    return pl.pallas_call(
        gather_kernel,
        name="gather",
        out_shape=tuple(
            jax.ShapeDtypeStruct((size, *value.shape), BF16)
            for value in (attn, ffn_in, ffn_out)
        )
        + (
            jax.ShapeDtypeStruct((size, *vec.shape), F32),
            jax.ShapeDtypeStruct(group.shape, jnp.int32),
            jax.ShapeDtypeStruct((rows, pad), F32),
            jax.ShapeDtypeStruct((rows, pad), F32),
        ),
        in_specs=[vmem] * 5 + [whole] * 2,
        out_specs=[vmem] * 5 + [whole] * 2,
        scratch_shapes=[
            pltpu.VMEM((2, size, packed_rows(attn.shape[0]), LANE), BF16),
            pltpu.VMEM((width, rows), BF16),
            pltpu.VMEM((width, rows), BF16),
            pltpu.VMEM((rows, pad), F32),
            pltpu.VMEM((rows, pad), F32),
            pltpu.SemaphoreType.DMA((2, parts)),
            pltpu.SemaphoreType.DMA((2, parts)),
        ]
        + [pltpu.SemaphoreType.DMA((size,))] * 4,
        compiler_params=pltpu.CompilerParams(
            collective_id=0, has_side_effects=True, vmem_limit_bytes=60 * 2**20
        ),
    )(group, attn, ffn_in, ffn_out, vec, tokens_t, cotangent_t)


def reduce_kernel(
    g_attn, g_in, g_out, g_vec,
    s_attn, s_in, s_out, s_vec,
    own, stage, twin, chip, near, relay, far, total,
    pass_sem, got_sem, near_send, near_recv, far_send, far_recv, last_sem,
):
    size, share = g_attn.shape[:2]
    split = g_in.shape[1]
    place = Place(size)
    me, core, layers, spots = place.me, place.core, place.layers, place.spots
    place.signal()

    def prepare(owner):
        own[0, owner] = pack(g_attn[owner], g_vec[owner])
        both = jnp.concatenate([g_in[owner], g_out[owner]], axis=0)
        own[1, owner] = pack(both, jnp.zeros((1, LANE), F32))
        stage[owner] = own[1 - core, owner].astype(BF16)

    over(0, size, prepare)
    place.wait()

    def to_twin(owner):
        return pltpu.make_async_remote_copy(
            src_ref=stage.at[owner],
            dst_ref=twin.at[owner],
            send_sem=pass_sem.at[owner],
            recv_sem=got_sem.at[owner],
            device_id=(me, 1 - core),
            device_id_type=MESH,
        )

    def within(layer, k, spot, owner_layer):
        owner = place.at(layer, k)
        slot = spot * layers + owner_layer
        return pltpu.make_async_remote_copy(
            src_ref=chip.at[owner],
            dst_ref=near.at[slot],
            send_sem=near_send.at[owner],
            recv_sem=near_recv.at[slot],
            device_id=(place.at(0, k), core),
            device_id_type=MESH,
        )

    def along(layer, sender):
        target = lax.rem(place.layer + layer, layers)
        return pltpu.make_async_remote_copy(
            src_ref=relay.at[target],
            dst_ref=far.at[sender],
            send_sem=far_send.at[target],
            recv_sem=far_recv.at[sender],
            device_id=(place.at(layer, 0), core),
            device_id_type=MESH,
        )

    def result(whose):
        return pltpu.make_async_remote_copy(
            src_ref=total.at[whose],
            dst_ref=total.at[whose],
            send_sem=last_sem.at[0],
            recv_sem=last_sem.at[1],
            device_id=(me, 1 - core),
            device_id_type=MESH,
        )

    def layer_of(layer):
        return lax.rem(place.layer + layer, layers)

    def send(k, layer):
        owner = place.at(layer, k)
        to_twin(owner).wait_recv()
        chip[owner] = (own[core, owner] + twin[owner].astype(F32)).astype(BF16)
        within(layer, k, place.spot, layer_of(layer)).start()

    def spot_sum(layer):
        owner = place.at(layer, 0)
        to_twin(owner).wait_recv()
        total[core] = own[core, owner] + twin[owner].astype(F32)

        def add(k):
            spot = lax.rem(place.spot + k, spots)
            within(layer, k, spot, layer_of(layer)).wait_recv()
            total[core] += near[spot * layers + layer_of(layer)].astype(F32)

        over(1, spots, add)

    def pass_on(layer):
        spot_sum(layer)
        relay[layer_of(layer)] = total[core].astype(BF16)
        along(layer, place.layer).start()

    def take(layer):
        sender = layer_of(layer)
        along(layer, sender).wait_recv()
        total[core] += far[sender].astype(F32)

    over(1, spots, lambda k: over(1, layers, lambda layer: to_twin(place.at(layer, k)).start()))
    over(1, layers, lambda layer: to_twin(place.at(layer, 0)).start())
    over(0, spots, lambda k: to_twin(place.at(0, k)).start())
    over(1, spots, lambda k: over(1, layers, lambda layer: send(k, layer)))
    over(1, spots, lambda k: send(k, 0))
    over(1, layers, pass_on)
    spot_sum(0)
    over(1, layers, take)
    result(core).start()
    over(1, spots, lambda k: over(
        0, layers, lambda layer: within(layer, k, place.spot, layer_of(layer)).wait_send()
    ))
    over(1, layers, lambda layer: along(layer, place.layer).wait_send())
    over(0, size, lambda owner: to_twin(owner).wait_send())
    result(core).wait_send()
    result(1 - core).wait_recv()
    value, last = unpack(total[0], share)
    s_attn[...] = value
    s_vec[...] = last[:, : s_vec.shape[1]]
    value, _ = unpack(total[1], share)
    s_in[...] = value[:split]
    s_out[...] = value[split:]


def reduce_scatter(g_attn, g_in, g_out, g_vec):
    grads = (g_attn, g_in, g_out, g_vec)
    size, share = g_attn.shape[:2]
    vmem = pl.BlockSpec(memory_space=pltpu.VMEM)
    block = (packed_rows(share), LANE)
    return pl.pallas_call(
        reduce_kernel,
        name="reduce",
        out_shape=tuple(jax.ShapeDtypeStruct(value.shape[1:], F32) for value in grads),
        in_specs=[vmem] * 4,
        out_specs=[vmem] * 4,
        scratch_shapes=[pltpu.VMEM((2, size, *block), F32)]
        + [pltpu.VMEM((size, *block), BF16)] * 6
        + [pltpu.VMEM((2, *block), F32)]
        + [pltpu.SemaphoreType.DMA((size,))] * 6
        + [pltpu.SemaphoreType.DMA((2,))],
        compiler_params=pltpu.CompilerParams(
            collective_id=1, has_side_effects=True, vmem_limit_bytes=60 * 2**20
        ),
    )(*grads)


def adamw_kernel(*refs):
    for member in range(4):
        master, first, second, grad = (refs[4 * kind + member][...] for kind in range(4))
        results = adamw_update(master, grad, first, second)
        for kind in range(3):
            refs[16 + 3 * member + kind][...] = results[kind]


def adamw(masters, firsts, seconds, grads):
    vmem = pl.BlockSpec(memory_space=pltpu.VMEM)
    return pl.pallas_call(
        adamw_kernel,
        name="adamw",
        out_shape=tuple(
            jax.ShapeDtypeStruct(value.shape, F32) for value in masters for kind in range(3)
        ),
        in_specs=[vmem] * 16,
        out_specs=[vmem] * 12,
        compiler_params=pltpu.CompilerParams(vmem_limit_bytes=60 * 2**20),
    )(*masters, *firsts, *seconds, *grads)


def local(
    tokens,
    cotangent,
    group,
    counts,
    attn_w,
    ffn_in,
    ffn_out,
    vectors,
    attn_m,
    attn_v,
    in_m,
    in_v,
    out_m,
    out_v,
    vec_m,
    vec_v,
):
    size = lax.axis_size("wide")
    width = tokens.shape[1]
    masters = (attn_w, ffn_in, ffn_out, vectors[None])
    attn, into, outof, vec, order, x_rows, c_rows = gather(
        size, group[None], *masters, tokens.T, cotangent.T
    )
    out_t, grad_t, *grads = layer(
        group,
        counts,
        order[0],
        x_rows,
        c_rows,
        attn.reshape(-1, width),
        into.reshape(-1, width),
        outof.reshape(-1, width),
        vec.reshape(-1, 1, LANE),
    )
    sums = reduce_scatter(
        *[g.reshape(size, -1, width) for g in grads[:3]], grads[3].reshape(size, 1, -1)
    )
    results = adamw(
        masters, (attn_m, in_m, out_m, vec_m[None]), (attn_v, in_v, out_v, vec_v[None]), sums
    )
    return (out_t.T, grad_t.T, *results[:9], *[value[0] for value in results[9:]])


def solution(mesh):
    rows = P(("wide", "narrow"), None)
    samples = P(("wide", "narrow"))
    weight = P("wide", None)
    vector = P("wide")
    return jax.shard_map(
        local,
        mesh=mesh,
        in_specs=(rows, rows, samples, samples, weight, weight, weight, vector)
        + (weight,) * 6
        + (vector,) * 2,
        out_specs=(rows, rows) + (weight,) * 9 + (vector,) * 3,
        check_vma=False,
    )
```

```python
import functools
import math

import jax
import jax.numpy as jnp
from jax import lax
from jax.experimental import pallas as pl
from jax.experimental.pallas import tpu as pltpu
from jax.sharding import PartitionSpec as P

HEADS = 8
SLOT = 104
L1 = 40
L2 = 68
L3 = 100
STEP = 10

NORM_EPS = 1e-05
BETA_ONE = 0.9
BETA_TWO = 0.999
ADAM_EPS = 1e-08
LEARN_RATE = 0.1
WEIGHT_DECAY = 0.01
MASK_VALUE = -1e30

F32 = jnp.float32
BF16 = jnp.bfloat16
LANE = 128
MESH = pl.DeviceIdType.MESH
STRIDE = 32
NN = (((1,), (0,)), ((), ()))
NT = (((1,), (1,)), ((), ()))
TN = (((0,), (0,)), ((), ()))
BATCH = 4
SPARE = 24
FILL = {
    40: (5, 1, 1, 5, 4, 4, 3, 4),
    72: (4, 2, 2, 4, 3, 4, 4, 3),
    104: (4, 2, 2, 5, 3, 3, 5, 2),
}
EARLY_D = {40: True, 72: False, 104: True}


def adamw_update(master, gradient, moment, square):
    moment_new = BETA_ONE * moment + (1.0 - BETA_ONE) * gradient
    square_new = BETA_TWO * square + (1.0 - BETA_TWO) * gradient * gradient
    moment_hat = moment_new / (1.0 - BETA_ONE**STEP)
    square_hat = square_new / (1.0 - BETA_TWO**STEP)
    master_new = master - LEARN_RATE * (
        moment_hat / (jnp.sqrt(square_hat) + ADAM_EPS) + WEIGHT_DECAY * master
    )
    return (master_new, moment_new, square_new)


def dot(a, b, dims=NN):
    return lax.dot_general(a, b, dims, preferred_element_type=F32)


def iota(shape, dim):
    return lax.broadcasted_iota(jnp.int32, shape, dim)


def partial_sums(value):
    rows, cols = value.shape
    return jnp.sum(value.reshape(rows // 8, 8, cols), axis=0)


def piece(vec, member, width):
    start = member * width
    parts, at = [], start
    while at < start + width:
        row, lane = divmod(at, LANE)
        take = min(LANE - lane, start + width - at)
        parts.append(vec[row : row + 1, lane : lane + take])
        at += take
    return jnp.concatenate(parts, axis=1)


def layer_kernel(
    group_ref,
    counts_ref,
    order,
    x_hbm,
    c_hbm,
    attn_ref,
    in_ref,
    out_ref,
    vec_ref,
    y_ref,
    dx_ref,
    g_attn_ref,
    g_in_ref,
    g_out_ref,
    g_vec_ref,
    xrow,
    crow,
    y_cols,
    dx_cols,
    row_sem,
    col_sem,
    w_qkv,
    w_qkv_t,
    w_o,
    w_o_t,
    w_in,
    w_in_t,
    w_out,
    w_out_t,
    probs,
    scores,
    k_rows,
    v_rows,
    v_cols,
    cols,
    acc_qkv,
    acc_o,
    acc_in,
    acc_out,
    acc_small,
    *carried,
):
    width = attn_ref.shape[1]
    hidden = out_ref.shape[0]
    samples = group_ref.shape[0]
    rows_all = x_hbm.shape[0]
    head = width // HEADS
    pad = HEADS * STRIDE
    scale = 1.0 / math.sqrt(head)
    log2e = math.log2(math.e)
    q_scale = scale * log2e

    steps = samples // (2 * BATCH)

    def fetch(step):
        for j in range(2 * BATCH):
            rows = pl.ds(pl.multiple_of(order[step * 2 * BATCH + j] * SLOT, 8), SLOT)
            for ref, held in ((x_hbm, xrow), (c_hbm, crow)):
                pltpu.make_async_copy(ref.at[rows], held.at[rows], row_sem.at[step]).start()

    def fetched(step):
        rows = pl.ds(0, 2 * BATCH * SLOT)
        for ref, held in ((x_hbm, xrow), (c_hbm, crow)):
            pltpu.make_async_copy(ref.at[rows], held.at[rows], row_sem.at[step]).wait()

    fetch(0)
    fetch(1)

    spread_row = iota((width, pad), 0)
    spread_col = iota((width, pad), 1)
    within = spread_col & (STRIDE - 1)
    spread = jnp.where(
        (within < head) & (spread_row == (spread_col >> 5) * head + within), 1.0, 0.0
    ).astype(BF16)
    vec = jnp.concatenate([vec_ref[row] for row in range(vec_ref.shape[0])], axis=0)
    bi = jnp.concatenate([vec[row : row + 1] for row in range(12, 16)], axis=1)

    def widen(value, fill=0.0):
        rows = value.shape[0]
        tail = jnp.where(iota((rows, pad - width), 1) == 0, fill, 0.0)
        return jnp.concatenate([value, tail], axis=1)

    def lengthen(value, row=None):
        cols = value.shape[1]
        if row is None:
            row = jnp.zeros((1, cols), F32)
        tail = jnp.concatenate([row, jnp.zeros((pad - width - 1, cols), F32)], axis=0)
        return jnp.concatenate([value, tail], axis=0)

    g1, b1, g2, b2, bq, bv, bo, bf = (piece(vec, member, width) for member in range(8))
    g1, b1, g2, b2 = widen(g1), widen(b1, 1.0), widen(g2), widen(b2, 1.0)
    bf = widen(bf)
    spare_lane = (iota((1, pad), 1) & (STRIDE - 1)) == SPARE
    for member in range(3):
        spread_w = dot(attn_ref[member * width : (member + 1) * width, :], spread)
        if member == 0:
            bias = dot(bq.astype(BF16), spread) + jnp.where(spare_lane, 1.0, 0.0)
        elif member == 1:
            bias = None
        else:
            bias = dot(bv.astype(BF16), spread)
        w_qkv[:, member * pad : (member + 1) * pad] = lengthen(spread_w, bias).astype(BF16)
        w_qkv_t[member * pad : (member + 1) * pad, :] = widen(spread_w.T).astype(BF16)
    spread_o = widen(dot(spread, attn_ref[3 * width :, :], TN))
    w_o_t[...] = spread_o.T.astype(BF16)
    w_o[...] = jnp.where(iota((pad, pad), 0) == SPARE, widen(bo), spread_o).astype(BF16)
    in_wide = widen(in_ref[...].astype(F32))
    out_wide = widen(out_ref[...].astype(F32))
    w_in_t[...] = in_wide.astype(BF16)
    w_in[...] = lengthen(in_wide[:, :width].T, bi).astype(BF16)
    w_out[...] = out_wide.astype(BF16)
    w_out_t[...] = out_wide.T.astype(BF16)

    for ref in (acc_qkv, acc_o, acc_in, acc_out, acc_small, *carried):
        ref[...] = jnp.zeros_like(ref)
    names = ("q_cols", "d_cols", "probs_low", "ds_low", "k_cols", "dq_cols", "hat", "inv")
    names += ("h2", "du", "hid", "df", "o", "da")
    kept = [
        dict(zip(names, carried[side * len(names) : (side + 1) * len(names)]))
        for side in range(2)
    ]

    features = iota((1, pad), 1) < width

    def norm_stats(x):
        mean = jnp.sum(x, -1, keepdims=True) * (1.0 / width)
        centre = jnp.where(features, x - mean, 0.0)
        spread_sq = jnp.sum(centre * centre, -1, keepdims=True) * (1.0 / width)
        inv = lax.rsqrt(spread_sq + NORM_EPS)
        return centre * inv, inv

    def norm_back(scaled, crossed, hat, inv):
        mean_one = jnp.sum(scaled, -1, keepdims=True) * (1.0 / width)
        mean_two = jnp.sum(crossed, -1, keepdims=True) * (1.0 / width)
        return inv * (scaled - mean_one - hat * mean_two)

    def pad_rows(value, size=LANE):
        rows = value.shape[0]
        return jnp.concatenate([value, jnp.zeros((size - rows, value.shape[1]), F32)], axis=0)

    lead = width + 8

    def grouping(n):
        per = 4 if n <= 64 else 2
        groups = HEADS // per
        return per, groups, [(j, group) for j in range(BATCH) for group in range(groups)]

    def tile(group, per):
        first = group * per // 4
        return slice(first * LANE, (first + 1) * LANE)

    def heads(group, per):
        return slice(per * STRIDE * group, per * STRIDE * (group + 1))

    def put_own(ref, j, per, value):
        size = 2 * LANE // per
        value = pad_rows(value, size)
        cols = stack([value] * (LANE // size)).astype(BF16).T
        for head_at in range(HEADS):
            group, i = divmod(head_at, per)
            rows = slice(head_at % 4 * STRIDE, (head_at % 4 + 1) * STRIDE)
            lanes = slice(i * size % LANE, i * size % LANE + size)
            ref[j, group, rows, i * size : (i + 1) * size] = cols[
                head_at * STRIDE : (head_at + 1) * STRIDE, lanes
            ]

    def own_rows(group, per):
        return slice(group * per % 4 * STRIDE, (group * per % 4 + per) * STRIDE)

    def keep_own(ref, j, group, per, product):
        size = 2 * LANE // per
        for i in range(per):
            block = product[i * STRIDE : (i + 1) * STRIDE]
            at = i * size // LANE
            block = block[:, at * LANE : (at + 1) * LANE]
            if i * size % LANE:
                block = pltpu.roll(block, LANE - i * size % LANE, 1)
            ref[j, per * group + i] = block

    def bases(first):
        return [pl.multiple_of(order[first + j] * SLOT, 8) for j in range(BATCH)]

    def stack(values):
        return jnp.concatenate(values, axis=0)

    def front(box, first, n):
        cuts = {40: (0, 40), 72: (0, 40, 72), 104: (0, 32, 64, 104)}[n]
        chunks = [
            (j, lo, hi) for j in range(BATCH) for lo, hi in zip(cuts[:-1], cuts[1:])
        ]
        at = bases(first)
        limits, live = [], []
        for j in range(BATCH):
            s = order[first + j]
            g = group_ref[s]
            limits.append(jnp.where(g == 0, L1, jnp.where(g == 1, L2, L3)))
            live.append(counts_ref[s])

        per, groups, every = grouping(n)

        def keep(j, lo, hi, value):
            return jnp.where(iota(value.shape, 0) < limits[j] - lo, value, 0.0)

        def rows_of(ref, j, lo, hi):
            return ref[pl.ds(at[j] + lo, hi - lo), :]

        def flat(j, lo, hi):
            return slice(j * n + lo, j * n + hi)

        h1 = []
        for j, lo, hi in chunks:
            hat1, inv1 = norm_stats(rows_of(xrow, j, lo, hi))
            box["hat"][j, lo:hi] = hat1
            box["inv"][j, lo:hi] = jnp.broadcast_to(inv1, (hi - lo, LANE))
            h1.append(hat1 * g1 + b1)
        yield 0
        qkv = dot(stack(h1).astype(BF16), w_qkv[...])
        yield FILL[n][0]
        keys = []
        for j in range(BATCH):
            rows = slice(j * n, (j + 1) * n)
            put_own(box["q_cols"], j, per, qkv[rows, :pad] * q_scale)
            dead = (iota((n, pad), 0) >= live[j]) & spare_lane
            k32 = jnp.where(dead, MASK_VALUE, qkv[rows, pad : 2 * pad])
            k_rows[j, :n] = k32.astype(BF16)
            keys.append(k32)
            yield 0
        for j, group in every:
            scores[j, group, :n] = dot(
                k_rows[j, :n, tile(group, per)], box["q_cols"][j, group]
            )
        for j in range(BATCH):
            v32 = qkv[j * n : (j + 1) * n, 2 * pad :]
            v_rows[j, :n] = v32.astype(BF16)
            v_cols[j] = pad_rows(v32).astype(BF16).T
            box["k_cols"][j] = pad_rows(keys[j]).astype(BF16).T
        yield FILL[n][1]
        for j, group in every:
            score = scores[j, group, :n]
            e = jnp.exp2(score - jnp.max(score, axis=0, keepdims=True))
            p = e * (1.0 / jnp.sum(e, axis=0, keepdims=True))
            probs[j, group, :n] = p
            box["probs_low"][j, group, :n] = p.astype(BF16)
            if group == groups - 1:
                yield 0
        def hidden_grad():
            df = stack([keep(*c, rows_of(crow, *c)) for c in chunks])
            df_low = df.astype(BF16)
            box["df"][: BATCH * n] = df_low
            acc_small[0:8, :] += partial_sums(df)
            return dot(df_low, w_out_t[...])

        for j, group in every:
            o_t = dot(v_cols[j, heads(group, per), :n], box["probs_low"][j, group, :n])
            keep_own(cols, j, group, per, o_t)
        if EARLY_D[n]:
            dhid = hidden_grad()
        yield FILL[n][2]
        mixed = stack([cols[j].reshape(pad, LANE).T[:n] for j in range(BATCH)])
        one = jnp.where(iota((1, LANE), 1) == SPARE, 1.0, mixed[:, :LANE])
        o = jnp.concatenate([one, mixed[:, LANE:]], axis=1).astype(BF16)
        box["o"][: BATCH * n] = o
        yield 0
        a = dot(o, w_o[...])
        yield FILL[n][3]
        y1, hat2, inv2, h2 = [], [], [], []
        for c in chunks:
            y = rows_of(xrow, *c) + keep(*c, a[flat(*c)])
            hat, inv = norm_stats(y)
            y1.append(y)
            hat2.append(hat)
            inv2.append(inv)
            h2.append(hat * g2 + b2)
        h2 = stack(h2).astype(BF16)
        box["h2"][: BATCH * n] = h2
        yield 0
        u = dot(h2, w_in[...])
        if not EARLY_D[n]:
            dhid = hidden_grad()
        yield FILL[n][4]
        hid, du = [], []
        alpha, beta = 0.7978845608028654, 0.044715
        for c in chunks:
            z, up = u[flat(*c), :hidden], u[flat(*c), hidden:]
            dh = dhid[flat(*c)]
            inner = alpha + (alpha * beta) * (z * z)
            gate = 0.5 + 0.5 * jnp.tanh(z * inner)
            act = z * gate
            slope = gate + (act * (1.0 - gate)) * (6.0 * inner - 4.0 * alpha)
            hid.append(act * up)
            du.append(jnp.concatenate([dh * up * slope, dh * act], axis=1))
            if c[1] == 0:
                yield 0
        hid = stack(hid).astype(BF16)
        box["hid"][: BATCH * n] = hid
        du = stack(du).astype(BF16)
        box["du"][: BATCH * n] = du
        yield 0
        dh2 = dot(du, w_in_t[...])
        f = dot(hid, w_out[...])
        yield FILL[n][5]
        da = []
        gain = jnp.zeros((8, pad), F32)
        for i, c in enumerate(chunks):
            j, lo, hi = c
            grad = dh2[flat(*c)]
            crossed = grad * hat2[i]
            gain += partial_sums(crossed)
            dy1 = rows_of(crow, *c) + norm_back(grad * g2, crossed * g2, hat2[i], inv2[i])
            crow[pl.ds(at[j] + lo, hi - lo), :] = dy1
            da.append(keep(*c, dy1))
        acc_small[8:16, :] += gain
        da = stack(da).astype(BF16)
        box["da"][: BATCH * n] = da
        yield 0
        do = dot(da, w_o_t[...])
        for i, c in enumerate(chunks):
            j, lo, hi = c
            xrow[pl.ds(at[j] + lo, hi - lo), :] = y1[i] + keep(*c, f[flat(*c)] + bf)
        yield FILL[n][6]
        for j in range(BATCH):
            put_own(box["d_cols"], j, per, do[j * n : (j + 1) * n])
        yield 0
        for j, group in every:
            scores[j, group, :n] = dot(
                v_rows[j, :n, tile(group, per)], box["d_cols"][j, group]
            )
        yield FILL[n][7]
        for j, group in every:
            dp = scores[j, group, :n]
            p = probs[j, group, :n]
            box["ds_low"][j, group, :n] = (
                p * (dp - jnp.sum(dp * p, axis=0, keepdims=True))
            ).astype(BF16)
            if group == groups - 1:
                yield 0

    def back(box, first, n, layout):
        per, groups, every = grouping(layout)
        rows = slice(0, BATCH * n)
        at = bases(first)
        for j, group in every:
            dq_t = dot(box["k_cols"][j, heads(group, per), :n], box["ds_low"][j, group, :n])
            keep_own(box["dq_cols"], j, group, per, dq_t)
            if group == groups - 1:
                yield
        parts = []
        for j in range(BATCH):
            dv_t, dk_t = [], []
            for group in range(groups):
                own = own_rows(group, per)
                dv_t.append(
                    dot(box["d_cols"][j, group, own], box["probs_low"][j, group, :n], NT)
                )
            yield
            for group in range(groups):
                own = own_rows(group, per)
                dk_t.append(dot(box["q_cols"][j, group, own], box["ds_low"][j, group, :n], NT))
            dq = (box["dq_cols"][j].reshape(pad, LANE) * scale).astype(BF16).T[:n]
            dk = (stack(dk_t) * (1.0 / log2e)).astype(BF16).T
            parts.append(jnp.concatenate([dq, dk, stack(dv_t).astype(BF16).T], axis=1))
            yield
        dqkv = stack(parts)
        dh1 = dot(dqkv, w_qkv_t[...])
        yield
        acc_out[...] += dot(box["df"][rows, :width], box["hid"][rows], TN)
        yield
        acc_o[...] += dot(box["da"][rows, :width], box["o"][rows], TN)
        yield
        h2 = box["h2"][rows, :lead]
        for part in range(2 * hidden // pad):
            lanes = slice(part * pad, (part + 1) * pad)
            acc_in[:, lanes] += dot(h2, box["du"][rows, lanes], TN)
            yield
        h1 = []
        gain = jnp.zeros((8, pad), F32)
        for j in range(BATCH):
            hat = box["hat"][j, :n]
            grad = dh1[j * n : (j + 1) * n]
            crossed = grad * hat
            gain += partial_sums(crossed)
            crow[pl.ds(at[j], n), :] += norm_back(
                grad * g1, crossed * g1, hat, jnp.concatenate([box["inv"][j, :n]] * 2, axis=1)
            )
            h1.append(hat * g1 + b1)
            if j % 2:
                yield
        acc_small[16:24, :] += gain
        h1 = stack(h1).astype(BF16)[:, :lead]
        for part in range(3):
            lanes = slice(part * pad, (part + 1) * pad)
            acc_qkv[:, lanes] += dot(h1, dqkv[:, lanes], TN)
            yield

    def together(fill, main):
        for steps_of in main:
            for _ in range(steps_of):
                next(fill, None)
        for _ in fill:
            pass

    def double(step, n):
        even = step * 2 * BATCH
        before = jnp.maximum(even - BATCH, 0)
        together(back(kept[1], before, n, n), front(kept[0], even, n))
        together(back(kept[0], even, n, n), front(kept[1], even + BATCH, n))

    lengths = (40, 72, 104)
    def kind_of(step):
        return group_ref[order[(step + 1) * 2 * BATCH - 1]]

    def finish_short(step):
        together(back(kept[1], step * 2 * BATCH - BATCH, 40, 40), iter(()))
        for name in ("ds_low", "du", "df", "da"):
            kept[1][name][...] = jnp.zeros_like(kept[1][name])
        for box in kept:
            for name in ("q_cols", "d_cols"):
                box[name][...] = jnp.zeros_like(box[name])

    def one_step(step, carry):
        kind = kind_of(jnp.minimum(step, steps - 1))
        last = kind_of(jnp.maximum(step - 1, 0))
        pl.when((step > 0) & (last == 0) & ((step == steps) | (kind != 0)))(
            functools.partial(finish_short, step)
        )
        pl.when(step < steps)(lambda: fetched(step))
        pl.when(step + 2 < steps)(lambda: fetch(step + 2))
        for member, n in enumerate(lengths):
            pl.when((step < steps) & (kind == member))(functools.partial(double, step, n))
        return carry

    lax.fori_loop(0, steps + 1, one_step, 0)

    cut = 4 * LANE

    def col_copies(part):
        lanes = pl.ds(pl.multiple_of(part * cut, cut), cut)
        return [
            pltpu.make_async_copy(held.at[:, lanes], ref.at[:, lanes], col_sem.at[i, part])
            for i, (held, ref) in enumerate(((y_cols, y_ref), (dx_cols, dx_ref)))
        ]

    def fold_y():
        for part in range(rows_all // cut):
            for member in range(4):
                at = slice(part * cut + member * LANE, part * cut + (member + 1) * LANE)
                y_cols[:, at] = xrow[at, :width].astype(BF16).T
                yield
            col_copies(part)[0].start()

    folding = fold_y()
    for _ in back(kept[1], samples - BATCH, SLOT, SLOT):
        for _ in range(3):
            next(folding, None)
    for _ in folding:
        pass

    def fold_dx():
        for part in range(rows_all // cut):
            for member in range(4):
                at = slice(part * cut + member * LANE, part * cut + (member + 1) * LANE)
                dx_cols[:, at] = crow[at, :width].T
                yield
            col_copies(part)[1].start()

    folding = fold_dx()

    def halves(value):
        high = value.astype(BF16)
        return high, (value - high.astype(F32)).astype(BF16)

    def twice(a, b, dims):
        if a.dtype == F32:
            return sum(dot(part, b, dims) for part in halves(a))
        return sum(dot(a, part, dims) for part in halves(b))

    def small(member):
        block = acc_small[8 * member : 8 * member + 8, :width]
        return jnp.sum(block, axis=0, keepdims=True)

    def gradients():
        for member in range(3):
            g_attn_ref[member * width : (member + 1) * width, :] = twice(
                acc_qkv[:width, member * pad : (member + 1) * pad], spread, NT
            )
            yield
        g_attn_ref[3 * width :, :] = twice(spread, acc_o[...], NT)
        yield
        g_in_ref[...] = acc_in[:width, :].T
        yield
        g_out_ref[...] = acc_out[...].T
        yield
        qkv_sums = acc_qkv[width : width + 8, :]
        in_sums = acc_in[width : width + 8, :]
        g_b1 = twice(qkv_sums, w_qkv_t[...], NN)[0:1, :width]
        g_b2 = twice(in_sums, w_in_t[...], NN)[0:1, :width]
        g_bq = twice(qkv_sums[:, :pad], spread, NT)[0:1]
        g_bv = twice(qkv_sums[:, 2 * pad :], spread, NT)[0:1]
        g_bo = acc_o[...].T[SPARE : SPARE + 1]
        yield
        flat = jnp.concatenate(
            [small(2), g_b1, small(1), g_b2, g_bq, g_bv, g_bo, small(0), in_sums[0:1]], axis=1
        )
        for row in range(16):
            g_vec_ref[row] = flat[:, row * LANE : (row + 1) * LANE]

    for _ in gradients():
        for _ in range(7):
            next(folding, None)
    for _ in folding:
        pass

    def folded(part, carry):
        for copy in col_copies(part):
            copy.wait()
        return carry

    lax.fori_loop(0, rows_all // cut, folded, 0)


def layer(group, counts, order, x_rows, c_rows, attn, ffn_in, ffn_out, vec):
    rows, width = x_rows.shape[0], attn.shape[1]
    hidden = ffn_out.shape[0]
    pad = HEADS * STRIDE
    vmem = pl.BlockSpec(memory_space=pltpu.VMEM)
    smem = pl.BlockSpec(memory_space=pltpu.SMEM)
    whole = pl.BlockSpec(memory_space=pl.ANY)
    return pl.pallas_call(
        layer_kernel,
        name="layer",
        out_shape=(
            jax.ShapeDtypeStruct((width, rows), BF16),
            jax.ShapeDtypeStruct((width, rows), F32),
            jax.ShapeDtypeStruct((4 * width, width), F32),
            jax.ShapeDtypeStruct((2 * hidden, width), F32),
            jax.ShapeDtypeStruct((hidden, width), F32),
            jax.ShapeDtypeStruct((16, 1, LANE), F32),
        ),
        in_specs=[smem] * 3 + [whole] * 2 + [vmem] * 4,
        out_specs=[whole] * 2 + [vmem] * 4,
        scratch_shapes=[
            pltpu.VMEM((rows, pad), F32),
            pltpu.VMEM((rows, pad), F32),
            pltpu.VMEM((width, rows), BF16),
            pltpu.VMEM((width, rows), F32),
            pltpu.SemaphoreType.DMA((group.shape[0] // (2 * BATCH),)),
            pltpu.SemaphoreType.DMA((2, rows // (4 * LANE))),
            pltpu.VMEM((pad, 3 * pad), BF16),
            pltpu.VMEM((3 * pad, pad), BF16),
            pltpu.VMEM((pad, pad), BF16),
            pltpu.VMEM((pad, pad), BF16),
            pltpu.VMEM((pad, 2 * hidden), BF16),
            pltpu.VMEM((2 * hidden, pad), BF16),
            pltpu.VMEM((hidden, pad), BF16),
            pltpu.VMEM((pad, hidden), BF16),
            pltpu.VMEM((BATCH, HEADS // 2, SLOT, 2 * LANE), F32),
            pltpu.VMEM((BATCH, HEADS // 2, SLOT, 2 * LANE), F32),
            pltpu.VMEM((BATCH, SLOT, pad), BF16),
            pltpu.VMEM((BATCH, SLOT, pad), BF16),
            pltpu.VMEM((BATCH, pad, LANE), BF16),
            pltpu.VMEM((BATCH, HEADS, STRIDE, LANE), F32),
            pltpu.VMEM((width + 8, 3 * pad), F32),
            pltpu.VMEM((width, pad), F32),
            pltpu.VMEM((width + 8, 2 * hidden), F32),
            pltpu.VMEM((width, hidden), F32),
            pltpu.VMEM((24, pad), F32),
        ]
        + [
            pltpu.VMEM((BATCH, HEADS // 2, LANE, 2 * LANE), BF16),
            pltpu.VMEM((BATCH, HEADS // 2, LANE, 2 * LANE), BF16),
            pltpu.VMEM((BATCH, HEADS // 2, SLOT, 2 * LANE), BF16),
            pltpu.VMEM((BATCH, HEADS // 2, SLOT, 2 * LANE), BF16),
            pltpu.VMEM((BATCH, pad, LANE), BF16),
            pltpu.VMEM((BATCH, HEADS, STRIDE, LANE), F32),
            pltpu.VMEM((BATCH, SLOT, pad), F32),
            pltpu.VMEM((BATCH, SLOT, LANE), F32),
            pltpu.VMEM((BATCH * SLOT, pad), BF16),
            pltpu.VMEM((BATCH * SLOT, 2 * hidden), BF16),
            pltpu.VMEM((BATCH * SLOT, hidden), BF16),
            pltpu.VMEM((BATCH * SLOT, pad), BF16),
            pltpu.VMEM((BATCH * SLOT, pad), BF16),
            pltpu.VMEM((BATCH * SLOT, pad), BF16),
        ]
        * 2,
        compiler_params=pltpu.CompilerParams(vmem_limit_bytes=60 * 2**20),
    )(group, counts, order, x_rows, c_rows, attn, ffn_in, ffn_out, vec)


class Place:
    def __init__(self, size):
        side = 1
        while 2 * (2 * side) ** 3 <= size:
            side *= 2
        self.size, self.spots = size, side * side
        self.layers = size // self.spots
        me, self.core = lax.axis_index("wide"), lax.axis_index("narrow")
        self.me = me
        self.layer, self.spot = me // self.spots, lax.rem(me, self.spots)

    def at(self, layer, spot):
        layer = lax.rem(self.layer + layer + self.layers, self.layers)
        return layer * self.spots + lax.rem(self.spot + spot + self.spots, self.spots)

    def signal(self):
        barrier = pltpu.get_barrier_semaphore()

        def tell(index, core):
            pl.semaphore_signal(
                barrier, inc=1, device_id=(index, core), device_id_type=MESH
            )

        over(1, self.layers, lambda k: tell(self.at(k, 0), self.core))
        over(1, self.spots, lambda k: tell(self.at(0, k), self.core))
        tell(self.me, 1 - self.core)

    def wait(self):
        pl.semaphore_wait(
            pltpu.get_barrier_semaphore(), self.layers + self.spots - 1
        )


def over(low, high, body):
    def step(k, carry):
        body(k)
        return carry

    lax.fori_loop(low, high, step, 0)


def packed_rows(share):
    return (share + share // 2 + 1 + 15) // 16 * 16


def pack(value, vec):
    share, width = value.shape
    tail = value[:, LANE:]
    tail = jnp.concatenate([tail[: share // 2], tail[share // 2 :]], axis=1)
    if vec.shape[1] < LANE:
        vec = jnp.concatenate([vec, jnp.zeros((1, LANE - vec.shape[1]), F32)], axis=1)
    rest = packed_rows(share) - share - share // 2 - 1
    return jnp.concatenate([value[:, :LANE], tail, vec, jnp.zeros((rest, LANE), F32)], axis=0)


def unpack(block, share):
    at = share + share // 2
    tail = block[share:at]
    tail = jnp.concatenate([tail[:, : LANE // 2], tail[:, LANE // 2 :]], axis=0)
    return jnp.concatenate([block[:share], tail], axis=1), block[at : at + 1]


def gather_kernel(
    group_ref, attn_ref, in_ref, out_ref, vec_ref, tok_hbm, cot_hbm,
    attn_all, in_all, out_all, vec_all, order_ref, x_hbm, c_hbm,
    blocks, tok, cot, xrow, crow, in_sem, row_sem, send_sem, recv_sem, pass_sem, got_sem,
):
    size = attn_all.shape[0]
    share, width = attn_ref.shape
    split = in_ref.shape[0]
    place = Place(size)
    me, core, layers, spots = place.me, place.core, place.layers, place.spots
    cut = 4 * LANE
    parts = tok_hbm.shape[1] // cut
    pad = xrow.shape[1]

    def lanes(part):
        return pl.ds(pl.multiple_of(part * cut, cut), cut)

    def col_copies(part):
        return [
            pltpu.make_async_copy(ref.at[:, lanes(part)], held.at[:, lanes(part)], in_sem.at[i, part])
            for i, (ref, held) in enumerate(((tok_hbm, tok), (cot_hbm, cot)))
        ]

    def row_copies(part):
        return [
            pltpu.make_async_copy(held.at[lanes(part)], ref.at[lanes(part)], row_sem.at[i, part])
            for i, (held, ref) in enumerate(((xrow, x_hbm), (crow, c_hbm)))
        ]

    place.signal()

    def begin(part):
        for copy in col_copies(part):
            copy.start()

    over(0, parts, begin)
    vec = vec_ref[...]
    blocks[0, me] = pack(attn_ref[...], vec).astype(BF16)
    both = jnp.concatenate([in_ref[...], out_ref[...]], axis=0)
    blocks[1, me] = pack(both, vec).astype(BF16)
    place.wait()

    def to_peer(owner, target, slot):
        return pltpu.make_async_remote_copy(
            src_ref=blocks.at[core, owner],
            dst_ref=blocks.at[core, owner],
            send_sem=send_sem.at[slot],
            recv_sem=recv_sem.at[owner],
            device_id=(target, core),
            device_id_type=MESH,
        )

    def to_twin(owner, whose):
        return pltpu.make_async_remote_copy(
            src_ref=blocks.at[whose, owner],
            dst_ref=blocks.at[whose, owner],
            send_sem=pass_sem.at[owner],
            recv_sem=got_sem.at[owner],
            device_id=(me, 1 - core),
            device_id_type=MESH,
        )

    def along(k):
        return to_peer(me, place.at(k, 0), layers * (spots - 1) + k - 1)

    def within(layer, k):
        owner = place.at(-layer, 0)
        return to_peer(owner, place.at(0, k), layer * (spots - 1) + k - 1)

    over(1, layers, lambda k: along(k).start())
    over(1, spots, lambda k: within(0, k).start())

    samples = group_ref.shape[1]
    key = group_ref[...] * samples + iota((1, samples), 1)
    wide = jnp.broadcast_to(key.astype(F32), (samples, samples))
    rank = jnp.sum(jnp.where(wide < wide.T, 1.0, 0.0), axis=1, keepdims=True)
    here = rank == iota((samples, samples), 1).astype(F32)
    found = jnp.where(here, iota((samples, samples), 0).astype(F32), 0.0)
    order_ref[...] = jnp.sum(found, axis=0, keepdims=True).astype(jnp.int32)

    zero = jnp.zeros((LANE, pad - width), F32)

    def unfold(part):
        for copy in col_copies(part):
            copy.wait()
        for member in range(4):
            at = pl.multiple_of(part * cut + member * LANE, LANE)
            for held, rows in ((tok, xrow), (cot, crow)):
                value = held[:, pl.ds(at, LANE)].T.astype(F32)
                rows[pl.ds(at, LANE), :] = jnp.concatenate([value, zero], axis=1)
        for copy in row_copies(part):
            copy.start()

    def arrived(owner):
        to_peer(owner, me, 0).wait_recv()
        to_twin(owner, core).start()

    def forward(layer):
        to_peer(place.at(-layer, 0), me, 0).wait_recv()
        over(1, spots, lambda k: within(layer, k).start())
        to_twin(place.at(-layer, 0), core).start()

    early = min(3, parts)
    over(0, early, unfold)
    over(1, layers, forward)
    over(early, parts, unfold)
    over(1, spots, lambda k: over(0, layers, lambda layer: arrived(place.at(-layer, -k))))

    def end(part):
        for copy in row_copies(part):
            copy.wait()

    def spread_out(owner):
        value, last = unpack(blocks[0, owner].astype(F32), share)
        attn_all[owner] = value.astype(BF16)
        vec_all[owner] = last[:, : vec_all.shape[2]]
        value, _ = unpack(blocks[1, owner].astype(F32), share)
        in_all[owner] = value[:split].astype(BF16)
        out_all[owner] = value[split:].astype(BF16)

    def finish(layer, k):
        owner = place.at(-layer, -k)
        to_twin(owner, 1 - core).wait_recv()
        spread_out(owner)

    spread_out(me)
    over(1, layers, lambda layer: finish(layer, 0))
    over(1, spots, lambda k: over(0, layers, lambda layer: finish(layer, k)))
    over(1, layers, lambda k: along(k).wait_send())
    over(0, layers, lambda layer: over(1, spots, lambda k: within(layer, k).wait_send()))
    over(1, size, lambda k: to_twin(lax.rem(me + k, size), core).wait_send())
    over(0, parts, end)


def gather(size, group, attn, ffn_in, ffn_out, vec, tokens_t, cotangent_t):
    vmem = pl.BlockSpec(memory_space=pltpu.VMEM)
    whole = pl.BlockSpec(memory_space=pl.ANY)
    width, rows = tokens_t.shape
    pad = HEADS * STRIDE
    parts = rows // (4 * LANE)
    return pl.pallas_call(
        gather_kernel,
        name="gather",
        out_shape=tuple(
            jax.ShapeDtypeStruct((size, *value.shape), BF16)
            for value in (attn, ffn_in, ffn_out)
        )
        + (
            jax.ShapeDtypeStruct((size, *vec.shape), F32),
            jax.ShapeDtypeStruct(group.shape, jnp.int32),
            jax.ShapeDtypeStruct((rows, pad), F32),
            jax.ShapeDtypeStruct((rows, pad), F32),
        ),
        in_specs=[vmem] * 5 + [whole] * 2,
        out_specs=[vmem] * 5 + [whole] * 2,
        scratch_shapes=[
            pltpu.VMEM((2, size, packed_rows(attn.shape[0]), LANE), BF16),
            pltpu.VMEM((width, rows), BF16),
            pltpu.VMEM((width, rows), BF16),
            pltpu.VMEM((rows, pad), F32),
            pltpu.VMEM((rows, pad), F32),
            pltpu.SemaphoreType.DMA((2, parts)),
            pltpu.SemaphoreType.DMA((2, parts)),
        ]
        + [pltpu.SemaphoreType.DMA((size,))] * 4,
        compiler_params=pltpu.CompilerParams(
            collective_id=0, has_side_effects=True, vmem_limit_bytes=60 * 2**20
        ),
    )(group, attn, ffn_in, ffn_out, vec, tokens_t, cotangent_t)


def reduce_kernel(
    g_attn, g_in, g_out, g_vec,
    s_attn, s_in, s_out, s_vec,
    own, stage, twin, chip, near, relay, far, total,
    pass_sem, got_sem, near_send, near_recv, far_send, far_recv, last_sem,
):
    size, share = g_attn.shape[:2]
    split = g_in.shape[1]
    place = Place(size)
    me, core, layers, spots = place.me, place.core, place.layers, place.spots
    place.signal()

    def prepare(owner):
        own[0, owner] = pack(g_attn[owner], g_vec[owner])
        both = jnp.concatenate([g_in[owner], g_out[owner]], axis=0)
        own[1, owner] = pack(both, jnp.zeros((1, LANE), F32))
        stage[owner] = own[1 - core, owner].astype(BF16)

    over(0, size, prepare)
    place.wait()

    def to_twin(owner):
        return pltpu.make_async_remote_copy(
            src_ref=stage.at[owner],
            dst_ref=twin.at[owner],
            send_sem=pass_sem.at[owner],
            recv_sem=got_sem.at[owner],
            device_id=(me, 1 - core),
            device_id_type=MESH,
        )

    def within(layer, k, spot, owner_layer):
        owner = place.at(layer, k)
        slot = spot * layers + owner_layer
        return pltpu.make_async_remote_copy(
            src_ref=chip.at[owner],
            dst_ref=near.at[slot],
            send_sem=near_send.at[owner],
            recv_sem=near_recv.at[slot],
            device_id=(place.at(0, k), core),
            device_id_type=MESH,
        )

    def along(layer, sender):
        target = lax.rem(place.layer + layer, layers)
        return pltpu.make_async_remote_copy(
            src_ref=relay.at[target],
            dst_ref=far.at[sender],
            send_sem=far_send.at[target],
            recv_sem=far_recv.at[sender],
            device_id=(place.at(layer, 0), core),
            device_id_type=MESH,
        )

    def result(whose):
        return pltpu.make_async_remote_copy(
            src_ref=total.at[whose],
            dst_ref=total.at[whose],
            send_sem=last_sem.at[0],
            recv_sem=last_sem.at[1],
            device_id=(me, 1 - core),
            device_id_type=MESH,
        )

    def layer_of(layer):
        return lax.rem(place.layer + layer, layers)

    def send(k, layer):
        owner = place.at(layer, k)
        to_twin(owner).wait_recv()
        chip[owner] = (own[core, owner] + twin[owner].astype(F32)).astype(BF16)
        within(layer, k, place.spot, layer_of(layer)).start()

    def spot_sum(layer):
        owner = place.at(layer, 0)
        to_twin(owner).wait_recv()
        total[core] = own[core, owner] + twin[owner].astype(F32)

        def add(k):
            spot = lax.rem(place.spot + k, spots)
            within(layer, k, spot, layer_of(layer)).wait_recv()
            total[core] += near[spot * layers + layer_of(layer)].astype(F32)

        over(1, spots, add)

    def pass_on(layer):
        spot_sum(layer)
        relay[layer_of(layer)] = total[core].astype(BF16)
        along(layer, place.layer).start()

    def take(layer):
        sender = layer_of(layer)
        along(layer, sender).wait_recv()
        total[core] += far[sender].astype(F32)

    over(1, spots, lambda k: over(1, layers, lambda layer: to_twin(place.at(layer, k)).start()))
    over(1, layers, lambda layer: to_twin(place.at(layer, 0)).start())
    over(0, spots, lambda k: to_twin(place.at(0, k)).start())
    over(1, spots, lambda k: over(1, layers, lambda layer: send(k, layer)))
    over(1, spots, lambda k: send(k, 0))
    over(1, layers, pass_on)
    spot_sum(0)
    over(1, layers, take)
    result(core).start()
    over(1, spots, lambda k: over(
        0, layers, lambda layer: within(layer, k, place.spot, layer_of(layer)).wait_send()
    ))
    over(1, layers, lambda layer: along(layer, place.layer).wait_send())
    over(0, size, lambda owner: to_twin(owner).wait_send())
    result(core).wait_send()
    result(1 - core).wait_recv()
    value, last = unpack(total[0], share)
    s_attn[...] = value
    s_vec[...] = last[:, : s_vec.shape[1]]
    value, _ = unpack(total[1], share)
    s_in[...] = value[:split]
    s_out[...] = value[split:]


def reduce_scatter(g_attn, g_in, g_out, g_vec):
    grads = (g_attn, g_in, g_out, g_vec)
    size, share = g_attn.shape[:2]
    vmem = pl.BlockSpec(memory_space=pltpu.VMEM)
    block = (packed_rows(share), LANE)
    return pl.pallas_call(
        reduce_kernel,
        name="reduce",
        out_shape=tuple(jax.ShapeDtypeStruct(value.shape[1:], F32) for value in grads),
        in_specs=[vmem] * 4,
        out_specs=[vmem] * 4,
        scratch_shapes=[pltpu.VMEM((2, size, *block), F32)]
        + [pltpu.VMEM((size, *block), BF16)] * 6
        + [pltpu.VMEM((2, *block), F32)]
        + [pltpu.SemaphoreType.DMA((size,))] * 6
        + [pltpu.SemaphoreType.DMA((2,))],
        compiler_params=pltpu.CompilerParams(
            collective_id=1, has_side_effects=True, vmem_limit_bytes=60 * 2**20
        ),
    )(*grads)


def adamw_kernel(*refs):
    for member in range(4):
        master, first, second, grad = (refs[4 * kind + member][...] for kind in range(4))
        results = adamw_update(master, grad, first, second)
        for kind in range(3):
            refs[16 + 3 * member + kind][...] = results[kind]


def adamw(masters, firsts, seconds, grads):
    vmem = pl.BlockSpec(memory_space=pltpu.VMEM)
    return pl.pallas_call(
        adamw_kernel,
        name="adamw",
        out_shape=tuple(
            jax.ShapeDtypeStruct(value.shape, F32) for value in masters for kind in range(3)
        ),
        in_specs=[vmem] * 16,
        out_specs=[vmem] * 12,
        compiler_params=pltpu.CompilerParams(vmem_limit_bytes=60 * 2**20),
    )(*masters, *firsts, *seconds, *grads)


def local(
    tokens,
    cotangent,
    group,
    counts,
    attn_w,
    ffn_in,
    ffn_out,
    vectors,
    attn_m,
    attn_v,
    in_m,
    in_v,
    out_m,
    out_v,
    vec_m,
    vec_v,
):
    size = lax.axis_size("wide")
    width = tokens.shape[1]
    masters = (attn_w, ffn_in, ffn_out, vectors[None])
    attn, into, outof, vec, order, x_rows, c_rows = gather(
        size, group[None], *masters, tokens.T, cotangent.T
    )
    out_t, grad_t, *grads = layer(
        group,
        counts,
        order[0],
        x_rows,
        c_rows,
        attn.reshape(-1, width),
        into.reshape(-1, width),
        outof.reshape(-1, width),
        vec.reshape(-1, 1, LANE),
    )
    sums = reduce_scatter(
        *[g.reshape(size, -1, width) for g in grads[:3]], grads[3].reshape(size, 1, -1)
    )
    results = adamw(
        masters, (attn_m, in_m, out_m, vec_m[None]), (attn_v, in_v, out_v, vec_v[None]), sums
    )
    return (out_t.T, grad_t.T, *results[:9], *[value[0] for value in results[9:]])


def solution(mesh):
    rows = P(("wide", "narrow"), None)
    samples = P(("wide", "narrow"))
    weight = P("wide", None)
    vector = P("wide")
    return jax.shard_map(
        local,
        mesh=mesh,
        in_specs=(rows, rows, samples, samples, weight, weight, weight, vector)
        + (weight,) * 6
        + (vector,) * 2,
        out_specs=(rows, rows) + (weight,) * 9 + (vector,) * 3,
        check_vma=False,
    )
```

```python
import functools
import math

import jax
import jax.numpy as jnp
from jax import lax
from jax.experimental import pallas as pl
from jax.experimental.pallas import tpu as pltpu
from jax.sharding import PartitionSpec as P

HEADS = 8
SLOT = 104
L1 = 40
L2 = 68
L3 = 100
STEP = 10

NORM_EPS = 1e-05
BETA_ONE = 0.9
BETA_TWO = 0.999
ADAM_EPS = 1e-08
LEARN_RATE = 0.1
WEIGHT_DECAY = 0.01
MASK_VALUE = -1e30

F32 = jnp.float32
BF16 = jnp.bfloat16
LANE = 128
MESH = pl.DeviceIdType.MESH
STRIDE = 32
NN = (((1,), (0,)), ((), ()))
NT = (((1,), (1,)), ((), ()))
TN = (((0,), (0,)), ((), ()))
BATCH = 4
SPARE = 24
FILL = {
    40: (5, 1, 1, 5, 4, 4, 3, 4),
    72: (4, 2, 2, 4, 3, 4, 4, 3),
    104: (4, 2, 2, 5, 3, 3, 5, 2),
}
EARLY_D = {40: True, 72: False, 104: True}


def adamw_update(master, gradient, moment, square):
    moment_new = BETA_ONE * moment + (1.0 - BETA_ONE) * gradient
    square_new = BETA_TWO * square + (1.0 - BETA_TWO) * gradient * gradient
    moment_hat = moment_new / (1.0 - BETA_ONE**STEP)
    square_hat = square_new / (1.0 - BETA_TWO**STEP)
    master_new = master - LEARN_RATE * (
        moment_hat / (jnp.sqrt(square_hat) + ADAM_EPS) + WEIGHT_DECAY * master
    )
    return (master_new, moment_new, square_new)


def dot(a, b, dims=NN):
    return lax.dot_general(a, b, dims, preferred_element_type=F32)


def iota(shape, dim):
    return lax.broadcasted_iota(jnp.int32, shape, dim)


def partial_sums(value):
    rows, cols = value.shape
    return jnp.sum(value.reshape(rows // 8, 8, cols), axis=0)


def piece(vec, member, width):
    start = member * width
    parts, at = [], start
    while at < start + width:
        row, lane = divmod(at, LANE)
        take = min(LANE - lane, start + width - at)
        parts.append(vec[row : row + 1, lane : lane + take])
        at += take
    return jnp.concatenate(parts, axis=1)


def layer_kernel(
    group_ref,
    counts_ref,
    order,
    x_hbm,
    c_hbm,
    attn_hbm,
    in_hbm,
    out_hbm,
    vec_hbm,
    y_ref,
    dx_ref,
    g_attn_hbm,
    g_in_hbm,
    g_out_hbm,
    g_vec_hbm,
    attn_ref,
    in_ref,
    out_ref,
    vec_ref,
    g_attn_ref,
    g_in_ref,
    g_out_ref,
    g_vec_ref,
    weight_sem,
    grad_sem,
    xrow,
    crow,
    y_cols,
    dx_cols,
    row_sem,
    col_sem,
    w_qkv,
    w_qkv_t,
    w_o,
    w_o_t,
    w_in,
    w_in_t,
    w_out,
    w_out_t,
    probs,
    scores,
    k_rows,
    v_rows,
    v_cols,
    cols,
    acc_qkv,
    acc_o,
    acc_in,
    acc_out,
    acc_small,
    *carried,
):
    width = attn_ref.shape[1]
    hidden = out_ref.shape[0]
    samples = group_ref.shape[0]
    rows_all = x_hbm.shape[0]
    head = width // HEADS
    pad = HEADS * STRIDE
    scale = 1.0 / math.sqrt(head)
    log2e = math.log2(math.e)
    q_scale = scale * log2e

    weight_copies = [
        pltpu.make_async_copy(ref, held, weight_sem.at[i])
        for i, (ref, held) in enumerate(
            (
                (attn_hbm, attn_ref),
                (in_hbm, in_ref),
                (out_hbm, out_ref),
                (vec_hbm, vec_ref),
            )
        )
    ]
    grad_copies = [
        pltpu.make_async_copy(held, ref, grad_sem.at[i])
        for i, (held, ref) in enumerate(
            (
                (g_attn_ref, g_attn_hbm),
                (g_in_ref, g_in_hbm),
                (g_out_ref, g_out_hbm),
                (g_vec_ref, g_vec_hbm),
            )
        )
    ]
    for copy in weight_copies:
        copy.start()

    steps = samples // (2 * BATCH)

    def fetch(step):
        for j in range(2 * BATCH):
            rows = pl.ds(pl.multiple_of(order[step * 2 * BATCH + j] * SLOT, 8), SLOT)
            for ref, held in ((x_hbm, xrow), (c_hbm, crow)):
                pltpu.make_async_copy(ref.at[rows], held.at[rows], row_sem.at[step]).start()

    def fetched(step):
        rows = pl.ds(0, 2 * BATCH * SLOT)
        for ref, held in ((x_hbm, xrow), (c_hbm, crow)):
            pltpu.make_async_copy(ref.at[rows], held.at[rows], row_sem.at[step]).wait()

    fetch(0)
    fetch(1)
    for ref in (acc_qkv, acc_o, acc_in, acc_out, acc_small, *carried):
        ref[...] = jnp.zeros_like(ref)
    for copy in weight_copies:
        copy.wait()

    spread_row = iota((width, pad), 0)
    spread_col = iota((width, pad), 1)
    within = spread_col & (STRIDE - 1)
    spread = jnp.where(
        (within < head) & (spread_row == (spread_col >> 5) * head + within), 1.0, 0.0
    ).astype(BF16)
    vec = jnp.concatenate([vec_ref[row] for row in range(vec_ref.shape[0])], axis=0)
    bi = jnp.concatenate([vec[row : row + 1] for row in range(12, 16)], axis=1)

    def widen(value, fill=0.0):
        rows = value.shape[0]
        tail = jnp.where(iota((rows, pad - width), 1) == 0, fill, 0.0)
        return jnp.concatenate([value, tail], axis=1)

    def lengthen(value, row=None):
        cols = value.shape[1]
        if row is None:
            row = jnp.zeros((1, cols), F32)
        tail = jnp.concatenate([row, jnp.zeros((pad - width - 1, cols), F32)], axis=0)
        return jnp.concatenate([value, tail], axis=0)

    g1, b1, g2, b2, bq, bv, bo, bf = (piece(vec, member, width) for member in range(8))
    g1, b1, g2, b2 = widen(g1), widen(b1, 1.0), widen(g2), widen(b2, 1.0)
    bf = widen(bf)
    spare_lane = (iota((1, pad), 1) & (STRIDE - 1)) == SPARE
    for member in range(3):
        spread_w = dot(attn_ref[member * width : (member + 1) * width, :], spread)
        if member == 0:
            bias = dot(bq.astype(BF16), spread) + jnp.where(spare_lane, 1.0, 0.0)
        elif member == 1:
            bias = None
        else:
            bias = dot(bv.astype(BF16), spread)
        w_qkv[:, member * pad : (member + 1) * pad] = lengthen(spread_w, bias).astype(BF16)
        w_qkv_t[member * pad : (member + 1) * pad, :] = widen(spread_w.T).astype(BF16)
    spread_o = widen(dot(spread, attn_ref[3 * width :, :], TN))
    w_o_t[...] = spread_o.T.astype(BF16)
    w_o[...] = jnp.where(iota((pad, pad), 0) == SPARE, widen(bo), spread_o).astype(BF16)
    in_wide = widen(in_ref[...].astype(F32))
    out_wide = widen(out_ref[...].astype(F32))
    w_in_t[...] = in_wide.astype(BF16)
    w_in[...] = lengthen(in_wide[:, :width].T, bi).astype(BF16)
    w_out[...] = out_wide.astype(BF16)
    w_out_t[...] = out_wide.T.astype(BF16)

    names = ("q_cols", "d_cols", "probs_low", "ds_low", "k_cols", "dq_cols", "hat", "inv")
    names += ("h2", "du", "hid", "df", "o", "da")
    kept = [
        dict(zip(names, carried[side * len(names) : (side + 1) * len(names)]))
        for side in range(2)
    ]

    features = iota((1, pad), 1) < width

    def norm_stats(x):
        mean = jnp.sum(x, -1, keepdims=True) * (1.0 / width)
        centre = jnp.where(features, x - mean, 0.0)
        spread_sq = jnp.sum(centre * centre, -1, keepdims=True) * (1.0 / width)
        inv = lax.rsqrt(spread_sq + NORM_EPS)
        return centre * inv, inv

    def norm_back(scaled, crossed, hat, inv):
        mean_one = jnp.sum(scaled, -1, keepdims=True) * (1.0 / width)
        mean_two = jnp.sum(crossed, -1, keepdims=True) * (1.0 / width)
        return inv * (scaled - mean_one - hat * mean_two)

    def pad_rows(value, size=LANE):
        rows = value.shape[0]
        return jnp.concatenate([value, jnp.zeros((size - rows, value.shape[1]), F32)], axis=0)

    lead = width + 8

    def grouping(n):
        per = 4 if n <= 64 else 2
        groups = HEADS // per
        return per, groups, [(j, group) for j in range(BATCH) for group in range(groups)]

    def tile(group, per):
        first = group * per // 4
        return slice(first * LANE, (first + 1) * LANE)

    def heads(group, per):
        return slice(per * STRIDE * group, per * STRIDE * (group + 1))

    def put_own(ref, j, per, value):
        size = 2 * LANE // per
        value = pad_rows(value, size)
        cols = stack([value] * (LANE // size)).astype(BF16).T
        for head_at in range(HEADS):
            group, i = divmod(head_at, per)
            rows = slice(head_at % 4 * STRIDE, (head_at % 4 + 1) * STRIDE)
            lanes = slice(i * size % LANE, i * size % LANE + size)
            ref[j, group, rows, i * size : (i + 1) * size] = cols[
                head_at * STRIDE : (head_at + 1) * STRIDE, lanes
            ]

    def own_rows(group, per):
        return slice(group * per % 4 * STRIDE, (group * per % 4 + per) * STRIDE)

    def keep_own(ref, j, group, per, product):
        size = 2 * LANE // per
        for i in range(per):
            block = product[i * STRIDE : (i + 1) * STRIDE]
            at = i * size // LANE
            block = block[:, at * LANE : (at + 1) * LANE]
            if i * size % LANE:
                block = pltpu.roll(block, LANE - i * size % LANE, 1)
            ref[j, per * group + i] = block

    def bases(first):
        return [pl.multiple_of(order[first + j] * SLOT, 8) for j in range(BATCH)]

    def stack(values):
        return jnp.concatenate(values, axis=0)

    def front(box, first, n):
        cuts = {40: (0, 40), 72: (0, 40, 72), 104: (0, 32, 64, 104)}[n]
        chunks = [
            (j, lo, hi) for j in range(BATCH) for lo, hi in zip(cuts[:-1], cuts[1:])
        ]
        at = bases(first)
        limits, live = [], []
        for j in range(BATCH):
            s = order[first + j]
            g = group_ref[s]
            limits.append(jnp.where(g == 0, L1, jnp.where(g == 1, L2, L3)))
            live.append(counts_ref[s])

        per, groups, every = grouping(n)

        def keep(j, lo, hi, value):
            return jnp.where(iota(value.shape, 0) < limits[j] - lo, value, 0.0)

        def rows_of(ref, j, lo, hi):
            return ref[pl.ds(at[j] + lo, hi - lo), :]

        def flat(j, lo, hi):
            return slice(j * n + lo, j * n + hi)

        h1 = []
        for j, lo, hi in chunks:
            hat1, inv1 = norm_stats(rows_of(xrow, j, lo, hi))
            box["hat"][j, lo:hi] = hat1
            box["inv"][j, lo:hi] = jnp.broadcast_to(inv1, (hi - lo, LANE))
            h1.append(hat1 * g1 + b1)
        yield 0
        qkv = dot(stack(h1).astype(BF16), w_qkv[...])
        yield FILL[n][0]
        keys = []
        for j in range(BATCH):
            rows = slice(j * n, (j + 1) * n)
            put_own(box["q_cols"], j, per, qkv[rows, :pad] * q_scale)
            dead = (iota((n, pad), 0) >= live[j]) & spare_lane
            k32 = jnp.where(dead, MASK_VALUE, qkv[rows, pad : 2 * pad])
            k_rows[j, :n] = k32.astype(BF16)
            keys.append(k32)
            yield 0
        for j, group in every:
            scores[j, group, :n] = dot(
                k_rows[j, :n, tile(group, per)], box["q_cols"][j, group]
            )
        for j in range(BATCH):
            v32 = qkv[j * n : (j + 1) * n, 2 * pad :]
            v_rows[j, :n] = v32.astype(BF16)
            v_cols[j] = pad_rows(v32).astype(BF16).T
            box["k_cols"][j] = pad_rows(keys[j]).astype(BF16).T
        yield FILL[n][1]
        for j, group in every:
            score = scores[j, group, :n]
            e = jnp.exp2(score - jnp.max(score, axis=0, keepdims=True))
            p = e * (1.0 / jnp.sum(e, axis=0, keepdims=True))
            probs[j, group, :n] = p
            box["probs_low"][j, group, :n] = p.astype(BF16)
            if group == groups - 1:
                yield 0
        def hidden_grad():
            df = stack([keep(*c, rows_of(crow, *c)) for c in chunks])
            df_low = df.astype(BF16)
            box["df"][: BATCH * n] = df_low
            acc_small[0:8, :] += partial_sums(df)
            return dot(df_low, w_out_t[...])

        for j, group in every:
            o_t = dot(v_cols[j, heads(group, per), :n], box["probs_low"][j, group, :n])
            keep_own(cols, j, group, per, o_t)
        if EARLY_D[n]:
            dhid = hidden_grad()
        yield FILL[n][2]
        mixed = stack([cols[j].reshape(pad, LANE).T[:n] for j in range(BATCH)])
        one = jnp.where(iota((1, LANE), 1) == SPARE, 1.0, mixed[:, :LANE])
        o = jnp.concatenate([one, mixed[:, LANE:]], axis=1).astype(BF16)
        box["o"][: BATCH * n] = o
        yield 0
        a = dot(o, w_o[...])
        yield FILL[n][3]
        y1, hat2, inv2, h2 = [], [], [], []
        for c in chunks:
            y = rows_of(xrow, *c) + keep(*c, a[flat(*c)])
            hat, inv = norm_stats(y)
            y1.append(y)
            hat2.append(hat)
            inv2.append(inv)
            h2.append(hat * g2 + b2)
        h2 = stack(h2).astype(BF16)
        box["h2"][: BATCH * n] = h2
        yield 0
        u = dot(h2, w_in[...])
        if not EARLY_D[n]:
            dhid = hidden_grad()
        yield FILL[n][4]
        hid, du = [], []
        alpha, beta = 0.7978845608028654, 0.044715
        for c in chunks:
            z, up = u[flat(*c), :hidden], u[flat(*c), hidden:]
            dh = dhid[flat(*c)]
            inner = alpha + (alpha * beta) * (z * z)
            gate = 0.5 + 0.5 * jnp.tanh(z * inner)
            act = z * gate
            slope = gate + (act * (1.0 - gate)) * (6.0 * inner - 4.0 * alpha)
            hid.append(act * up)
            du.append(jnp.concatenate([dh * up * slope, dh * act], axis=1))
            if c[1] == 0:
                yield 0
        hid = stack(hid).astype(BF16)
        box["hid"][: BATCH * n] = hid
        du = stack(du).astype(BF16)
        box["du"][: BATCH * n] = du
        yield 0
        dh2 = dot(du, w_in_t[...])
        f = dot(hid, w_out[...])
        yield FILL[n][5]
        da = []
        gain = jnp.zeros((8, pad), F32)
        for i, c in enumerate(chunks):
            j, lo, hi = c
            grad = dh2[flat(*c)]
            crossed = grad * hat2[i]
            gain += partial_sums(crossed)
            dy1 = rows_of(crow, *c) + norm_back(grad * g2, crossed * g2, hat2[i], inv2[i])
            crow[pl.ds(at[j] + lo, hi - lo), :] = dy1
            da.append(keep(*c, dy1))
        acc_small[8:16, :] += gain
        da = stack(da).astype(BF16)
        box["da"][: BATCH * n] = da
        yield 0
        do = dot(da, w_o_t[...])
        for i, c in enumerate(chunks):
            j, lo, hi = c
            xrow[pl.ds(at[j] + lo, hi - lo), :] = y1[i] + keep(*c, f[flat(*c)] + bf)
        yield FILL[n][6]
        for j in range(BATCH):
            put_own(box["d_cols"], j, per, do[j * n : (j + 1) * n])
        yield 0
        for j, group in every:
            scores[j, group, :n] = dot(
                v_rows[j, :n, tile(group, per)], box["d_cols"][j, group]
            )
        yield FILL[n][7]
        for j, group in every:
            dp = scores[j, group, :n]
            p = probs[j, group, :n]
            box["ds_low"][j, group, :n] = (
                p * (dp - jnp.sum(dp * p, axis=0, keepdims=True))
            ).astype(BF16)
            if group == groups - 1:
                yield 0

    def back(box, first, n, layout):
        per, groups, every = grouping(layout)
        rows = slice(0, BATCH * n)
        at = bases(first)
        for j, group in every:
            dq_t = dot(box["k_cols"][j, heads(group, per), :n], box["ds_low"][j, group, :n])
            keep_own(box["dq_cols"], j, group, per, dq_t)
            if group == groups - 1:
                yield
        parts = []
        for j in range(BATCH):
            dv_t, dk_t = [], []
            for group in range(groups):
                own = own_rows(group, per)
                dv_t.append(
                    dot(box["d_cols"][j, group, own], box["probs_low"][j, group, :n], NT)
                )
            yield
            for group in range(groups):
                own = own_rows(group, per)
                dk_t.append(dot(box["q_cols"][j, group, own], box["ds_low"][j, group, :n], NT))
            dq = (box["dq_cols"][j].reshape(pad, LANE) * scale).astype(BF16).T[:n]
            dk = (stack(dk_t) * (1.0 / log2e)).astype(BF16).T
            parts.append(jnp.concatenate([dq, dk, stack(dv_t).astype(BF16).T], axis=1))
            yield
        dqkv = stack(parts)
        dh1 = dot(dqkv, w_qkv_t[...])
        yield
        acc_out[...] += dot(box["df"][rows, :width], box["hid"][rows], TN)
        yield
        acc_o[...] += dot(box["da"][rows, :width], box["o"][rows], TN)
        yield
        h2 = box["h2"][rows, :lead]
        for part in range(2 * hidden // pad):
            lanes = slice(part * pad, (part + 1) * pad)
            acc_in[:, lanes] += dot(h2, box["du"][rows, lanes], TN)
            yield
        h1 = []
        gain = jnp.zeros((8, pad), F32)
        for j in range(BATCH):
            hat = box["hat"][j, :n]
            grad = dh1[j * n : (j + 1) * n]
            crossed = grad * hat
            gain += partial_sums(crossed)
            crow[pl.ds(at[j], n), :] += norm_back(
                grad * g1, crossed * g1, hat, jnp.concatenate([box["inv"][j, :n]] * 2, axis=1)
            )
            h1.append(hat * g1 + b1)
            if j % 2:
                yield
        acc_small[16:24, :] += gain
        h1 = stack(h1).astype(BF16)[:, :lead]
        for part in range(3):
            lanes = slice(part * pad, (part + 1) * pad)
            acc_qkv[:, lanes] += dot(h1, dqkv[:, lanes], TN)
            yield

    def together(fill, main):
        for steps_of in main:
            for _ in range(steps_of):
                next(fill, None)
        for _ in fill:
            pass

    def double(step, n):
        even = step * 2 * BATCH
        before = jnp.maximum(even - BATCH, 0)
        together(back(kept[1], before, n, n), front(kept[0], even, n))
        together(back(kept[0], even, n, n), front(kept[1], even + BATCH, n))

    lengths = (40, 72, 104)
    def kind_of(step):
        return group_ref[order[(step + 1) * 2 * BATCH - 1]]

    def finish_short(step):
        together(back(kept[1], step * 2 * BATCH - BATCH, 40, 40), iter(()))
        for name in ("ds_low", "du", "df", "da"):
            kept[1][name][...] = jnp.zeros_like(kept[1][name])
        for box in kept:
            for name in ("q_cols", "d_cols"):
                box[name][...] = jnp.zeros_like(box[name])

    def one_step(step, carry):
        kind = kind_of(jnp.minimum(step, steps - 1))
        last = kind_of(jnp.maximum(step - 1, 0))
        pl.when((step > 0) & (last == 0) & ((step == steps) | (kind != 0)))(
            functools.partial(finish_short, step)
        )
        pl.when(step < steps)(lambda: fetched(step))
        pl.when(step + 2 < steps)(lambda: fetch(step + 2))
        for member, n in enumerate(lengths):
            pl.when((step < steps) & (kind == member))(functools.partial(double, step, n))
        return carry

    lax.fori_loop(0, steps + 1, one_step, 0)

    cut = 4 * LANE

    def col_copies(part):
        lanes = pl.ds(pl.multiple_of(part * cut, cut), cut)
        return [
            pltpu.make_async_copy(held.at[:, lanes], ref.at[:, lanes], col_sem.at[i, part])
            for i, (held, ref) in enumerate(((y_cols, y_ref), (dx_cols, dx_ref)))
        ]

    def fold_y():
        for part in range(rows_all // cut):
            for member in range(4):
                at = slice(part * cut + member * LANE, part * cut + (member + 1) * LANE)
                y_cols[:, at] = xrow[at, :width].astype(BF16).T
                yield
            col_copies(part)[0].start()

    folding = fold_y()
    for _ in back(kept[1], samples - BATCH, SLOT, SLOT):
        for _ in range(3):
            next(folding, None)
    for _ in folding:
        pass

    def fold_dx():
        for part in range(rows_all // cut):
            for member in range(4):
                at = slice(part * cut + member * LANE, part * cut + (member + 1) * LANE)
                dx_cols[:, at] = crow[at, :width].T
                yield
            col_copies(part)[1].start()

    folding = fold_dx()

    def halves(value):
        high = value.astype(BF16)
        return high, (value - high.astype(F32)).astype(BF16)

    def twice(a, b, dims):
        if a.dtype == F32:
            return sum(dot(part, b, dims) for part in halves(a))
        return sum(dot(a, part, dims) for part in halves(b))

    def small(member):
        block = acc_small[8 * member : 8 * member + 8, :width]
        return jnp.sum(block, axis=0, keepdims=True)

    def gradients():
        for member in range(3):
            g_attn_ref[member * width : (member + 1) * width, :] = twice(
                acc_qkv[:width, member * pad : (member + 1) * pad], spread, NT
            )
            yield
        g_attn_ref[3 * width :, :] = twice(spread, acc_o[...], NT)
        grad_copies[0].start()
        yield
        g_in_ref[...] = acc_in[:width, :].T
        grad_copies[1].start()
        yield
        g_out_ref[...] = acc_out[...].T
        grad_copies[2].start()
        yield
        qkv_sums = acc_qkv[width : width + 8, :]
        in_sums = acc_in[width : width + 8, :]
        g_b1 = twice(qkv_sums, w_qkv_t[...], NN)[0:1, :width]
        g_b2 = twice(in_sums, w_in_t[...], NN)[0:1, :width]
        g_bq = twice(qkv_sums[:, :pad], spread, NT)[0:1]
        g_bv = twice(qkv_sums[:, 2 * pad :], spread, NT)[0:1]
        g_bo = acc_o[...].T[SPARE : SPARE + 1]
        yield
        flat = jnp.concatenate(
            [small(2), g_b1, small(1), g_b2, g_bq, g_bv, g_bo, small(0), in_sums[0:1]], axis=1
        )
        for row in range(16):
            g_vec_ref[row] = flat[:, row * LANE : (row + 1) * LANE]
        grad_copies[3].start()

    for _ in gradients():
        for _ in range(7):
            next(folding, None)
    for _ in folding:
        pass

    def folded(part, carry):
        for copy in col_copies(part):
            copy.wait()
        return carry

    lax.fori_loop(0, rows_all // cut, folded, 0)
    for copy in grad_copies:
        copy.wait()


def layer(group, counts, order, x_rows, c_rows, attn, ffn_in, ffn_out, vec):
    rows, width = x_rows.shape[0], attn.shape[1]
    weights = (attn, ffn_in, ffn_out, vec)
    hidden = ffn_out.shape[0]
    pad = HEADS * STRIDE
    smem = pl.BlockSpec(memory_space=pltpu.SMEM)
    whole = pl.BlockSpec(memory_space=pl.ANY)
    return pl.pallas_call(
        layer_kernel,
        name="layer",
        out_shape=(
            jax.ShapeDtypeStruct((width, rows), BF16),
            jax.ShapeDtypeStruct((width, rows), F32),
            jax.ShapeDtypeStruct((4 * width, width), F32),
            jax.ShapeDtypeStruct((2 * hidden, width), F32),
            jax.ShapeDtypeStruct((hidden, width), F32),
            jax.ShapeDtypeStruct((16, 1, LANE), F32),
        ),
        in_specs=[smem] * 3 + [whole] * 6,
        out_specs=[whole] * 6,
        scratch_shapes=[pltpu.VMEM(value.shape, value.dtype) for value in weights]
        + [
            pltpu.VMEM((4 * width, width), F32),
            pltpu.VMEM((2 * hidden, width), F32),
            pltpu.VMEM((hidden, width), F32),
            pltpu.VMEM((16, 1, LANE), F32),
            pltpu.SemaphoreType.DMA((4,)),
            pltpu.SemaphoreType.DMA((4,)),
            pltpu.VMEM((rows, pad), F32),
            pltpu.VMEM((rows, pad), F32),
            pltpu.VMEM((width, rows), BF16),
            pltpu.VMEM((width, rows), F32),
            pltpu.SemaphoreType.DMA((group.shape[0] // (2 * BATCH),)),
            pltpu.SemaphoreType.DMA((2, rows // (4 * LANE))),
            pltpu.VMEM((pad, 3 * pad), BF16),
            pltpu.VMEM((3 * pad, pad), BF16),
            pltpu.VMEM((pad, pad), BF16),
            pltpu.VMEM((pad, pad), BF16),
            pltpu.VMEM((pad, 2 * hidden), BF16),
            pltpu.VMEM((2 * hidden, pad), BF16),
            pltpu.VMEM((hidden, pad), BF16),
            pltpu.VMEM((pad, hidden), BF16),
            pltpu.VMEM((BATCH, HEADS // 2, SLOT, 2 * LANE), F32),
            pltpu.VMEM((BATCH, HEADS // 2, SLOT, 2 * LANE), F32),
            pltpu.VMEM((BATCH, SLOT + 8, pad), BF16),
            pltpu.VMEM((BATCH, SLOT + 8, pad), BF16),
            pltpu.VMEM((BATCH, pad, LANE), BF16),
            pltpu.VMEM((BATCH, HEADS, STRIDE, LANE), F32),
            pltpu.VMEM((width + 8, 3 * pad), F32),
            pltpu.VMEM((width, pad), F32),
            pltpu.VMEM((width + 8, 2 * hidden), F32),
            pltpu.VMEM((width, hidden), F32),
            pltpu.VMEM((24, pad), F32),
        ]
        + [
            pltpu.VMEM((BATCH, HEADS // 2, LANE, 2 * LANE), BF16),
            pltpu.VMEM((BATCH, HEADS // 2, LANE, 2 * LANE), BF16),
            pltpu.VMEM((BATCH, HEADS // 2, SLOT + 8, 2 * LANE), BF16),
            pltpu.VMEM((BATCH, HEADS // 2, SLOT + 8, 2 * LANE), BF16),
            pltpu.VMEM((BATCH, pad, LANE), BF16),
            pltpu.VMEM((BATCH, HEADS, STRIDE, LANE), F32),
            pltpu.VMEM((BATCH, SLOT, pad), F32),
            pltpu.VMEM((BATCH, SLOT, LANE), F32),
            pltpu.VMEM((BATCH * SLOT, pad), BF16),
            pltpu.VMEM((BATCH * SLOT, 2 * hidden), BF16),
            pltpu.VMEM((BATCH * SLOT, hidden), BF16),
            pltpu.VMEM((BATCH * SLOT, pad), BF16),
            pltpu.VMEM((BATCH * SLOT, pad), BF16),
            pltpu.VMEM((BATCH * SLOT, pad), BF16),
        ]
        * 2,
        compiler_params=pltpu.CompilerParams(vmem_limit_bytes=60 * 2**20),
    )(group, counts, order, x_rows, c_rows, attn, ffn_in, ffn_out, vec)


class Place:
    def __init__(self, size):
        side = 1
        while 2 * (2 * side) ** 3 <= size:
            side *= 2
        self.size, self.spots = size, side * side
        self.layers = size // self.spots
        me, self.core = lax.axis_index("wide"), lax.axis_index("narrow")
        self.me = me
        self.layer, self.spot = me // self.spots, lax.rem(me, self.spots)

    def at(self, layer, spot):
        layer = lax.rem(self.layer + layer + self.layers, self.layers)
        return layer * self.spots + lax.rem(self.spot + spot + self.spots, self.spots)

    def signal(self):
        barrier = pltpu.get_barrier_semaphore()

        def tell(index, core):
            pl.semaphore_signal(
                barrier, inc=1, device_id=(index, core), device_id_type=MESH
            )

        over(1, self.layers, lambda k: tell(self.at(k, 0), self.core))
        over(1, self.spots, lambda k: tell(self.at(0, k), self.core))
        tell(self.me, 1 - self.core)

    def wait(self):
        pl.semaphore_wait(
            pltpu.get_barrier_semaphore(), self.layers + self.spots - 1
        )


def over(low, high, body):
    def step(k, carry):
        body(k)
        return carry

    lax.fori_loop(low, high, step, 0)


def packed_rows(share):
    return (share + share // 2 + 1 + 15) // 16 * 16


def pack(value, vec):
    share, width = value.shape
    tail = value[:, LANE:]
    tail = jnp.concatenate([tail[: share // 2], tail[share // 2 :]], axis=1)
    if vec.shape[1] < LANE:
        vec = jnp.concatenate([vec, jnp.zeros((1, LANE - vec.shape[1]), F32)], axis=1)
    rest = packed_rows(share) - share - share // 2 - 1
    return jnp.concatenate([value[:, :LANE], tail, vec, jnp.zeros((rest, LANE), F32)], axis=0)


def unpack(block, share):
    at = share + share // 2
    tail = block[share:at]
    tail = jnp.concatenate([tail[:, : LANE // 2], tail[:, LANE // 2 :]], axis=0)
    return jnp.concatenate([block[:share], tail], axis=1), block[at : at + 1]


def gather_kernel(
    group_ref, attn_ref, in_ref, out_ref, vec_ref, tok_hbm, cot_hbm,
    attn_all, in_all, out_all, vec_all, order_ref, x_hbm, c_hbm,
    blocks, tok, cot, xrow, crow, in_sem, row_sem, send_sem, recv_sem, pass_sem, got_sem,
):
    size = attn_all.shape[0]
    share, width = attn_ref.shape
    split = in_ref.shape[0]
    place = Place(size)
    me, core, layers, spots = place.me, place.core, place.layers, place.spots
    cut = 4 * LANE
    parts = tok_hbm.shape[1] // cut
    pad = xrow.shape[1]

    def lanes(part):
        return pl.ds(pl.multiple_of(part * cut, cut), cut)

    def col_copies(part):
        return [
            pltpu.make_async_copy(ref.at[:, lanes(part)], held.at[:, lanes(part)], in_sem.at[i, part])
            for i, (ref, held) in enumerate(((tok_hbm, tok), (cot_hbm, cot)))
        ]

    def row_copies(part):
        return [
            pltpu.make_async_copy(held.at[lanes(part)], ref.at[lanes(part)], row_sem.at[i, part])
            for i, (held, ref) in enumerate(((xrow, x_hbm), (crow, c_hbm)))
        ]

    place.signal()

    def begin(part):
        for copy in col_copies(part):
            copy.start()

    over(0, parts, begin)
    vec = vec_ref[...]
    blocks[0, me] = pack(attn_ref[...], vec).astype(BF16)
    both = jnp.concatenate([in_ref[...], out_ref[...]], axis=0)
    blocks[1, me] = pack(both, vec).astype(BF16)
    place.wait()

    def to_peer(owner, target, slot):
        return pltpu.make_async_remote_copy(
            src_ref=blocks.at[core, owner],
            dst_ref=blocks.at[core, owner],
            send_sem=send_sem.at[slot],
            recv_sem=recv_sem.at[owner],
            device_id=(target, core),
            device_id_type=MESH,
        )

    def to_twin(owner, whose):
        return pltpu.make_async_remote_copy(
            src_ref=blocks.at[whose, owner],
            dst_ref=blocks.at[whose, owner],
            send_sem=pass_sem.at[owner],
            recv_sem=got_sem.at[owner],
            device_id=(me, 1 - core),
            device_id_type=MESH,
        )

    def along(k):
        return to_peer(me, place.at(k, 0), layers * (spots - 1) + k - 1)

    def within(layer, k):
        owner = place.at(-layer, 0)
        return to_peer(owner, place.at(0, k), layer * (spots - 1) + k - 1)

    over(1, layers, lambda k: along(k).start())
    over(1, spots, lambda k: within(0, k).start())

    samples = group_ref.shape[1]
    key = group_ref[...] * samples + iota((1, samples), 1)
    wide = jnp.broadcast_to(key.astype(F32), (samples, samples))
    rank = jnp.sum(jnp.where(wide < wide.T, 1.0, 0.0), axis=1, keepdims=True)
    here = rank == iota((samples, samples), 1).astype(F32)
    found = jnp.where(here, iota((samples, samples), 0).astype(F32), 0.0)
    order_ref[...] = jnp.sum(found, axis=0, keepdims=True).astype(jnp.int32)

    zero = jnp.zeros((LANE, pad - width), F32)

    def unfold(part):
        for copy in col_copies(part):
            copy.wait()
        for member in range(4):
            at = pl.multiple_of(part * cut + member * LANE, LANE)
            for held, rows in ((tok, xrow), (cot, crow)):
                value = held[:, pl.ds(at, LANE)].T.astype(F32)
                rows[pl.ds(at, LANE), :] = jnp.concatenate([value, zero], axis=1)
        for copy in row_copies(part):
            copy.start()

    def arrived(owner):
        to_peer(owner, me, 0).wait_recv()
        to_twin(owner, core).start()

    def forward(layer):
        to_peer(place.at(-layer, 0), me, 0).wait_recv()
        over(1, spots, lambda k: within(layer, k).start())
        to_twin(place.at(-layer, 0), core).start()

    early = min(3, parts)
    over(0, early, unfold)
    over(1, layers, forward)
    over(early, parts, unfold)
    over(1, spots, lambda k: over(0, layers, lambda layer: arrived(place.at(-layer, -k))))

    def end(part):
        for copy in row_copies(part):
            copy.wait()

    def spread_out(owner):
        value, last = unpack(blocks[0, owner].astype(F32), share)
        attn_all[owner] = value.astype(BF16)
        vec_all[owner] = last[:, : vec_all.shape[2]]
        value, _ = unpack(blocks[1, owner].astype(F32), share)
        in_all[owner] = value[:split].astype(BF16)
        out_all[owner] = value[split:].astype(BF16)

    def finish(layer, k):
        owner = place.at(-layer, -k)
        to_twin(owner, 1 - core).wait_recv()
        spread_out(owner)

    spread_out(me)
    over(1, layers, lambda layer: finish(layer, 0))
    over(1, spots, lambda k: over(0, layers, lambda layer: finish(layer, k)))
    over(1, layers, lambda k: along(k).wait_send())
    over(0, layers, lambda layer: over(1, spots, lambda k: within(layer, k).wait_send()))
    over(1, size, lambda k: to_twin(lax.rem(me + k, size), core).wait_send())
    over(0, parts, end)


def gather(size, group, attn, ffn_in, ffn_out, vec, tokens_t, cotangent_t):
    vmem = pl.BlockSpec(memory_space=pltpu.VMEM)
    whole = pl.BlockSpec(memory_space=pl.ANY)
    width, rows = tokens_t.shape
    pad = HEADS * STRIDE
    parts = rows // (4 * LANE)
    return pl.pallas_call(
        gather_kernel,
        name="gather",
        out_shape=tuple(
            jax.ShapeDtypeStruct((size, *value.shape), BF16)
            for value in (attn, ffn_in, ffn_out)
        )
        + (
            jax.ShapeDtypeStruct((size, *vec.shape), F32),
            jax.ShapeDtypeStruct(group.shape, jnp.int32),
            jax.ShapeDtypeStruct((rows, pad), F32),
            jax.ShapeDtypeStruct((rows, pad), F32),
        ),
        in_specs=[vmem] * 5 + [whole] * 2,
        out_specs=[vmem] * 5 + [whole] * 2,
        scratch_shapes=[
            pltpu.VMEM((2, size, packed_rows(attn.shape[0]), LANE), BF16),
            pltpu.VMEM((width, rows), BF16),
            pltpu.VMEM((width, rows), BF16),
            pltpu.VMEM((rows, pad), F32),
            pltpu.VMEM((rows, pad), F32),
            pltpu.SemaphoreType.DMA((2, parts)),
            pltpu.SemaphoreType.DMA((2, parts)),
        ]
        + [pltpu.SemaphoreType.DMA((size,))] * 4,
        compiler_params=pltpu.CompilerParams(
            collective_id=0, has_side_effects=True, vmem_limit_bytes=60 * 2**20
        ),
    )(group, attn, ffn_in, ffn_out, vec, tokens_t, cotangent_t)


def reduce_kernel(
    g_attn, g_in, g_out, g_vec,
    s_attn, s_in, s_out, s_vec,
    own, stage, twin, chip, near, relay, far, total,
    pass_sem, got_sem, near_send, near_recv, far_send, far_recv, last_sem,
):
    size, share = g_attn.shape[:2]
    split = g_in.shape[1]
    place = Place(size)
    me, core, layers, spots = place.me, place.core, place.layers, place.spots
    place.signal()

    def prepare(owner):
        own[0, owner] = pack(g_attn[owner], g_vec[owner])
        both = jnp.concatenate([g_in[owner], g_out[owner]], axis=0)
        own[1, owner] = pack(both, jnp.zeros((1, LANE), F32))
        stage[owner] = own[1 - core, owner].astype(BF16)

    over(0, size, prepare)
    place.wait()

    def to_twin(owner):
        return pltpu.make_async_remote_copy(
            src_ref=stage.at[owner],
            dst_ref=twin.at[owner],
            send_sem=pass_sem.at[owner],
            recv_sem=got_sem.at[owner],
            device_id=(me, 1 - core),
            device_id_type=MESH,
        )

    def within(layer, k, spot, owner_layer):
        owner = place.at(layer, k)
        slot = spot * layers + owner_layer
        return pltpu.make_async_remote_copy(
            src_ref=chip.at[owner],
            dst_ref=near.at[slot],
            send_sem=near_send.at[owner],
            recv_sem=near_recv.at[slot],
            device_id=(place.at(0, k), core),
            device_id_type=MESH,
        )

    def along(layer, sender):
        target = lax.rem(place.layer + layer, layers)
        return pltpu.make_async_remote_copy(
            src_ref=relay.at[target],
            dst_ref=far.at[sender],
            send_sem=far_send.at[target],
            recv_sem=far_recv.at[sender],
            device_id=(place.at(layer, 0), core),
            device_id_type=MESH,
        )

    def result(whose):
        return pltpu.make_async_remote_copy(
            src_ref=total.at[whose],
            dst_ref=total.at[whose],
            send_sem=last_sem.at[0],
            recv_sem=last_sem.at[1],
            device_id=(me, 1 - core),
            device_id_type=MESH,
        )

    def layer_of(layer):
        return lax.rem(place.layer + layer, layers)

    def send(k, layer):
        owner = place.at(layer, k)
        to_twin(owner).wait_recv()
        chip[owner] = (own[core, owner] + twin[owner].astype(F32)).astype(BF16)
        within(layer, k, place.spot, layer_of(layer)).start()

    def spot_sum(layer):
        owner = place.at(layer, 0)
        to_twin(owner).wait_recv()
        total[core] = own[core, owner] + twin[owner].astype(F32)

        def add(k):
            spot = lax.rem(place.spot + k, spots)
            within(layer, k, spot, layer_of(layer)).wait_recv()
            total[core] += near[spot * layers + layer_of(layer)].astype(F32)

        over(1, spots, add)

    def pass_on(layer):
        spot_sum(layer)
        relay[layer_of(layer)] = total[core].astype(BF16)
        along(layer, place.layer).start()

    def take(layer):
        sender = layer_of(layer)
        along(layer, sender).wait_recv()
        total[core] += far[sender].astype(F32)

    over(1, spots, lambda k: over(1, layers, lambda layer: to_twin(place.at(layer, k)).start()))
    over(1, layers, lambda layer: to_twin(place.at(layer, 0)).start())
    over(0, spots, lambda k: to_twin(place.at(0, k)).start())
    over(1, spots, lambda k: over(1, layers, lambda layer: send(k, layer)))
    over(1, spots, lambda k: send(k, 0))
    over(1, layers, pass_on)
    spot_sum(0)
    over(1, layers, take)
    result(core).start()
    over(1, spots, lambda k: over(
        0, layers, lambda layer: within(layer, k, place.spot, layer_of(layer)).wait_send()
    ))
    over(1, layers, lambda layer: along(layer, place.layer).wait_send())
    over(0, size, lambda owner: to_twin(owner).wait_send())
    result(core).wait_send()
    result(1 - core).wait_recv()
    value, last = unpack(total[0], share)
    s_attn[...] = value
    s_vec[...] = last[:, : s_vec.shape[1]]
    value, _ = unpack(total[1], share)
    s_in[...] = value[:split]
    s_out[...] = value[split:]


def reduce_scatter(g_attn, g_in, g_out, g_vec):
    grads = (g_attn, g_in, g_out, g_vec)
    size, share = g_attn.shape[:2]
    vmem = pl.BlockSpec(memory_space=pltpu.VMEM)
    block = (packed_rows(share), LANE)
    return pl.pallas_call(
        reduce_kernel,
        name="reduce",
        out_shape=tuple(jax.ShapeDtypeStruct(value.shape[1:], F32) for value in grads),
        in_specs=[vmem] * 4,
        out_specs=[vmem] * 4,
        scratch_shapes=[pltpu.VMEM((2, size, *block), F32)]
        + [pltpu.VMEM((size, *block), BF16)] * 6
        + [pltpu.VMEM((2, *block), F32)]
        + [pltpu.SemaphoreType.DMA((size,))] * 6
        + [pltpu.SemaphoreType.DMA((2,))],
        compiler_params=pltpu.CompilerParams(
            collective_id=1, has_side_effects=True, vmem_limit_bytes=60 * 2**20
        ),
    )(*grads)


def adamw_kernel(*refs):
    for member in range(4):
        master, first, second, grad = (refs[4 * kind + member][...] for kind in range(4))
        results = adamw_update(master, grad, first, second)
        for kind in range(3):
            refs[16 + 3 * member + kind][...] = results[kind]


def adamw(masters, firsts, seconds, grads):
    vmem = pl.BlockSpec(memory_space=pltpu.VMEM)
    return pl.pallas_call(
        adamw_kernel,
        name="adamw",
        out_shape=tuple(
            jax.ShapeDtypeStruct(value.shape, F32) for value in masters for kind in range(3)
        ),
        in_specs=[vmem] * 16,
        out_specs=[vmem] * 12,
        compiler_params=pltpu.CompilerParams(vmem_limit_bytes=60 * 2**20),
    )(*masters, *firsts, *seconds, *grads)


def local(
    tokens,
    cotangent,
    group,
    counts,
    attn_w,
    ffn_in,
    ffn_out,
    vectors,
    attn_m,
    attn_v,
    in_m,
    in_v,
    out_m,
    out_v,
    vec_m,
    vec_v,
):
    size = lax.axis_size("wide")
    width = tokens.shape[1]
    masters = (attn_w, ffn_in, ffn_out, vectors[None])
    attn, into, outof, vec, order, x_rows, c_rows = gather(
        size, group[None], *masters, tokens.T, cotangent.T
    )
    out_t, grad_t, *grads = layer(
        group,
        counts,
        order[0],
        x_rows,
        c_rows,
        attn.reshape(-1, width),
        into.reshape(-1, width),
        outof.reshape(-1, width),
        vec.reshape(-1, 1, LANE),
    )
    sums = reduce_scatter(
        *[g.reshape(size, -1, width) for g in grads[:3]], grads[3].reshape(size, 1, -1)
    )
    results = adamw(
        masters, (attn_m, in_m, out_m, vec_m[None]), (attn_v, in_v, out_v, vec_v[None]), sums
    )
    return (out_t.T, grad_t.T, *results[:9], *[value[0] for value in results[9:]])


def solution(mesh):
    rows = P(("wide", "narrow"), None)
    samples = P(("wide", "narrow"))
    weight = P("wide", None)
    vector = P("wide")
    return jax.shard_map(
        local,
        mesh=mesh,
        in_specs=(rows, rows, samples, samples, weight, weight, weight, vector)
        + (weight,) * 6
        + (vector,) * 2,
        out_specs=(rows, rows) + (weight,) * 9 + (vector,) * 3,
        check_vma=False,
    )
```

```python
import functools
import math

import jax
import jax.numpy as jnp
from jax import lax
from jax.experimental import pallas as pl
from jax.experimental.pallas import tpu as pltpu
from jax.sharding import PartitionSpec as P

HEADS = 8
SLOT = 104
L1 = 40
L2 = 68
L3 = 100
STEP = 10

NORM_EPS = 1e-05
BETA_ONE = 0.9
BETA_TWO = 0.999
ADAM_EPS = 1e-08
LEARN_RATE = 0.1
WEIGHT_DECAY = 0.01
MASK_VALUE = -1e30

F32 = jnp.float32
BF16 = jnp.bfloat16
LANE = 128
MESH = pl.DeviceIdType.MESH
STRIDE = 32
NN = (((1,), (0,)), ((), ()))
NT = (((1,), (1,)), ((), ()))
TN = (((0,), (0,)), ((), ()))
BATCH = 4
SPARE = 24
FILL = {
    40: (5, 1, 1, 5, 4, 4, 3, 4),
    72: (4, 2, 2, 4, 3, 4, 4, 3),
    104: (4, 2, 2, 5, 3, 3, 5, 2),
}
EARLY_D = {40: True, 72: False, 104: True}


def adamw_update(master, gradient, moment, square):
    moment_new = BETA_ONE * moment + (1.0 - BETA_ONE) * gradient
    square_new = BETA_TWO * square + (1.0 - BETA_TWO) * gradient * gradient
    moment_hat = moment_new / (1.0 - BETA_ONE**STEP)
    square_hat = square_new / (1.0 - BETA_TWO**STEP)
    master_new = master - LEARN_RATE * (
        moment_hat / (jnp.sqrt(square_hat) + ADAM_EPS) + WEIGHT_DECAY * master
    )
    return (master_new, moment_new, square_new)


def dot(a, b, dims=NN):
    return lax.dot_general(a, b, dims, preferred_element_type=F32)


def iota(shape, dim):
    return lax.broadcasted_iota(jnp.int32, shape, dim)


def partial_sums(value):
    rows, cols = value.shape
    return jnp.sum(value.reshape(rows // 8, 8, cols), axis=0)


def piece(vec, member, width):
    start = member * width
    parts, at = [], start
    while at < start + width:
        row, lane = divmod(at, LANE)
        take = min(LANE - lane, start + width - at)
        parts.append(vec[row : row + 1, lane : lane + take])
        at += take
    return jnp.concatenate(parts, axis=1)


def layer_kernel(
    group_ref,
    counts_ref,
    order,
    x_hbm,
    c_hbm,
    attn_hbm,
    in_hbm,
    out_hbm,
    vec_hbm,
    y_ref,
    dx_ref,
    g_attn_hbm,
    g_in_hbm,
    g_out_hbm,
    g_vec_hbm,
    attn_ref,
    in_ref,
    out_ref,
    vec_ref,
    g_attn_ref,
    g_in_ref,
    g_out_ref,
    g_vec_ref,
    weight_sem,
    grad_sem,
    xrow,
    crow,
    y_cols,
    dx_cols,
    row_sem,
    col_sem,
    w_qkv,
    w_qkv_t,
    w_o,
    w_o_t,
    w_in,
    w_in_t,
    w_out,
    w_out_t,
    probs,
    scores,
    k_rows,
    v_rows,
    v_cols,
    cols,
    acc_qkv,
    acc_o,
    acc_in,
    acc_out,
    acc_small,
    *carried,
):
    width = attn_ref.shape[1]
    hidden = out_ref.shape[0]
    samples = group_ref.shape[0]
    rows_all = x_hbm.shape[0]
    head = width // HEADS
    pad = HEADS * STRIDE
    scale = 1.0 / math.sqrt(head)
    log2e = math.log2(math.e)
    q_scale = scale * log2e

    weight_copies = [
        pltpu.make_async_copy(ref, held, weight_sem.at[i])
        for i, (ref, held) in enumerate(
            (
                (attn_hbm, attn_ref),
                (in_hbm, in_ref),
                (out_hbm, out_ref),
                (vec_hbm, vec_ref),
            )
        )
    ]
    grad_copies = [
        pltpu.make_async_copy(held, ref, grad_sem.at[i])
        for i, (held, ref) in enumerate(
            (
                (g_attn_ref, g_attn_hbm),
                (g_in_ref, g_in_hbm),
                (g_out_ref, g_out_hbm),
                (g_vec_ref, g_vec_hbm),
            )
        )
    ]
    for copy in weight_copies:
        copy.start()

    steps = samples // (2 * BATCH)

    def fetch(step):
        for j in range(2 * BATCH):
            rows = pl.ds(pl.multiple_of(order[step * 2 * BATCH + j] * SLOT, 8), SLOT)
            for ref, held in ((x_hbm, xrow), (c_hbm, crow)):
                pltpu.make_async_copy(ref.at[rows], held.at[rows], row_sem.at[step]).start()

    def fetched(step):
        rows = pl.ds(0, 2 * BATCH * SLOT)
        for ref, held in ((x_hbm, xrow), (c_hbm, crow)):
            pltpu.make_async_copy(ref.at[rows], held.at[rows], row_sem.at[step]).wait()

    fetch(0)
    fetch(1)
    for ref in (acc_qkv, acc_o, acc_in, acc_out, acc_small, *carried):
        ref[...] = jnp.zeros_like(ref)
    for copy in weight_copies:
        copy.wait()

    spread_row = iota((width, pad), 0)
    spread_col = iota((width, pad), 1)
    within = spread_col & (STRIDE - 1)
    spread = jnp.where(
        (within < head) & (spread_row == (spread_col >> 5) * head + within), 1.0, 0.0
    ).astype(BF16)
    vec = jnp.concatenate([vec_ref[row] for row in range(vec_ref.shape[0])], axis=0)
    bi = jnp.concatenate([vec[row : row + 1] for row in range(12, 16)], axis=1)

    def widen(value, fill=0.0):
        rows = value.shape[0]
        tail = jnp.where(iota((rows, pad - width), 1) == 0, fill, 0.0)
        return jnp.concatenate([value, tail], axis=1)

    def lengthen(value, row=None):
        cols = value.shape[1]
        if row is None:
            row = jnp.zeros((1, cols), F32)
        tail = jnp.concatenate([row, jnp.zeros((pad - width - 1, cols), F32)], axis=0)
        return jnp.concatenate([value, tail], axis=0)

    g1, b1, g2, b2, bq, bv, bo, bf = (piece(vec, member, width) for member in range(8))
    g1, b1, g2, b2 = widen(g1), widen(b1, 1.0), widen(g2), widen(b2, 1.0)
    bf = widen(bf)
    spare_lane = (iota((1, pad), 1) & (STRIDE - 1)) == SPARE
    for member in range(3):
        spread_w = dot(attn_ref[member * width : (member + 1) * width, :], spread)
        if member == 0:
            bias = dot(bq.astype(BF16), spread) + jnp.where(spare_lane, 1.0, 0.0)
        elif member == 1:
            bias = None
        else:
            bias = dot(bv.astype(BF16), spread)
        w_qkv[:, member * pad : (member + 1) * pad] = lengthen(spread_w, bias).astype(BF16)
        w_qkv_t[member * pad : (member + 1) * pad, :] = widen(spread_w.T).astype(BF16)
    spread_o = widen(dot(spread, attn_ref[3 * width :, :], TN))
    w_o_t[...] = spread_o.T.astype(BF16)
    w_o[...] = jnp.where(iota((pad, pad), 0) == SPARE, widen(bo), spread_o).astype(BF16)
    in_wide = widen(in_ref[...].astype(F32))
    out_wide = widen(out_ref[...].astype(F32))
    w_in_t[...] = in_wide.astype(BF16)
    w_in[...] = lengthen(in_wide[:, :width].T, bi).astype(BF16)
    w_out[...] = out_wide.astype(BF16)
    w_out_t[...] = out_wide.T.astype(BF16)

    names = ("q_cols", "d_cols", "probs_low", "ds_low", "k_cols", "dq_cols", "hat", "inv")
    names += ("h2", "du", "hid", "df", "o", "da")
    kept = [
        dict(zip(names, carried[side * len(names) : (side + 1) * len(names)]))
        for side in range(2)
    ]

    features = iota((1, pad), 1) < width

    def norm_stats(x):
        mean = jnp.sum(x, -1, keepdims=True) * (1.0 / width)
        centre = jnp.where(features, x - mean, 0.0)
        spread_sq = jnp.sum(centre * centre, -1, keepdims=True) * (1.0 / width)
        inv = lax.rsqrt(spread_sq + NORM_EPS)
        return centre * inv, inv

    def norm_back(scaled, crossed, hat, inv):
        mean_one = jnp.sum(scaled, -1, keepdims=True) * (1.0 / width)
        mean_two = jnp.sum(crossed, -1, keepdims=True) * (1.0 / width)
        return inv * (scaled - mean_one - hat * mean_two)

    def pad_rows(value, size=LANE):
        rows = value.shape[0]
        return jnp.concatenate([value, jnp.zeros((size - rows, value.shape[1]), F32)], axis=0)

    lead = width + 8

    def grouping(n):
        per = 4 if n <= 64 else 2
        groups = HEADS // per
        return per, groups, [(j, group) for j in range(BATCH) for group in range(groups)]

    def tile(group, per):
        first = group * per // 4
        return slice(first * LANE, (first + 1) * LANE)

    def heads(group, per):
        return slice(per * STRIDE * group, per * STRIDE * (group + 1))

    def put_own(ref, j, per, value):
        size = 2 * LANE // per
        value = pad_rows(value, size)
        cols = stack([value] * (LANE // size)).astype(BF16).T
        for head_at in range(HEADS):
            group, i = divmod(head_at, per)
            rows = slice(head_at % 4 * STRIDE, (head_at % 4 + 1) * STRIDE)
            lanes = slice(i * size % LANE, i * size % LANE + size)
            ref[j, group, rows, i * size : (i + 1) * size] = cols[
                head_at * STRIDE : (head_at + 1) * STRIDE, lanes
            ]

    def own_rows(group, per):
        return slice(group * per % 4 * STRIDE, (group * per % 4 + per) * STRIDE)

    def keep_own(ref, j, group, per, product):
        size = 2 * LANE // per
        for i in range(per):
            block = product[i * STRIDE : (i + 1) * STRIDE]
            at = i * size // LANE
            block = block[:, at * LANE : (at + 1) * LANE]
            if i * size % LANE:
                block = pltpu.roll(block, LANE - i * size % LANE, 1)
            ref[j, per * group + i] = block

    def bases(first):
        return [pl.multiple_of(order[first + j] * SLOT, 8) for j in range(BATCH)]

    def stack(values):
        return jnp.concatenate(values, axis=0)

    def front(box, first, n):
        cuts = {40: (0, 40), 72: (0, 40, 72), 104: (0, 32, 64, 104)}[n]
        chunks = [
            (j, lo, hi) for j in range(BATCH) for lo, hi in zip(cuts[:-1], cuts[1:])
        ]
        at = bases(first)
        limits, live = [], []
        for j in range(BATCH):
            s = order[first + j]
            g = group_ref[s]
            limits.append(jnp.where(g == 0, L1, jnp.where(g == 1, L2, L3)))
            live.append(counts_ref[s])

        per, groups, every = grouping(n)

        def keep(j, lo, hi, value):
            return jnp.where(iota(value.shape, 0) < limits[j] - lo, value, 0.0)

        def rows_of(ref, j, lo, hi):
            return ref[pl.ds(at[j] + lo, hi - lo), :]

        def flat(j, lo, hi):
            return slice(j * n + lo, j * n + hi)

        h1 = []
        for j, lo, hi in chunks:
            hat1, inv1 = norm_stats(rows_of(xrow, j, lo, hi))
            box["hat"][j, lo:hi] = hat1
            box["inv"][j, lo:hi] = jnp.broadcast_to(inv1, (hi - lo, LANE))
            h1.append(hat1 * g1 + b1)
        yield 0
        qkv = dot(stack(h1).astype(BF16), w_qkv[...])
        yield FILL[n][0]
        keys = []
        for j in range(BATCH):
            rows = slice(j * n, (j + 1) * n)
            put_own(box["q_cols"], j, per, qkv[rows, :pad] * q_scale)
            dead = (iota((n, pad), 0) >= live[j]) & spare_lane
            k32 = jnp.where(dead, MASK_VALUE, qkv[rows, pad : 2 * pad])
            k_rows[j, :n] = k32.astype(BF16)
            keys.append(k32)
            yield 0
        for j, group in every:
            scores[j, group, :n] = dot(
                k_rows[j, :n, tile(group, per)], box["q_cols"][j, group]
            )
        for j in range(BATCH):
            v32 = qkv[j * n : (j + 1) * n, 2 * pad :]
            v_rows[j, :n] = v32.astype(BF16)
            v_cols[j] = pad_rows(v32).astype(BF16).T
            box["k_cols"][j] = pad_rows(keys[j]).astype(BF16).T
        yield FILL[n][1]
        for j, group in every:
            score = scores[j, group, :n]
            e = jnp.exp2(score - jnp.max(score, axis=0, keepdims=True))
            p = e * (1.0 / jnp.sum(e, axis=0, keepdims=True))
            probs[j, group, :n] = p
            box["probs_low"][j, group, :n] = p.astype(BF16)
            if group == groups - 1:
                yield 0
        def hidden_grad():
            df = stack([keep(*c, rows_of(crow, *c)) for c in chunks])
            df_low = df.astype(BF16)
            box["df"][: BATCH * n] = df_low
            acc_small[0:8, :] += partial_sums(df)
            return dot(df_low, w_out_t[...])

        for j, group in every:
            o_t = dot(v_cols[j, heads(group, per), :n], box["probs_low"][j, group, :n])
            keep_own(cols, j, group, per, o_t)
        if EARLY_D[n]:
            dhid = hidden_grad()
        yield FILL[n][2]
        mixed = stack([cols[j].reshape(pad, LANE).T[:n] for j in range(BATCH)])
        one = jnp.where(iota((1, LANE), 1) == SPARE, 1.0, mixed[:, :LANE])
        o = jnp.concatenate([one, mixed[:, LANE:]], axis=1).astype(BF16)
        box["o"][: BATCH * n] = o
        yield 0
        a = dot(o, w_o[...])
        yield FILL[n][3]
        y1, hat2, inv2, h2 = [], [], [], []
        for c in chunks:
            y = rows_of(xrow, *c) + keep(*c, a[flat(*c)])
            hat, inv = norm_stats(y)
            y1.append(y)
            hat2.append(hat)
            inv2.append(inv)
            h2.append(hat * g2 + b2)
        h2 = stack(h2).astype(BF16)
        box["h2"][: BATCH * n] = h2
        yield 0
        u = dot(h2, w_in[...])
        if not EARLY_D[n]:
            dhid = hidden_grad()
        yield FILL[n][4]
        hid, du = [], []
        alpha, beta = 0.7978845608028654, 0.044715
        for c in chunks:
            z, up = u[flat(*c), :hidden], u[flat(*c), hidden:]
            dh = dhid[flat(*c)]
            inner = alpha + (alpha * beta) * (z * z)
            gate = 0.5 + 0.5 * jnp.tanh(z * inner)
            act = z * gate
            slope = gate + (act * (1.0 - gate)) * (6.0 * inner - 4.0 * alpha)
            hid.append(act * up)
            du.append(jnp.concatenate([dh * up * slope, dh * act], axis=1))
            if c[1] == 0:
                yield 0
        hid = stack(hid).astype(BF16)
        box["hid"][: BATCH * n] = hid
        du = stack(du).astype(BF16)
        box["du"][: BATCH * n] = du
        yield 0
        dh2 = dot(du, w_in_t[...])
        f = dot(hid, w_out[...])
        yield FILL[n][5]
        da = []
        gain = jnp.zeros((8, pad), F32)
        for i, c in enumerate(chunks):
            j, lo, hi = c
            grad = dh2[flat(*c)]
            crossed = grad * hat2[i]
            gain += partial_sums(crossed)
            dy1 = rows_of(crow, *c) + norm_back(grad * g2, crossed * g2, hat2[i], inv2[i])
            crow[pl.ds(at[j] + lo, hi - lo), :] = dy1
            da.append(keep(*c, dy1))
        acc_small[8:16, :] += gain
        da = stack(da).astype(BF16)
        box["da"][: BATCH * n] = da
        yield 0
        do = dot(da, w_o_t[...])
        for i, c in enumerate(chunks):
            j, lo, hi = c
            xrow[pl.ds(at[j] + lo, hi - lo), :] = y1[i] + keep(*c, f[flat(*c)] + bf)
        yield FILL[n][6]
        for j in range(BATCH):
            put_own(box["d_cols"], j, per, do[j * n : (j + 1) * n])
        yield 0
        for j, group in every:
            scores[j, group, :n] = dot(
                v_rows[j, :n, tile(group, per)], box["d_cols"][j, group]
            )
        yield FILL[n][7]
        for j, group in every:
            dp = scores[j, group, :n]
            p = probs[j, group, :n]
            box["ds_low"][j, group, :n] = (
                p * (dp - jnp.sum(dp * p, axis=0, keepdims=True))
            ).astype(BF16)
            if group == groups - 1:
                yield 0

    def back(box, first, n, layout):
        per, groups, every = grouping(layout)
        rows = slice(0, BATCH * n)
        at = bases(first)
        for j, group in every:
            dq_t = dot(box["k_cols"][j, heads(group, per), :n], box["ds_low"][j, group, :n])
            keep_own(box["dq_cols"], j, group, per, dq_t)
            if group == groups - 1:
                yield
        parts = []
        for j in range(BATCH):
            dv_t, dk_t = [], []
            for group in range(groups):
                own = own_rows(group, per)
                dv_t.append(
                    dot(box["d_cols"][j, group, own], box["probs_low"][j, group, :n], NT)
                )
            yield
            for group in range(groups):
                own = own_rows(group, per)
                dk_t.append(dot(box["q_cols"][j, group, own], box["ds_low"][j, group, :n], NT))
            dq = (box["dq_cols"][j].reshape(pad, LANE) * scale).astype(BF16).T[:n]
            dk = (stack(dk_t) * (1.0 / log2e)).astype(BF16).T
            parts.append(jnp.concatenate([dq, dk, stack(dv_t).astype(BF16).T], axis=1))
            yield
        dqkv = stack(parts)
        dh1 = dot(dqkv, w_qkv_t[...])
        yield
        acc_out[...] += dot(box["df"][rows, :width], box["hid"][rows], TN)
        yield
        acc_o[...] += dot(box["da"][rows, :width], box["o"][rows], TN)
        yield
        h2 = box["h2"][rows, :lead]
        for part in range(2 * hidden // pad):
            lanes = slice(part * pad, (part + 1) * pad)
            acc_in[:, lanes] += dot(h2, box["du"][rows, lanes], TN)
            yield
        h1 = []
        gain = jnp.zeros((8, pad), F32)
        for j in range(BATCH):
            hat = box["hat"][j, :n]
            grad = dh1[j * n : (j + 1) * n]
            crossed = grad * hat
            gain += partial_sums(crossed)
            crow[pl.ds(at[j], n), :] += norm_back(
                grad * g1, crossed * g1, hat, jnp.concatenate([box["inv"][j, :n]] * 2, axis=1)
            )
            h1.append(hat * g1 + b1)
            if j % 2:
                yield
        acc_small[16:24, :] += gain
        h1 = stack(h1).astype(BF16)[:, :lead]
        for part in range(3):
            lanes = slice(part * pad, (part + 1) * pad)
            acc_qkv[:, lanes] += dot(h1, dqkv[:, lanes], TN)
            yield

    def together(fill, main):
        for steps_of in main:
            for _ in range(steps_of):
                next(fill, None)
        for _ in fill:
            pass

    def double(step, n):
        even = step * 2 * BATCH
        before = jnp.maximum(even - BATCH, 0)
        together(back(kept[1], before, n, n), front(kept[0], even, n))
        together(back(kept[0], even, n, n), front(kept[1], even + BATCH, n))

    lengths = (40, 72, 104)
    def kind_of(step):
        return group_ref[order[(step + 1) * 2 * BATCH - 1]]

    def finish_short(step):
        together(back(kept[1], step * 2 * BATCH - BATCH, 40, 40), iter(()))
        for name in ("ds_low", "du", "df", "da"):
            kept[1][name][...] = jnp.zeros_like(kept[1][name])
        for box in kept:
            for name in ("q_cols", "d_cols"):
                box[name][...] = jnp.zeros_like(box[name])

    def one_step(step, carry):
        kind = kind_of(jnp.minimum(step, steps - 1))
        last = kind_of(jnp.maximum(step - 1, 0))
        pl.when((step > 0) & (last == 0) & ((step == steps) | (kind != 0)))(
            functools.partial(finish_short, step)
        )
        pl.when(step < steps)(lambda: fetched(step))
        pl.when(step + 2 < steps)(lambda: fetch(step + 2))
        for member, n in enumerate(lengths):
            pl.when((step < steps) & (kind == member))(functools.partial(double, step, n))
        return carry

    lax.fori_loop(0, steps + 1, one_step, 0)

    cut = 4 * LANE

    def col_copies(part):
        lanes = pl.ds(pl.multiple_of(part * cut, cut), cut)
        return [
            pltpu.make_async_copy(held.at[:, lanes], ref.at[:, lanes], col_sem.at[i, part])
            for i, (held, ref) in enumerate(((y_cols, y_ref), (dx_cols, dx_ref)))
        ]

    def fold_y():
        for part in range(rows_all // cut):
            for member in range(4):
                at = slice(part * cut + member * LANE, part * cut + (member + 1) * LANE)
                y_cols[:, at] = xrow[at, :width].astype(BF16).T
                yield
            col_copies(part)[0].start()

    folding = fold_y()
    for _ in back(kept[1], samples - BATCH, SLOT, SLOT):
        for _ in range(3):
            next(folding, None)
    for _ in folding:
        pass

    def fold_dx():
        for part in range(rows_all // cut):
            for member in range(4):
                at = slice(part * cut + member * LANE, part * cut + (member + 1) * LANE)
                dx_cols[:, at] = crow[at, :width].T
                yield
            col_copies(part)[1].start()

    folding = fold_dx()

    def halves(value):
        high = value.astype(BF16)
        return high, (value - high.astype(F32)).astype(BF16)

    def twice(a, b, dims):
        if a.dtype == F32:
            return sum(dot(part, b, dims) for part in halves(a))
        return sum(dot(a, part, dims) for part in halves(b))

    def small(member):
        block = acc_small[8 * member : 8 * member + 8, :width]
        return jnp.sum(block, axis=0, keepdims=True)

    def gradients():
        for member in range(3):
            g_attn_ref[member * width : (member + 1) * width, :] = twice(
                acc_qkv[:width, member * pad : (member + 1) * pad], spread, NT
            )
            yield
        g_attn_ref[3 * width :, :] = twice(spread, acc_o[...], NT)
        grad_copies[0].start()
        yield
        g_in_ref[...] = acc_in[:width, :].T
        grad_copies[1].start()
        yield
        g_out_ref[...] = acc_out[...].T
        grad_copies[2].start()
        yield
        qkv_sums = acc_qkv[width : width + 8, :]
        in_sums = acc_in[width : width + 8, :]
        g_b1 = twice(qkv_sums, w_qkv_t[...], NN)[0:1, :width]
        g_b2 = twice(in_sums, w_in_t[...], NN)[0:1, :width]
        g_bq = twice(qkv_sums[:, :pad], spread, NT)[0:1]
        g_bv = twice(qkv_sums[:, 2 * pad :], spread, NT)[0:1]
        g_bo = acc_o[...].T[SPARE : SPARE + 1]
        yield
        flat = jnp.concatenate(
            [small(2), g_b1, small(1), g_b2, g_bq, g_bv, g_bo, small(0), in_sums[0:1]], axis=1
        )
        for row in range(16):
            g_vec_ref[row] = flat[:, row * LANE : (row + 1) * LANE]
        grad_copies[3].start()

    for _ in gradients():
        for _ in range(7):
            next(folding, None)
    for _ in folding:
        pass

    def folded(part, carry):
        for copy in col_copies(part):
            copy.wait()
        return carry

    lax.fori_loop(0, rows_all // cut, folded, 0)
    for copy in grad_copies:
        copy.wait()


def layer(group, counts, order, x_rows, c_rows, attn, ffn_in, ffn_out, vec):
    rows, width = x_rows.shape[0], attn.shape[1]
    weights = (attn, ffn_in, ffn_out, vec)
    hidden = ffn_out.shape[0]
    pad = HEADS * STRIDE
    smem = pl.BlockSpec(memory_space=pltpu.SMEM)
    whole = pl.BlockSpec(memory_space=pl.ANY)
    return pl.pallas_call(
        layer_kernel,
        name="layer",
        out_shape=(
            jax.ShapeDtypeStruct((width, rows), BF16),
            jax.ShapeDtypeStruct((width, rows), F32),
            jax.ShapeDtypeStruct((4 * width, width), F32),
            jax.ShapeDtypeStruct((2 * hidden, width), F32),
            jax.ShapeDtypeStruct((hidden, width), F32),
            jax.ShapeDtypeStruct((16, 1, LANE), F32),
        ),
        in_specs=[smem] * 3 + [whole] * 6,
        out_specs=[whole] * 6,
        scratch_shapes=[pltpu.VMEM(value.shape, value.dtype) for value in weights]
        + [
            pltpu.VMEM((4 * width, width), F32),
            pltpu.VMEM((2 * hidden, width), F32),
            pltpu.VMEM((hidden, width), F32),
            pltpu.VMEM((16, 1, LANE), F32),
            pltpu.SemaphoreType.DMA((4,)),
            pltpu.SemaphoreType.DMA((4,)),
            pltpu.VMEM((rows, pad), F32),
            pltpu.VMEM((rows, pad), F32),
            pltpu.VMEM((width, rows), BF16),
            pltpu.VMEM((width, rows), F32),
            pltpu.SemaphoreType.DMA((group.shape[0] // (2 * BATCH),)),
            pltpu.SemaphoreType.DMA((2, rows // (4 * LANE))),
            pltpu.VMEM((pad, 3 * pad), BF16),
            pltpu.VMEM((3 * pad, pad), BF16),
            pltpu.VMEM((pad, pad), BF16),
            pltpu.VMEM((pad, pad), BF16),
            pltpu.VMEM((pad, 2 * hidden), BF16),
            pltpu.VMEM((2 * hidden, pad), BF16),
            pltpu.VMEM((hidden, pad), BF16),
            pltpu.VMEM((pad, hidden), BF16),
            pltpu.VMEM((BATCH, HEADS // 2, SLOT, 2 * LANE), F32),
            pltpu.VMEM((BATCH, HEADS // 2, SLOT, 2 * LANE), F32),
            pltpu.VMEM((BATCH, SLOT + 8, pad), BF16),
            pltpu.VMEM((BATCH, SLOT + 8, pad), BF16),
            pltpu.VMEM((BATCH, pad, LANE), BF16),
            pltpu.VMEM((BATCH, HEADS, STRIDE, LANE), F32),
            pltpu.VMEM((width + 8, 3 * pad), F32),
            pltpu.VMEM((width, pad), F32),
            pltpu.VMEM((width + 8, 2 * hidden), F32),
            pltpu.VMEM((width, hidden), F32),
            pltpu.VMEM((24, pad), F32),
        ]
        + [
            pltpu.VMEM((BATCH, HEADS // 2, LANE, 2 * LANE), BF16),
            pltpu.VMEM((BATCH, HEADS // 2, LANE, 2 * LANE), BF16),
            pltpu.VMEM((BATCH, HEADS // 2, SLOT + 8, 2 * LANE), BF16),
            pltpu.VMEM((BATCH, HEADS // 2, SLOT + 8, 2 * LANE), BF16),
            pltpu.VMEM((BATCH, pad, LANE), BF16),
            pltpu.VMEM((BATCH, HEADS, STRIDE, LANE), F32),
            pltpu.VMEM((BATCH, SLOT, pad), F32),
            pltpu.VMEM((BATCH, SLOT, LANE), F32),
            pltpu.VMEM((BATCH * SLOT, pad), BF16),
            pltpu.VMEM((BATCH * SLOT, 2 * hidden), BF16),
            pltpu.VMEM((BATCH * SLOT, hidden), BF16),
            pltpu.VMEM((BATCH * SLOT, pad), BF16),
            pltpu.VMEM((BATCH * SLOT, pad), BF16),
            pltpu.VMEM((BATCH * SLOT, pad), BF16),
        ]
        * 2,
        compiler_params=pltpu.CompilerParams(vmem_limit_bytes=60 * 2**20),
    )(group, counts, order, x_rows, c_rows, attn, ffn_in, ffn_out, vec)


class Place:
    def __init__(self, size):
        side = 1
        while 2 * (2 * side) ** 3 <= size:
            side *= 2
        self.size, self.spots = size, side * side
        self.layers = size // self.spots
        me, self.core = lax.axis_index("wide"), lax.axis_index("narrow")
        self.me = me
        self.layer, self.spot = me // self.spots, lax.rem(me, self.spots)

    def at(self, layer, spot):
        layer = lax.rem(self.layer + layer + self.layers, self.layers)
        return layer * self.spots + lax.rem(self.spot + spot + self.spots, self.spots)

    def signal(self):
        barrier = pltpu.get_barrier_semaphore()

        def tell(index, core):
            pl.semaphore_signal(
                barrier, inc=1, device_id=(index, core), device_id_type=MESH
            )

        over(1, self.layers, lambda k: tell(self.at(k, 0), self.core))
        over(1, self.spots, lambda k: tell(self.at(0, k), self.core))
        tell(self.me, 1 - self.core)

    def wait(self):
        pl.semaphore_wait(
            pltpu.get_barrier_semaphore(), self.layers + self.spots - 1
        )


def over(low, high, body):
    def step(k, carry):
        body(k)
        return carry

    lax.fori_loop(low, high, step, 0)


def packed_rows(share):
    return (share + share // 2 + 1 + 15) // 16 * 16


def pack(value, vec):
    share, width = value.shape
    tail = value[:, LANE:]
    tail = jnp.concatenate([tail[: share // 2], tail[share // 2 :]], axis=1)
    if vec.shape[1] < LANE:
        vec = jnp.concatenate([vec, jnp.zeros((1, LANE - vec.shape[1]), F32)], axis=1)
    rest = packed_rows(share) - share - share // 2 - 1
    return jnp.concatenate([value[:, :LANE], tail, vec, jnp.zeros((rest, LANE), F32)], axis=0)


def unpack(block, share):
    at = share + share // 2
    tail = block[share:at]
    tail = jnp.concatenate([tail[:, : LANE // 2], tail[:, LANE // 2 :]], axis=0)
    return jnp.concatenate([block[:share], tail], axis=1), block[at : at + 1]


def gather_kernel(
    group_hbm, attn_hbm, in_hbm, out_hbm, vec_hbm, tok_hbm, cot_hbm,
    attn_all, in_all, out_all, vec_all, order_ref, x_hbm, c_hbm,
    group_ref, attn_ref, in_ref, out_ref, vec_ref, first_sem,
    blocks, tok, cot, xrow, crow, in_sem, row_sem, send_sem, recv_sem, pass_sem, got_sem,
):
    size = attn_all.shape[0]
    share, width = attn_ref.shape
    split = in_ref.shape[0]
    place = Place(size)
    me, core, layers, spots = place.me, place.core, place.layers, place.spots
    cut = 4 * LANE
    parts = tok_hbm.shape[1] // cut
    pad = xrow.shape[1]

    def lanes(part):
        return pl.ds(pl.multiple_of(part * cut, cut), cut)

    def col_copies(part):
        return [
            pltpu.make_async_copy(ref.at[:, lanes(part)], held.at[:, lanes(part)], in_sem.at[i, part])
            for i, (ref, held) in enumerate(((tok_hbm, tok), (cot_hbm, cot)))
        ]

    def row_copies(part):
        return [
            pltpu.make_async_copy(held.at[lanes(part)], ref.at[lanes(part)], row_sem.at[i, part])
            for i, (held, ref) in enumerate(((xrow, x_hbm), (crow, c_hbm)))
        ]

    place.signal()
    first = [
        pltpu.make_async_copy(ref, held, first_sem.at[i])
        for i, (ref, held) in enumerate(
            (
                (attn_hbm, attn_ref),
                (in_hbm, in_ref),
                (out_hbm, out_ref),
                (vec_hbm, vec_ref),
                (group_hbm, group_ref),
            )
        )
    ]
    for copy in first:
        copy.start()

    def begin(part):
        for copy in col_copies(part):
            copy.start()

    over(0, parts, begin)
    for copy in first:
        copy.wait()
    vec = vec_ref[...]
    blocks[0, me] = pack(attn_ref[...], vec).astype(BF16)
    both = jnp.concatenate([in_ref[...], out_ref[...]], axis=0)
    blocks[1, me] = pack(both, vec).astype(BF16)
    place.wait()

    def to_peer(owner, target, slot):
        return pltpu.make_async_remote_copy(
            src_ref=blocks.at[core, owner],
            dst_ref=blocks.at[core, owner],
            send_sem=send_sem.at[slot],
            recv_sem=recv_sem.at[owner],
            device_id=(target, core),
            device_id_type=MESH,
        )

    def to_twin(owner, whose):
        return pltpu.make_async_remote_copy(
            src_ref=blocks.at[whose, owner],
            dst_ref=blocks.at[whose, owner],
            send_sem=pass_sem.at[owner],
            recv_sem=got_sem.at[owner],
            device_id=(me, 1 - core),
            device_id_type=MESH,
        )

    def along(k):
        return to_peer(me, place.at(k, 0), layers * (spots - 1) + k - 1)

    def within(layer, k):
        owner = place.at(-layer, 0)
        return to_peer(owner, place.at(0, k), layer * (spots - 1) + k - 1)

    over(1, layers, lambda k: along(k).start())
    over(1, spots, lambda k: within(0, k).start())

    samples = group_ref.shape[1]
    key = group_ref[...] * samples + iota((1, samples), 1)
    wide = jnp.broadcast_to(key.astype(F32), (samples, samples))
    rank = jnp.sum(jnp.where(wide < wide.T, 1.0, 0.0), axis=1, keepdims=True)
    here = rank == iota((samples, samples), 1).astype(F32)
    found = jnp.where(here, iota((samples, samples), 0).astype(F32), 0.0)
    order_ref[...] = jnp.sum(found, axis=0, keepdims=True).astype(jnp.int32)

    zero = jnp.zeros((LANE, pad - width), F32)

    def unfold(part):
        for copy in col_copies(part):
            copy.wait()
        for member in range(4):
            at = pl.multiple_of(part * cut + member * LANE, LANE)
            for held, rows in ((tok, xrow), (cot, crow)):
                value = held[:, pl.ds(at, LANE)].T.astype(F32)
                rows[pl.ds(at, LANE), :] = jnp.concatenate([value, zero], axis=1)
        for copy in row_copies(part):
            copy.start()

    def arrived(owner):
        to_peer(owner, me, 0).wait_recv()
        to_twin(owner, core).start()

    def forward(layer):
        to_peer(place.at(-layer, 0), me, 0).wait_recv()
        over(1, spots, lambda k: within(layer, k).start())
        to_twin(place.at(-layer, 0), core).start()

    early = min(3, parts)
    over(0, early, unfold)
    over(1, layers, forward)
    over(early, parts, unfold)
    over(1, spots, lambda k: over(0, layers, lambda layer: arrived(place.at(-layer, -k))))

    def end(part):
        for copy in row_copies(part):
            copy.wait()

    def spread_out(owner):
        value, last = unpack(blocks[0, owner].astype(F32), share)
        attn_all[owner] = value.astype(BF16)
        vec_all[owner] = last[:, : vec_all.shape[2]]
        value, _ = unpack(blocks[1, owner].astype(F32), share)
        in_all[owner] = value[:split].astype(BF16)
        out_all[owner] = value[split:].astype(BF16)

    def finish(layer, k):
        owner = place.at(-layer, -k)
        to_twin(owner, 1 - core).wait_recv()
        spread_out(owner)

    spread_out(me)
    over(1, layers, lambda layer: finish(layer, 0))
    over(1, spots, lambda k: over(0, layers, lambda layer: finish(layer, k)))
    over(1, layers, lambda k: along(k).wait_send())
    over(0, layers, lambda layer: over(1, spots, lambda k: within(layer, k).wait_send()))
    over(1, size, lambda k: to_twin(lax.rem(me + k, size), core).wait_send())
    over(0, parts, end)


def gather(size, group, attn, ffn_in, ffn_out, vec, tokens_t, cotangent_t):
    vmem = pl.BlockSpec(memory_space=pltpu.VMEM)
    whole = pl.BlockSpec(memory_space=pl.ANY)
    width, rows = tokens_t.shape
    pad = HEADS * STRIDE
    parts = rows // (4 * LANE)
    return pl.pallas_call(
        gather_kernel,
        name="gather",
        out_shape=tuple(
            jax.ShapeDtypeStruct((size, *value.shape), BF16)
            for value in (attn, ffn_in, ffn_out)
        )
        + (
            jax.ShapeDtypeStruct((size, *vec.shape), F32),
            jax.ShapeDtypeStruct(group.shape, jnp.int32),
            jax.ShapeDtypeStruct((rows, pad), F32),
            jax.ShapeDtypeStruct((rows, pad), F32),
        ),
        in_specs=[whole] * 7,
        out_specs=[vmem] * 5 + [whole] * 2,
        scratch_shapes=[
            pltpu.VMEM(value.shape, value.dtype)
            for value in (group, attn, ffn_in, ffn_out, vec)
        ]
        + [
            pltpu.SemaphoreType.DMA((5,)),
            pltpu.VMEM((2, size, packed_rows(attn.shape[0]), LANE), BF16),
            pltpu.VMEM((width, rows), BF16),
            pltpu.VMEM((width, rows), BF16),
            pltpu.VMEM((rows, pad), F32),
            pltpu.VMEM((rows, pad), F32),
            pltpu.SemaphoreType.DMA((2, parts)),
            pltpu.SemaphoreType.DMA((2, parts)),
        ]
        + [pltpu.SemaphoreType.DMA((size,))] * 4,
        compiler_params=pltpu.CompilerParams(
            collective_id=0, has_side_effects=True, vmem_limit_bytes=60 * 2**20
        ),
    )(group, attn, ffn_in, ffn_out, vec, tokens_t, cotangent_t)


def reduce_kernel(
    attn_hbm, in_hbm, out_hbm, vec_hbm,
    s_attn, s_in, s_out, s_vec,
    g_attn, g_in, g_out, g_vec, first_sem,
    own, stage, twin, chip, near, relay, far, total,
    pass_sem, got_sem, near_send, near_recv, far_send, far_recv, last_sem,
):
    size, share = g_attn.shape[:2]
    split = g_in.shape[1]
    place = Place(size)
    me, core, layers, spots = place.me, place.core, place.layers, place.spots
    place.signal()
    first = [
        pltpu.make_async_copy(ref, held, first_sem.at[i])
        for i, (ref, held) in enumerate(
            ((attn_hbm, g_attn), (in_hbm, g_in), (out_hbm, g_out), (vec_hbm, g_vec))
        )
    ]
    for copy in first:
        copy.start()
    for copy in first:
        copy.wait()

    def prepare(owner):
        own[0, owner] = pack(g_attn[owner], g_vec[owner])
        both = jnp.concatenate([g_in[owner], g_out[owner]], axis=0)
        own[1, owner] = pack(both, jnp.zeros((1, LANE), F32))
        stage[owner] = own[1 - core, owner].astype(BF16)

    over(0, size, prepare)
    place.wait()

    def to_twin(owner):
        return pltpu.make_async_remote_copy(
            src_ref=stage.at[owner],
            dst_ref=twin.at[owner],
            send_sem=pass_sem.at[owner],
            recv_sem=got_sem.at[owner],
            device_id=(me, 1 - core),
            device_id_type=MESH,
        )

    def within(layer, k, spot, owner_layer):
        owner = place.at(layer, k)
        slot = spot * layers + owner_layer
        return pltpu.make_async_remote_copy(
            src_ref=chip.at[owner],
            dst_ref=near.at[slot],
            send_sem=near_send.at[owner],
            recv_sem=near_recv.at[slot],
            device_id=(place.at(0, k), core),
            device_id_type=MESH,
        )

    def along(layer, sender):
        target = lax.rem(place.layer + layer, layers)
        return pltpu.make_async_remote_copy(
            src_ref=relay.at[target],
            dst_ref=far.at[sender],
            send_sem=far_send.at[target],
            recv_sem=far_recv.at[sender],
            device_id=(place.at(layer, 0), core),
            device_id_type=MESH,
        )

    def result(whose):
        return pltpu.make_async_remote_copy(
            src_ref=total.at[whose],
            dst_ref=total.at[whose],
            send_sem=last_sem.at[0],
            recv_sem=last_sem.at[1],
            device_id=(me, 1 - core),
            device_id_type=MESH,
        )

    def layer_of(layer):
        return lax.rem(place.layer + layer, layers)

    def send(k, layer):
        owner = place.at(layer, k)
        to_twin(owner).wait_recv()
        chip[owner] = (own[core, owner] + twin[owner].astype(F32)).astype(BF16)
        within(layer, k, place.spot, layer_of(layer)).start()

    def spot_sum(layer):
        owner = place.at(layer, 0)
        to_twin(owner).wait_recv()
        total[core] = own[core, owner] + twin[owner].astype(F32)

        def add(k):
            spot = lax.rem(place.spot + k, spots)
            within(layer, k, spot, layer_of(layer)).wait_recv()
            total[core] += near[spot * layers + layer_of(layer)].astype(F32)

        over(1, spots, add)

    def pass_on(layer):
        spot_sum(layer)
        relay[layer_of(layer)] = total[core].astype(BF16)
        along(layer, place.layer).start()

    def take(layer):
        sender = layer_of(layer)
        along(layer, sender).wait_recv()
        total[core] += far[sender].astype(F32)

    over(1, spots, lambda k: over(1, layers, lambda layer: to_twin(place.at(layer, k)).start()))
    over(1, layers, lambda layer: to_twin(place.at(layer, 0)).start())
    over(0, spots, lambda k: to_twin(place.at(0, k)).start())
    over(1, spots, lambda k: over(1, layers, lambda layer: send(k, layer)))
    over(1, spots, lambda k: send(k, 0))
    over(1, layers, pass_on)
    spot_sum(0)
    over(1, layers, take)
    result(core).start()
    over(1, spots, lambda k: over(
        0, layers, lambda layer: within(layer, k, place.spot, layer_of(layer)).wait_send()
    ))
    over(1, layers, lambda layer: along(layer, place.layer).wait_send())
    over(0, size, lambda owner: to_twin(owner).wait_send())
    result(core).wait_send()
    result(1 - core).wait_recv()
    value, last = unpack(total[0], share)
    s_attn[...] = value
    s_vec[...] = last[:, : s_vec.shape[1]]
    value, _ = unpack(total[1], share)
    s_in[...] = value[:split]
    s_out[...] = value[split:]


def reduce_scatter(g_attn, g_in, g_out, g_vec):
    grads = (g_attn, g_in, g_out, g_vec)
    size, share = g_attn.shape[:2]
    vmem = pl.BlockSpec(memory_space=pltpu.VMEM)
    block = (packed_rows(share), LANE)
    return pl.pallas_call(
        reduce_kernel,
        name="reduce",
        out_shape=tuple(jax.ShapeDtypeStruct(value.shape[1:], F32) for value in grads),
        in_specs=[pl.BlockSpec(memory_space=pl.ANY)] * 4,
        out_specs=[vmem] * 4,
        scratch_shapes=[pltpu.VMEM(value.shape, F32) for value in grads]
        + [pltpu.SemaphoreType.DMA((4,))]
        + [pltpu.VMEM((2, size, *block), F32)]
        + [pltpu.VMEM((size, *block), BF16)] * 6
        + [pltpu.VMEM((2, *block), F32)]
        + [pltpu.SemaphoreType.DMA((size,))] * 6
        + [pltpu.SemaphoreType.DMA((2,))],
        compiler_params=pltpu.CompilerParams(
            collective_id=1, has_side_effects=True, vmem_limit_bytes=60 * 2**20
        ),
    )(*grads)


def adamw_kernel(*refs):
    for member in range(4):
        master, first, second, grad = (refs[4 * kind + member][...] for kind in range(4))
        results = adamw_update(master, grad, first, second)
        for kind in range(3):
            refs[16 + 3 * member + kind][...] = results[kind]


def adamw(masters, firsts, seconds, grads):
    vmem = pl.BlockSpec(memory_space=pltpu.VMEM)
    return pl.pallas_call(
        adamw_kernel,
        name="adamw",
        out_shape=tuple(
            jax.ShapeDtypeStruct(value.shape, F32) for value in masters for kind in range(3)
        ),
        in_specs=[vmem] * 16,
        out_specs=[vmem] * 12,
        compiler_params=pltpu.CompilerParams(vmem_limit_bytes=60 * 2**20),
    )(*masters, *firsts, *seconds, *grads)


def local(
    tokens,
    cotangent,
    group,
    counts,
    attn_w,
    ffn_in,
    ffn_out,
    vectors,
    attn_m,
    attn_v,
    in_m,
    in_v,
    out_m,
    out_v,
    vec_m,
    vec_v,
):
    size = lax.axis_size("wide")
    width = tokens.shape[1]
    masters = (attn_w, ffn_in, ffn_out, vectors[None])
    attn, into, outof, vec, order, x_rows, c_rows = gather(
        size, group[None], *masters, tokens.T, cotangent.T
    )
    out_t, grad_t, *grads = layer(
        group,
        counts,
        order[0],
        x_rows,
        c_rows,
        attn.reshape(-1, width),
        into.reshape(-1, width),
        outof.reshape(-1, width),
        vec.reshape(-1, 1, LANE),
    )
    sums = reduce_scatter(
        *[g.reshape(size, -1, width) for g in grads[:3]], grads[3].reshape(size, 1, -1)
    )
    results = adamw(
        masters, (attn_m, in_m, out_m, vec_m[None]), (attn_v, in_v, out_v, vec_v[None]), sums
    )
    return (out_t.T, grad_t.T, *results[:9], *[value[0] for value in results[9:]])


def solution(mesh):
    rows = P(("wide", "narrow"), None)
    samples = P(("wide", "narrow"))
    weight = P("wide", None)
    vector = P("wide")
    return jax.shard_map(
        local,
        mesh=mesh,
        in_specs=(rows, rows, samples, samples, weight, weight, weight, vector)
        + (weight,) * 6
        + (vector,) * 2,
        out_specs=(rows, rows) + (weight,) * 9 + (vector,) * 3,
        check_vma=False,
    )
```
